128 devices in a mesh: dp: 16 (over z_lo, x, core), ctx: 8 (over z_hi, y).
Axes of the slice: x: 4, y: 4, z: 4 (z_hi: 2, z_lo: 2; z = z_hi * 2 + z_lo), core: 2. Of those that a mesh axis runs over, the one named last changes fastest.
Arguments:
- layer_input: bfloat16 [16, 1024, 8192], P('dp', 'ctx')
- w_qkv: bfloat16 [8192, 1280], replicated
- d_out: bfloat16 [16, 1024, 1024], P('dp', 'ctx'), may hold values from -6 to 6
- span_order: int32 [16, 16], P('dp'), may hold values from 0 to 15, each once within a row
- doc_lengths: int32 [16, 4], P('dp'), may hold values from 1 to 512, 1024 in all within a row
Outputs:
- d_x: bfloat16 [16, 1024, 8192], P('dp', 'ctx')
- d_w: float32 [8192, 1280], P(('dp', 'ctx'))
The draws below stay inside these ranges and needn't reach their ends.
All inputs are finite; a program needn't handle non-finite values.
Results may differ from the reference program's by a relative error of at most 0.029.
Values may be sent and summed in bfloat16 or wider, within the bound.
No kernel may reach another device: no remote copies, remote signals or barrier semaphores. Data moves between devices by JAX's collectives and lax.ppermute only.
A program may use at most 128 MiB of HBM per device.

```python
import math
import jax
import jax.numpy as jnp
import numpy as np
from jax import lax

D = 8192
HD = 128
HQ = 8
TOK_DEV = 128
DOCS = 4
C = 1280
LEN = 1024
BATCH = 16
SPANS = 16
SPAN = 64
N_CTX = 8


def draw_layer_input(key, part):
    key = jax.random.fold_in(key, 1)
    first = jax.random.fold_in(key, 0)
    values = jnp.clip(jax.random.normal(first, (BATCH, LEN, D), jnp.float32), -6.0, 6.0)
    return values.astype(jnp.bfloat16)


def draw_w_qkv(key, part):
    key = jax.random.fold_in(key, 2)
    noise = jax.random.normal(key, (D, C), jnp.float32)
    values = noise
    return (jnp.clip(values, -6.0, 6.0) * D ** (-0.5)).astype(jnp.bfloat16)


def shard_levels(key, dims, shards, smallest, high):
    gain, own = 1.0, jax.random.fold_in(key, 6)
    for axis_at, blocks in shards:
        draws = jnp.exp(jax.random.uniform(jax.random.fold_in(own, axis_at), (blocks,), jnp.float32, smallest / len(shards), high / len(shards)))
        gain = gain * jnp.repeat(draws, dims[axis_at] // blocks).reshape([-1 if axis == axis_at else 1 for axis in range(len(dims))])
    return gain


def split_up(number_of, total, reach, lean):
    portions = [(1 << 20) // math.isqrt(standing ** lean) + 1 for standing in range(2, number_of + 1)]
    spare, counts = total - reach - (number_of - 1), [1] * (number_of - 1)
    while spare > 0:
        free = [i for i in range(number_of - 1) if counts[i] < reach]
        whole, budget = sum([portions[i] for i in free]), spare
        for i in free:
            addition = min(reach - counts[i], max(1, budget * portions[i] // whole), spare)
            counts[i] = counts[i] + addition
            spare = spare - addition
    return np.array([reach] + counts)


def ragged(rng, count, total, reach, slope):
    if count == 2:
        one = jax.random.randint(rng, (), max(1, total - reach), min(reach, total - 1) + 1)
        return jnp.stack([one, total - one])
    tallies = jnp.asarray(split_up(count, total, reach, slope), jnp.int32)
    twos = (count - 1) // 2
    giver, receiver = tallies[1:1 + 2 * twos:2], tallies[2:2 + 2 * twos:2]
    margin = jnp.minimum(giver - 1, reach - receiver)
    passed = jax.random.randint(jax.random.fold_in(rng, 1), (twos,), 0, 1 << 20) % (margin + 1)
    tallies = tallies.at[1:1 + 2 * twos:2].set(giver - passed).at[2:2 + 2 * twos:2].set(receiver + passed)
    return tallies[jax.random.permutation(jax.random.fold_in(rng, 2), count)]


def gaussian(rng, dims, width, bound, shards=(), held_as=jnp.bfloat16):
    gain = shard_levels(rng, dims, shards, -0.22, 0.18) if shards else 1.0
    values = jax.random.normal(rng, dims, jnp.float32) * width * gain
    return jnp.minimum(jnp.maximum(values, -bound), bound).astype(held_as)


def setup_inputs(seed: int = 0) -> dict:
    arg_keys = jax.random.split(jax.random.key(seed), 6)
    layer_input = draw_layer_input(jax.random.fold_in(arg_keys[5], 71), 0)
    w_qkv = draw_w_qkv(jax.random.fold_in(arg_keys[5], 71), 0)
    d_out = gaussian(arg_keys[2], (BATCH, LEN, HQ * HD), 1.0, 6.0, ((0, 16), (1, 8)))
    span_order = jax.vmap(lambda own: jax.random.permutation(own, SPANS))(jax.random.split(arg_keys[3], BATCH)).reshape((BATCH, SPANS)).astype(jnp.int32)
    doc_lengths = jax.vmap(lambda own: ragged(own, DOCS, LEN, LEN // 2, 0))(jax.random.split(arg_keys[4], BATCH)).reshape((BATCH, DOCS)).astype(jnp.int32)
    return {"layer_input": layer_input, "w_qkv": w_qkv, "d_out": d_out, "span_order": span_order, "doc_lengths": doc_lengths}


def place_rows(order, lengths, total):
    stored = jnp.arange(total, dtype=jnp.int32)
    positions = order[stored // SPAN] * SPAN + stored % SPAN
    ends = jnp.cumsum(lengths).astype(jnp.int32)
    documents = jnp.sum((positions[:, None] >= ends[None, :]).astype(jnp.int32), axis=1)
    return positions, documents


def reference(layer_input, w_qkv, d_out, span_order, doc_lengths):
    scale = HD ** -0.5

    def one_sequence(total, inputs):
        rows, grad_out, order, lengths = inputs
        positions, documents = place_rows(order, lengths, LEN)
        qkv = jnp.dot(rows, w_qkv, preferred_element_type=jnp.float32).astype(jnp.bfloat16)
        query = qkv[:, :HQ * HD].reshape(LEN, HQ, HD).astype(jnp.float32)
        key = qkv[:, HQ * HD:(HQ + 1) * HD].astype(jnp.float32)
        value = qkv[:, (HQ + 1) * HD:].astype(jnp.float32)
        allowed = (positions[None, :] <= positions[:, None]) & (documents[None, :] == documents[:, None])
        scores = jnp.einsum('qhd,kd->hqk', query, key) * scale
        scores = jnp.where(allowed[None], scores, -1e30)
        peak = jnp.max(scores, axis=2, keepdims=True)
        expo = jnp.where(allowed[None], jnp.exp(scores - peak), 0.0)
        probs = expo / jnp.sum(expo, axis=2, keepdims=True)
        probs_low = probs.astype(jnp.bfloat16).astype(jnp.float32)
        grad_heads = grad_out.reshape(LEN, HQ, HD).astype(jnp.float32)
        out_heads = jnp.einsum('hqk,kd->qhd', probs_low, value)
        delta = jnp.sum(grad_heads * out_heads, axis=2)
        grad_probs = jnp.einsum('qhd,kd->hqk', grad_heads, value)
        d_scores = (probs * (grad_probs - jnp.transpose(delta)[:, :, None]) * scale).astype(jnp.bfloat16).astype(jnp.float32)
        d_query = jnp.einsum('hqk,kd->qhd', d_scores, key).reshape(LEN, HQ * HD)
        d_key = jnp.einsum('hqk,qhd->kd', d_scores, query)
        d_value = jnp.einsum('hqk,qhd->kd', probs_low, grad_heads)
        d_qkv = jnp.concatenate([d_query, d_key, d_value], axis=1).astype(jnp.bfloat16)
        d_rows = jnp.dot(d_qkv, jnp.transpose(w_qkv), preferred_element_type=jnp.float32).astype(jnp.bfloat16)
        for block in range(N_CTX):
            lower = block * TOK_DEV
            term = jnp.dot(jnp.transpose(rows[lower:lower + TOK_DEV]), d_qkv[lower:lower + TOK_DEV], preferred_element_type=jnp.float32)
            term = lax.optimization_barrier(term.astype(jnp.bfloat16))
            total = total + term.astype(jnp.float32)
        return total, d_rows

    start = jnp.zeros((D, C), jnp.float32)
    d_w, d_x = lax.scan(one_sequence, start, (layer_input, d_out, span_order, doc_lengths))
    return d_x, d_w
```

```python
import jax
import jax.numpy as jnp
from jax import lax
from jax.experimental import pallas as pl
from jax.experimental.pallas import tpu as pltpu
from jax.sharding import Mesh, PartitionSpec as P

HD = 128
HQ = 8
SPAN = 64
LOG2E = 1.4426950408889634
SEQ = ("zhi", "y")
OWN = ("zlo", "zhi", "y")


def nt(a, b):
    return lax.dot_general(a, b, (((1,), (1,)), ((), ())), preferred_element_type=jnp.float32)


def tn(a, b):
    return lax.dot_general(a, b, (((0,), (0,)), ((), ())), preferred_element_type=jnp.float32)


def nn(a, b):
    return jnp.dot(a, b, preferred_element_type=jnp.float32)


def attention_kernel(place_ref, order_ref, lens_ref, q_ref, do_ref, kv_ref, dq_ref, dkv_ref, bias_ref, dk_ref, dv_ref):
    scale = HD ** (-0.5)
    spans = order_ref.shape[1]
    docs = lens_ref.shape[1]
    place = place_ref[0]
    lane = lax.broadcasted_iota(jnp.int32, (1, 2 * SPAN), 1)
    pos_q = jnp.where(
        lane < SPAN,
        order_ref[0, 2 * place] * SPAN + lane,
        order_ref[0, 2 * place + 1] * SPAN + lane - SPAN,
    )
    start = jnp.zeros_like(pos_q)
    end = jnp.int32(0)
    for i in range(docs):
        end = end + lens_ref[0, i]
        start = jnp.where(pos_q >= end, end, start)
    row = lax.broadcasted_iota(jnp.int32, (SPAN, 2 * SPAN), 0)
    for s in range(spans):
        pos_k = order_ref[0, s] * SPAN + row
        allowed = (pos_k <= pos_q) & (pos_k >= start)
        bias_ref[s * SPAN : (s + 1) * SPAN, :] = jnp.where(allowed, 0.0, -jnp.inf)
    k = kv_ref[:, :HD]
    v = kv_ref[:, HD:]
    for h in range(0, HQ, 2):
        a, b, c = h * HD, (h + 1) * HD, (h + 2) * HD
        q2 = jnp.concatenate([q_ref[:, a:b], q_ref[:, b:c]], axis=0)
        d2 = jnp.concatenate([do_ref[:, a:b], do_ref[:, b:c]], axis=0)
        bias = bias_ref[...]
        s2 = nt(k, q2) + jnp.concatenate([bias, bias], axis=1)
        peak = jnp.max(s2, axis=0, keepdims=True)
        expo = jnp.exp2((s2 - peak) * (scale * LOG2E))
        inverse = 1.0 / jnp.sum(expo, axis=0, keepdims=True)
        probs = expo * inverse
        low = probs.astype(jnp.bfloat16)
        dp = nt(v, d2)
        delta = jnp.sum(low.astype(jnp.float32) * dp, axis=0, keepdims=True)
        ds = (probs * ((dp - delta) * scale)).astype(jnp.bfloat16)
        dv = nn(low, d2)
        dk = nn(ds, q2)
        if h == 0:
            dv_ref[...] = dv
            dk_ref[...] = dk
        elif h < HQ - 2:
            dv_ref[...] += dv
            dk_ref[...] += dk
        else:
            dkv_ref[:, HD:] = (dv_ref[...] + dv).astype(jnp.bfloat16)
            dkv_ref[:, :HD] = (dk_ref[...] + dk).astype(jnp.bfloat16)
        dq = tn(ds, k).astype(jnp.bfloat16)
        dq_ref[:, a:b] = dq[:HD]
        dq_ref[:, b:c] = dq[HD:]


def attention(place, order, lens, query, grad, key_value):
    tokens = query.shape[0]
    total = key_value.shape[0]
    smem = pl.BlockSpec(memory_space=pltpu.SMEM)
    vmem = pl.BlockSpec(memory_space=pltpu.VMEM)
    return pl.pallas_call(
        attention_kernel,
        out_shape=(
            jax.ShapeDtypeStruct((tokens, HQ * HD), jnp.bfloat16),
            jax.ShapeDtypeStruct((total, 2 * HD), jnp.bfloat16),
        ),
        in_specs=[smem, smem, smem, vmem, vmem, vmem],
        out_specs=(vmem, vmem),
        scratch_shapes=[
            pltpu.VMEM((total, tokens), jnp.float32),
            pltpu.VMEM((total, HD), jnp.float32),
            pltpu.VMEM((total, HD), jnp.float32),
        ],
        compiler_params=pltpu.CompilerParams(vmem_limit_bytes=24 * 1024 * 1024),
        cost_estimate=pl.CostEstimate(flops=2 * 10**9, bytes_accessed=4 * 10**6, transcendentals=10**6),
        name="attention",
    )(place, order, lens, query, grad, key_value)


def shifted(value, s):
    n = lax.axis_size("x")
    return lax.ppermute(value, "x", [(i, (i + s) % n) for i in range(n)])


def swapped(value):
    return lax.ppermute(value, "core", [(0, 1), (1, 0)])


def gather_chips(value):
    mine = jnp.concatenate([value] + [shifted(value, s) for s in range(1, lax.axis_size("x"))], axis=0)
    return mine, swapped(mine)


def local(layer_input, w_qkv, d_out, span_order, doc_lengths):
    rows = layer_input[0]
    tokens, features = rows.shape
    chips = lax.axis_size("x")
    zlos = lax.axis_size("zlo")
    at_x = lax.axis_index("x")
    at_core = lax.axis_index("core")
    seq = lax.axis_size("zhi") * lax.axis_size("y")
    place = lax.axis_index("zhi") * lax.axis_size("y") + lax.axis_index("y")
    width = features // (zlos * chips * 2)

    parts = rows.reshape(tokens, zlos, chips, 2 * width)
    pieces = []
    for s in range(chips):
        piece = lax.dynamic_index_in_dim(parts, (at_x + s) % chips, 2, keepdims=False)
        pieces.append(shifted(piece, s) if s else piece)
    pieces = jnp.stack(pieces).reshape(chips * tokens, zlos, 2, width)
    rows_own = lax.dynamic_index_in_dim(pieces, at_core, 2, keepdims=False).reshape(chips * tokens, zlos * width)
    rows_send = lax.dynamic_index_in_dim(pieces, 1 - at_core, 2, keepdims=False).reshape(chips * tokens, zlos * width)
    rows_other = swapped(rows_send)

    key_value = nn(rows, w_qkv[:, HQ * HD :]).astype(jnp.bfloat16)
    copies = jnp.broadcast_to(key_value[None], (seq, tokens, 2 * HD))
    gathered = lax.all_to_all(copies, SEQ, 0, 0, tiled=True).reshape(seq * tokens, 2 * HD)
    query = nn(rows, w_qkv[:, : HQ * HD]).astype(jnp.bfloat16)
    d_query, terms = attention(place[None], span_order, doc_lengths, query, d_out[0], gathered)
    arrived = lax.all_to_all(terms.reshape(seq, tokens, 2 * HD), SEQ, 0, 0, tiled=True)
    owned = jnp.sum(arrived.astype(jnp.float32), axis=0).astype(jnp.bfloat16)

    q_own, q_other = gather_chips(d_query)
    kv_own, kv_other = gather_chips(owned)
    grad_q = (tn(rows_own, q_own) + tn(rows_other, q_other)).astype(jnp.bfloat16)
    grad_kv = (tn(rows_own, kv_own) + tn(rows_other, kv_other)).astype(jnp.bfloat16)
    term = jnp.concatenate([grad_q, grad_kv], axis=1)
    owners = zlos * seq
    received = lax.all_to_all(term.reshape(owners, -1, term.shape[1]), OWN, 0, 0, tiled=True)
    d_w = jnp.sum(received.astype(jnp.float32), axis=0)

    d_qkv = jnp.concatenate([d_query, owned], axis=1)
    d_rows = nt(d_qkv, w_qkv).astype(jnp.bfloat16)
    return (d_rows[None], d_w)


def solution(mesh):
    fine = Mesh(mesh.devices.reshape(2, 4, 2, 2, 4), ("zlo", "x", "core", "zhi", "y"))
    dp, ctx = ("zlo", "x", "core"), ("zhi", "y")
    placed = (P(dp, ctx, None), P(), P(dp, ctx, None), P(dp, None), P(dp, None))
    return jax.shard_map(
        local,
        mesh=fine,
        in_specs=placed,
        out_specs=(P(dp, ctx, None), P(dp + ctx, None)),
        check_vma=False,
    )
```

```python
import jax
import jax.numpy as jnp
from jax import lax
from jax.experimental import pallas as pl
from jax.experimental.pallas import tpu as pltpu
from jax.sharding import Mesh, PartitionSpec as P

HD = 128
HQ = 8
SPAN = 64
LOG2E = 1.4426950408889634
SEQ = ("zhi", "y")
OWN = ("zlo", "zhi", "y")


def nt(a, b):
    return lax.dot_general(a, b, (((1,), (1,)), ((), ())), preferred_element_type=jnp.float32)


def tn(a, b):
    return lax.dot_general(a, b, (((0,), (0,)), ((), ())), preferred_element_type=jnp.float32)


def nn(a, b):
    return jnp.dot(a, b, preferred_element_type=jnp.float32)


SMEM = pl.BlockSpec(memory_space=pltpu.SMEM)
VMEM = pl.BlockSpec(memory_space=pltpu.VMEM)
MIB = 1024 * 1024


def project_kernel(x_ref, w_ref, out_ref, acc_ref):
    step = pl.program_id(0)
    part = nn(x_ref[...], w_ref[...])

    @pl.when(step == 0)
    def _():
        acc_ref[...] = part

    @pl.when(step > 0)
    def _():
        acc_ref[...] += part

    @pl.when(step == pl.num_programs(0) - 1)
    def _():
        low = acc_ref[...].astype(jnp.bfloat16)
        if len(out_ref.shape) == 3:
            for i in range(out_ref.shape[0]):
                out_ref[i] = low
        else:
            out_ref[...] = low


def project(x, w, first, width, copies, depth, name):
    tokens, features = x.shape
    shape = (copies, tokens, width) if copies else (tokens, width)
    return pl.pallas_call(
        project_kernel,
        grid=(features // depth,),
        out_shape=jax.ShapeDtypeStruct(shape, jnp.bfloat16),
        in_specs=[
            pl.BlockSpec((tokens, depth), lambda i: (0, i)),
            pl.BlockSpec((depth, width), lambda i: (i, first)),
        ],
        out_specs=pl.BlockSpec(shape, lambda i: (0,) * len(shape)),
        scratch_shapes=[pltpu.VMEM((tokens, width), jnp.float32)],
        compiler_params=pltpu.CompilerParams(vmem_limit_bytes=60 * MIB),
        cost_estimate=pl.CostEstimate(
            flops=2 * tokens * features * width, bytes_accessed=2 * features * (width + tokens), transcendentals=0
        ),
        name=name,
    )(x, w)


def pack_kernel(where_ref, x_ref, *out_refs):
    chips = len(out_refs)
    features = x_ref.shape[1]
    width = features // (4 * chips)
    for s in range(chips):
        chip = lax.rem(where_ref[0] + s, chips)
        for c in range(2):
            for z in range(2):
                at = pl.multiple_of(z * (features // 2) + chip * 2 * width + c * width, width)
                out_refs[s][(2 * c + z) * width : (2 * c + z + 1) * width, :] = x_ref[:, pl.ds(at, width)].T


def pack(where, x, chips):
    tokens, features = x.shape
    shape = jax.ShapeDtypeStruct((features // chips, tokens), x.dtype)
    return pl.pallas_call(
        pack_kernel,
        out_shape=(shape,) * chips,
        in_specs=[SMEM, VMEM],
        out_specs=(VMEM,) * chips,
        compiler_params=pltpu.CompilerParams(vmem_limit_bytes=16 * MIB),
        cost_estimate=pl.CostEstimate(flops=0, bytes_accessed=4 * tokens * features, transcendentals=0),
        name="pack",
    )(where, x)


def send_kernel(where_ref, *refs):
    pieces, out_ref, sem = refs[:-2], refs[-2], refs[-1]
    half = pieces[0].shape[0] // 2
    at = pl.multiple_of((1 - where_ref[1]) * half, half)
    copies = [pltpu.make_async_copy(piece.at[pl.ds(at, half), :], out_ref.at[i], sem.at[i]) for i, piece in enumerate(pieces)]
    for copy in copies:
        copy.start()
    for copy in copies:
        copy.wait()


def send_half(where, pieces):
    rows, tokens = pieces[0].shape
    n = len(pieces)
    anywhere = pl.BlockSpec(memory_space=pl.ANY)
    return pl.pallas_call(
        send_kernel,
        out_shape=jax.ShapeDtypeStruct((n, rows // 2, tokens), pieces[0].dtype),
        in_specs=[SMEM] + [anywhere] * n,
        out_specs=anywhere,
        scratch_shapes=[pltpu.SemaphoreType.DMA((n,))],
        cost_estimate=pl.CostEstimate(flops=0, bytes_accessed=2 * n * rows * tokens, transcendentals=0),
        name="send_half",
    )(where, *pieces)


def attention_kernel(heads, last, where_ref, order_ref, lens_ref, q_ref, do_ref, kv_ref, *refs):
    if last:
        dk_in, dv_in, dq_ref, dkv_ref, bias_ref, dk_ref, dv_ref = refs
    else:
        dq_ref, dk_ref, dv_ref, bias_ref = refs
    scale = HD ** (-0.5)
    spans = order_ref.shape[1]
    docs = lens_ref.shape[1]
    place = where_ref[2]
    lane = lax.broadcasted_iota(jnp.int32, (1, 2 * SPAN), 1)
    pos_q = jnp.where(
        lane < SPAN,
        order_ref[0, 2 * place] * SPAN + lane,
        order_ref[0, 2 * place + 1] * SPAN + lane - SPAN,
    )
    start = jnp.zeros_like(pos_q)
    end = jnp.int32(0)
    for i in range(docs):
        end = end + lens_ref[0, i]
        start = jnp.where(pos_q >= end, end, start)
    row = lax.broadcasted_iota(jnp.int32, (SPAN, 2 * SPAN), 0)
    for s in range(spans):
        pos_k = order_ref[0, s] * SPAN + row
        allowed = (pos_k <= pos_q) & (pos_k >= start)
        bias_ref[s * SPAN : (s + 1) * SPAN, :] = jnp.where(allowed, 0.0, -jnp.inf)
    k = kv_ref[:, :HD]
    v = kv_ref[:, HD:]
    for h in heads:
        a, b, c = h * HD, (h + 1) * HD, (h + 2) * HD
        q2 = jnp.concatenate([q_ref[:, a:b], q_ref[:, b:c]], axis=0)
        d2 = jnp.concatenate([do_ref[:, a:b], do_ref[:, b:c]], axis=0)
        bias = bias_ref[...]
        s2 = nt(k, q2) + jnp.concatenate([bias, bias], axis=1)
        peak = jnp.max(s2, axis=0, keepdims=True)
        expo = jnp.exp2((s2 - peak) * (scale * LOG2E))
        inverse = 1.0 / jnp.sum(expo, axis=0, keepdims=True)
        probs = expo * inverse
        low = probs.astype(jnp.bfloat16)
        dp = nt(v, d2)
        delta = jnp.sum(low.astype(jnp.float32) * dp, axis=0, keepdims=True)
        ds = (probs * ((dp - delta) * scale)).astype(jnp.bfloat16)
        dq = tn(ds, k).astype(jnp.bfloat16)
        o = (h - heads[0]) * HD
        dq_ref[:, o : o + HD] = dq[:HD]
        dq_ref[:, o + HD : o + 2 * HD] = dq[HD:]
        dv = nn(low, d2)
        dk = nn(ds, q2)
        if h == heads[0] and not last:
            dv_ref[...] = dv
            dk_ref[...] = dk
        else:
            if h == heads[0]:
                dv += dv_in[...]
                dk += dk_in[...]
            else:
                dv += dv_ref[...]
                dk += dk_ref[...]
            if h == heads[-1] and last:
                dkv_ref[:, :HD] = dk.astype(jnp.bfloat16)
                dkv_ref[:, HD:] = dv.astype(jnp.bfloat16)
            else:
                dv_ref[...] = dv
                dk_ref[...] = dk


def attention(heads, where, order, lens, query, grad, key_value, carried=()):
    tokens = query.shape[0]
    total = key_value.shape[0]
    last = bool(carried)
    count = len(heads) * 2
    sums = [jax.ShapeDtypeStruct((total, HD), jnp.float32)] * 2
    outs = [jax.ShapeDtypeStruct((tokens, count * HD), jnp.bfloat16)]
    outs += [jax.ShapeDtypeStruct((total, 2 * HD), jnp.bfloat16)] if last else sums
    scratch = [pltpu.VMEM((total, tokens), jnp.float32)]
    if last:
        scratch += [pltpu.VMEM((total, HD), jnp.float32)] * 2
    work = count * tokens * total
    return pl.pallas_call(
        lambda *refs: attention_kernel(heads, last, *refs),
        out_shape=tuple(outs),
        in_specs=[SMEM, SMEM, SMEM, VMEM, VMEM, VMEM] + [VMEM] * len(carried),
        out_specs=(VMEM,) * len(outs),
        scratch_shapes=scratch,
        compiler_params=pltpu.CompilerParams(vmem_limit_bytes=24 * MIB),
        cost_estimate=pl.CostEstimate(flops=10 * work * HD, bytes_accessed=4 * 10**6, transcendentals=work),
        name="attention_last" if last else "attention_first",
    )(where, order, lens, query, grad, key_value, *carried)


def term_kernel(chips, where_ref, *refs):
    x_own, x_other = refs[:chips], refs[chips]
    g_own, g_other = refs[chips + 1 : 2 * chips + 1], refs[2 * chips + 1 : 3 * chips + 1]
    out_ref = refs[-1]
    half = x_own[0].shape[0] // 2
    at = pl.multiple_of(where_ref[1] * half, half)
    left = [x[pl.ds(at, half), :] for x in x_own] + [x_other[i] for i in range(chips)]
    right = [g[...] for g in g_own] + [g[...] for g in g_other]
    out_ref[...] = nn(jnp.concatenate(left, axis=1), jnp.concatenate(right, axis=0)).astype(out_ref.dtype)


def term(where, x_own, x_other, g_own, g_other, name):
    chips = len(x_own)
    half, tokens = x_other.shape[1:]
    width = g_own[0].shape[1]
    return pl.pallas_call(
        lambda *refs: term_kernel(chips, *refs),
        out_shape=jax.ShapeDtypeStruct((half, width), jnp.bfloat16),
        in_specs=[SMEM] + [VMEM] * (3 * chips + 1),
        out_specs=VMEM,
        compiler_params=pltpu.CompilerParams(vmem_limit_bytes=24 * MIB),
        cost_estimate=pl.CostEstimate(
            flops=4 * chips * tokens * half * width, bytes_accessed=2 * half * width, transcendentals=0
        ),
        name=name,
    )(where, *x_own, x_other, *g_own, *g_other)


def shifted(value, s):
    n = lax.axis_size("x")
    return lax.ppermute(value, "x", [(i, (i + s) % n) for i in range(n)])


def swapped(value):
    return lax.ppermute(value, "core", [(0, 1), (1, 0)])


def gather_chips(value):
    own = [value] + [shifted(value, s) for s in range(1, lax.axis_size("x"))]
    return own, [swapped(piece) for piece in own]


def after(value, *others):
    return lax.optimization_barrier((value,) + others)[0]


def to_owners(value):
    owners = lax.axis_size("zlo") * lax.axis_size("zhi") * lax.axis_size("y")
    blocks = value.reshape(owners, value.shape[0] // owners, value.shape[1])
    return lax.all_to_all(blocks, OWN, 0, 0, tiled=True)


def local(layer_input, w_qkv, d_out, span_order, doc_lengths):
    rows = layer_input[0]
    tokens = rows.shape[0]
    chips = lax.axis_size("x")
    seq = lax.axis_size("zhi") * lax.axis_size("y")
    where = jnp.stack(
        [lax.axis_index("x"), lax.axis_index("core"), lax.axis_index("zhi") * lax.axis_size("y") + lax.axis_index("y")]
    ).astype(jnp.int32)

    copies = project(rows, w_qkv, HQ // 2, 2 * HD, seq, 2048, "project_kv")
    gathered = lax.all_to_all(copies, SEQ, 0, 0, tiled=True).reshape(seq * tokens, 2 * HD)

    packed = pack(where, after(rows, copies), chips)
    pieces = [packed[0]] + [shifted(packed[s], s) for s in range(1, chips)]

    query = project(after(rows, packed[0]), w_qkv, 0, HQ * HD, 0, 1024, "project_q")
    grad = d_out[0]
    dq_a, dk_a, dv_a = attention((0, 2, 4), where, span_order, doc_lengths, query, grad, gathered)
    own_a, other_a = gather_chips(dq_a)
    sent = send_half(where, [after(piece, dq_a) for piece in pieces])
    x_other = swapped(sent)
    dq_b, terms = attention((6,), where, span_order, doc_lengths, query, after(grad, sent), gathered, (dk_a, dv_a))
    arrived = lax.all_to_all(terms.reshape(seq, tokens, 2 * HD), SEQ, 0, 0, tiled=True)

    term_a = term(where, pieces, x_other, own_a, other_a, "term_a")
    owned = jnp.sum(arrived.astype(jnp.float32), axis=0).astype(jnp.bfloat16)
    ready = after(jnp.concatenate([dq_b, owned], axis=1), term_a)
    own_b, other_b = gather_chips(ready)
    received_a = to_owners(term_a)
    term_b = term(where, pieces, x_other, own_b, other_b, "term_b")
    received_b = to_owners(after(term_b, received_a))
    d_qkv = jnp.concatenate([dq_a, own_b[0]], axis=1)
    d_rows = nt(d_qkv, w_qkv).astype(jnp.bfloat16)
    d_w = jnp.concatenate(
        [jnp.sum(received_a.astype(jnp.float32), axis=0), jnp.sum(received_b.astype(jnp.float32), axis=0)], axis=1
    )
    return (d_rows[None], d_w)


def solution(mesh):
    fine = Mesh(mesh.devices.reshape(2, 4, 2, 2, 4), ("zlo", "x", "core", "zhi", "y"))
    dp, ctx = ("zlo", "x", "core"), ("zhi", "y")
    placed = (P(dp, ctx, None), P(), P(dp, ctx, None), P(dp, None), P(dp, None))
    return jax.shard_map(
        local,
        mesh=fine,
        in_specs=placed,
        out_specs=(P(dp, ctx, None), P(dp + ctx, None)),
        check_vma=False,
    )
```

```python
import jax
import jax.numpy as jnp
from jax import lax
from jax.experimental import pallas as pl
from jax.experimental.pallas import tpu as pltpu
from jax.sharding import Mesh, PartitionSpec as P

HD = 128
HQ = 8
SPAN = 64
LOG2E = 1.4426950408889634
SEQ = ("zhi", "y")
OWN = ("zlo", "zhi", "y")


def nt(a, b):
    return lax.dot_general(a, b, (((1,), (1,)), ((), ())), preferred_element_type=jnp.float32)


def tn(a, b):
    return lax.dot_general(a, b, (((0,), (0,)), ((), ())), preferred_element_type=jnp.float32)


def nn(a, b):
    return jnp.dot(a, b, preferred_element_type=jnp.float32)


SMEM = pl.BlockSpec(memory_space=pltpu.SMEM)
VMEM = pl.BlockSpec(memory_space=pltpu.VMEM)
MIB = 1024 * 1024


def first_kernel(chips, where_ref, x_ref, w_ref, kv_ref, *refs):
    out_refs, acc_ref = refs[:chips], refs[chips]
    step = pl.program_id(0)
    depth = w_ref.shape[0]
    part = nn(x_ref[:, pl.ds(pl.multiple_of(step * depth, depth), depth)], w_ref[...])

    features = x_ref.shape[1]
    width = features // (4 * chips)
    for s in range(chips):
        chip = lax.rem(where_ref[0] + s, chips)
        for z in range(2):
            at = pl.multiple_of(z * (features // 2) + chip * 2 * width + step * width, width)
            out_refs[s][z * width : (z + 1) * width, :] = x_ref[:, pl.ds(at, width)].T

    @pl.when(step == 0)
    def _():
        acc_ref[...] = part

    @pl.when(step > 0)
    def _():
        acc_ref[...] += part

    @pl.when(step == pl.num_programs(0) - 1)
    def _():
        low = acc_ref[...].astype(jnp.bfloat16)
        for i in range(kv_ref.shape[0]):
            kv_ref[i] = low


def first(where, x, w, copies, chips):
    tokens, features = x.shape
    width = 2 * HD
    depth = features // 2
    pieces = jax.ShapeDtypeStruct((features // chips, tokens), x.dtype)
    return pl.pallas_call(
        lambda *refs: first_kernel(chips, *refs),
        grid=(features // depth,),
        out_shape=(jax.ShapeDtypeStruct((copies, tokens, width), jnp.bfloat16),) + (pieces,) * chips,
        in_specs=[
            SMEM,
            pl.BlockSpec((tokens, features), lambda i: (0, 0)),
            pl.BlockSpec((depth, width), lambda i: (i, HQ // 2)),
        ],
        out_specs=(pl.BlockSpec((copies, tokens, width), lambda i: (0, 0, 0)),)
        + (pl.BlockSpec((features // chips // 2, tokens), lambda i: (i, 0)),) * chips,
        scratch_shapes=[pltpu.VMEM((tokens, width), jnp.float32)],
        compiler_params=pltpu.CompilerParams(vmem_limit_bytes=50 * MIB),
        cost_estimate=pl.CostEstimate(flops=2 * tokens * features * width, bytes_accessed=10 * MIB, transcendentals=0),
        name="first",
    )(where, x, w)


def query_kernel(x_ref, w_ref, out_ref):
    out_ref[...] = nn(x_ref[...], w_ref[...]).astype(jnp.bfloat16)


def project_query(x, w):
    tokens, features = x.shape
    width = 2 * HD
    return pl.pallas_call(
        query_kernel,
        grid=(HQ // 2,),
        out_shape=jax.ShapeDtypeStruct((tokens, HQ * HD), jnp.bfloat16),
        in_specs=[pl.BlockSpec((tokens, features), lambda i: (0, 0)), pl.BlockSpec((features, width), lambda i: (0, i))],
        out_specs=pl.BlockSpec((tokens, width), lambda i: (0, i)),
        compiler_params=pltpu.CompilerParams(vmem_limit_bytes=44 * MIB),
        cost_estimate=pl.CostEstimate(flops=2 * tokens * features * HQ * HD, bytes_accessed=20 * MIB, transcendentals=0),
        name="project_query",
    )(x, w)


def send_kernel(where_ref, *refs):
    pieces, out_ref = refs[:-1], refs[-1]
    half = pieces[0].shape[0] // 2
    at = pl.multiple_of((1 - where_ref[1]) * half, half)
    for i, piece in enumerate(pieces):
        out_ref[i] = piece[pl.ds(at, half), :]


def send_half(where, pieces):
    rows, tokens = pieces[0].shape
    n = len(pieces)
    return pl.pallas_call(
        send_kernel,
        out_shape=jax.ShapeDtypeStruct((n, rows // 2, tokens), pieces[0].dtype),
        in_specs=[SMEM] + [VMEM] * n,
        out_specs=VMEM,
        compiler_params=pltpu.CompilerParams(vmem_limit_bytes=8 * MIB),
        cost_estimate=pl.CostEstimate(flops=0, bytes_accessed=MIB, transcendentals=0),
        name="send_half",
    )(where, *pieces)


def join_kernel(where_ref, *refs):
    pieces, other, out_ref = refs[:-2], refs[-2], refs[-1]
    half, tokens = other.shape[1:]
    n = len(pieces)
    at = pl.multiple_of(where_ref[1] * half, half)
    for i in range(n):
        out_ref[:, i * tokens : (i + 1) * tokens] = pieces[i][pl.ds(at, half), :]
        out_ref[:, (n + i) * tokens : (n + i + 1) * tokens] = other[i]


def join(where, pieces, other):
    n, half, tokens = other.shape
    return pl.pallas_call(
        join_kernel,
        out_shape=jax.ShapeDtypeStruct((half, 2 * n * tokens), other.dtype),
        in_specs=[SMEM] + [VMEM] * (n + 1),
        out_specs=VMEM,
        compiler_params=pltpu.CompilerParams(vmem_limit_bytes=8 * MIB),
        cost_estimate=pl.CostEstimate(flops=0, bytes_accessed=MIB, transcendentals=0),
        name="join",
    )(where, *pieces, other)


def attention_kernel(where_ref, order_ref, lens_ref, q_ref, do_ref, kv_ref, dq_ref, dkv_ref, bias_ref, dk_ref, dv_ref):
    scale = HD ** (-0.5)
    spans = order_ref.shape[1]
    docs = lens_ref.shape[1]
    place = where_ref[2]
    lane = lax.broadcasted_iota(jnp.int32, (1, 2 * SPAN), 1)
    pos_q = jnp.where(
        lane < SPAN,
        order_ref[0, 2 * place] * SPAN + lane,
        order_ref[0, 2 * place + 1] * SPAN + lane - SPAN,
    )
    start = jnp.zeros_like(pos_q)
    end = jnp.int32(0)
    for i in range(docs):
        end = end + lens_ref[0, i]
        start = jnp.where(pos_q >= end, end, start)
    row = lax.broadcasted_iota(jnp.int32, (SPAN, 2 * SPAN), 0)
    for s in range(spans):
        pos_k = order_ref[0, s] * SPAN + row
        allowed = (pos_k <= pos_q) & (pos_k >= start)
        bias_ref[s * SPAN : (s + 1) * SPAN, :] = jnp.where(allowed, 0.0, -jnp.inf)
    k = kv_ref[:, :HD]
    v = kv_ref[:, HD:]
    for h in range(0, HQ, 2):
        a, b, c = h * HD, (h + 1) * HD, (h + 2) * HD
        q2 = jnp.concatenate([q_ref[:, a:b], q_ref[:, b:c]], axis=0)
        d2 = jnp.concatenate([do_ref[:, a:b], do_ref[:, b:c]], axis=0)
        bias = bias_ref[...]
        s2 = nt(k, q2) + jnp.concatenate([bias, bias], axis=1)
        peak = jnp.max(s2, axis=0, keepdims=True)
        expo = jnp.exp2((s2 - peak) * (scale * LOG2E))
        inverse = 1.0 / jnp.sum(expo, axis=0, keepdims=True)
        probs = expo * inverse
        low = probs.astype(jnp.bfloat16)
        dp = nt(v, d2)
        delta = jnp.sum(low.astype(jnp.float32) * dp, axis=0, keepdims=True)
        ds = (probs * ((dp - delta) * scale)).astype(jnp.bfloat16)
        dq = tn(ds, k).astype(jnp.bfloat16)
        dq_ref[:, a:b] = dq[:HD]
        dq_ref[:, b:c] = dq[HD:]
        dv = nn(low, d2)
        dk = nn(ds, q2)
        if h > 0:
            dv += dv_ref[...]
            dk += dk_ref[...]
        if h < HQ - 2:
            dv_ref[...] = dv
            dk_ref[...] = dk
        else:
            dkv_ref[:, :HD] = dk.astype(jnp.bfloat16)
            dkv_ref[:, HD:] = dv.astype(jnp.bfloat16)


def attention(where, order, lens, query, grad, key_value):
    tokens = query.shape[0]
    total = key_value.shape[0]
    work = HQ * tokens * total
    return pl.pallas_call(
        attention_kernel,
        out_shape=(
            jax.ShapeDtypeStruct((tokens, HQ * HD), jnp.bfloat16),
            jax.ShapeDtypeStruct((total, 2 * HD), jnp.bfloat16),
        ),
        in_specs=[SMEM, SMEM, SMEM, VMEM, VMEM, VMEM],
        out_specs=(VMEM, VMEM),
        scratch_shapes=[
            pltpu.VMEM((total, tokens), jnp.float32),
            pltpu.VMEM((total, HD), jnp.float32),
            pltpu.VMEM((total, HD), jnp.float32),
        ],
        compiler_params=pltpu.CompilerParams(vmem_limit_bytes=24 * MIB),
        cost_estimate=pl.CostEstimate(flops=10 * work * HD, bytes_accessed=4 * 10**6, transcendentals=work),
        name="attention",
    )(where, order, lens, query, grad, key_value)


def term_kernel(x_ref, *refs):
    pieces, out_ref = refs[:-1], refs[-1]
    step = 2 * HD
    for at in range(0, out_ref.shape[1], step):
        right = jnp.concatenate([g[:, at : at + step] for g in pieces], axis=0)
        out_ref[:, at : at + step] = nn(x_ref[...], right).astype(out_ref.dtype)


def term(joined, pieces, name):
    half, depth = joined.shape
    width = pieces[0].shape[1]
    return pl.pallas_call(
        term_kernel,
        out_shape=jax.ShapeDtypeStruct((half, width), jnp.bfloat16),
        in_specs=[VMEM] * (1 + len(pieces)),
        out_specs=VMEM,
        compiler_params=pltpu.CompilerParams(vmem_limit_bytes=16 * MIB),
        cost_estimate=pl.CostEstimate(flops=2 * depth * half * width, bytes_accessed=2 * half * width, transcendentals=0),
        name=name,
    )(joined, *pieces)


def last_kernel(x_ref, done_ref, *refs):
    pieces, out_ref = refs[:-1], refs[-1]
    width = done_ref.shape[1]
    right = jnp.concatenate([g[...] for g in pieces], axis=0)
    out_ref[:, width:] = nn(x_ref[...], right).astype(out_ref.dtype)
    out_ref[:, :width] = done_ref[...]


def last(joined, done, pieces):
    half, depth = joined.shape
    width = pieces[0].shape[1]
    return pl.pallas_call(
        last_kernel,
        out_shape=jax.ShapeDtypeStruct((half, done.shape[1] + width), jnp.bfloat16),
        in_specs=[VMEM] * (2 + len(pieces)),
        out_specs=VMEM,
        compiler_params=pltpu.CompilerParams(vmem_limit_bytes=16 * MIB),
        cost_estimate=pl.CostEstimate(flops=2 * depth * half * width, bytes_accessed=2 * half * width, transcendentals=0),
        name="term_kv",
    )(joined, done, *pieces)


def shifted(value, s):
    n = lax.axis_size("x")
    return lax.ppermute(value, "x", [(i, (i + s) % n) for i in range(n)])


def swapped(value):
    return lax.ppermute(value, "core", [(0, 1), (1, 0)])


def gather_chips(value):
    own = [value] + [shifted(value, s) for s in range(1, lax.axis_size("x"))]
    return own, [swapped(piece) for piece in own]


def after(value, *others):
    return lax.optimization_barrier((value,) + others)[0]


def to_owners(value):
    owners = lax.axis_size("zlo") * lax.axis_size("zhi") * lax.axis_size("y")
    blocks = value.reshape(owners, value.shape[0] // owners, value.shape[1])
    return lax.all_to_all(blocks, OWN, 0, 0, tiled=True)


def local(layer_input, w_qkv, d_out, span_order, doc_lengths):
    rows = layer_input[0]
    tokens = rows.shape[0]
    chips = lax.axis_size("x")
    seq = lax.axis_size("zhi") * lax.axis_size("y")
    where = jnp.stack(
        [lax.axis_index("x"), lax.axis_index("core"), lax.axis_index("zhi") * lax.axis_size("y") + lax.axis_index("y")]
    ).astype(jnp.int32)

    copies, *packed = first(where, rows, w_qkv, seq, chips)
    gathered = lax.all_to_all(copies, SEQ, 0, 0, tiled=True).reshape(seq * tokens, 2 * HD)
    pieces = [packed[0]] + [shifted(packed[s], s) for s in range(1, chips)]
    query = project_query(after(rows, packed[0]), w_qkv)
    d_query, terms = attention(where, span_order, doc_lengths, query, d_out[0], gathered)
    own_q, other_q = gather_chips(d_query)
    arrived = lax.all_to_all(terms.reshape(seq, tokens, 2 * HD), SEQ, 0, 0, tiled=True)

    pieces = [after(piece, terms) for piece in pieces]
    x_other = swapped(send_half(where, pieces))
    joined = join(where, pieces, x_other)
    term_q = term(joined, own_q + other_q, "term_q")
    owned = jnp.sum(arrived.astype(jnp.float32), axis=0).astype(jnp.bfloat16)
    own_kv, other_kv = gather_chips(owned)
    received = to_owners(last(joined, term_q, own_kv + other_kv))
    d_qkv = jnp.concatenate([d_query, owned], axis=1)
    d_rows = nt(d_qkv, w_qkv).astype(jnp.bfloat16)
    d_w = jnp.sum(received.astype(jnp.float32), axis=0)
    return (d_rows[None], d_w)


def solution(mesh):
    fine = Mesh(mesh.devices.reshape(2, 4, 2, 2, 4), ("zlo", "x", "core", "zhi", "y"))
    dp, ctx = ("zlo", "x", "core"), ("zhi", "y")
    placed = (P(dp, ctx, None), P(), P(dp, ctx, None), P(dp, None), P(dp, None))
    return jax.shard_map(
        local,
        mesh=fine,
        in_specs=placed,
        out_specs=(P(dp, ctx, None), P(dp + ctx, None)),
        check_vma=False,
    )
```

```python
import jax
import jax.numpy as jnp
from jax import lax
from jax.experimental import pallas as pl
from jax.experimental.pallas import tpu as pltpu
from jax.sharding import Mesh, PartitionSpec as P

HD = 128
HQ = 8
SPAN = 64
LOG2E = 1.4426950408889634
FIRST = 768
SEQ = ("zhi", "y")
DEPTH = ("zlo", "zhi")


def nt(a, b):
    return lax.dot_general(a, b, (((1,), (1,)), ((), ())), preferred_element_type=jnp.float32)


def tn(a, b):
    return lax.dot_general(a, b, (((0,), (0,)), ((), ())), preferred_element_type=jnp.float32)


def nn(a, b):
    return jnp.dot(a, b, preferred_element_type=jnp.float32)


SMEM = pl.BlockSpec(memory_space=pltpu.SMEM)
VMEM = pl.BlockSpec(memory_space=pltpu.VMEM)
MIB = 1024 * 1024
SMALL = pl.CostEstimate(flops=1, bytes_accessed=1, transcendentals=0)


def whole(value):
    return pl.BlockSpec(value.shape, lambda i: (0,) * value.ndim)


def pack_kernel(where_ref, x_ref, *out_refs):
    chips = len(out_refs)
    step = pl.program_id(0)
    features = x_ref.shape[1]
    width = features // (4 * chips)
    for s in range(chips):
        chip = lax.rem(where_ref[0] + s, chips)
        for z in range(2):
            at = pl.multiple_of(z * (features // 2) + chip * 2 * width + step * width, width)
            out_refs[s][z * width : (z + 1) * width, :] = x_ref[:, pl.ds(at, width)].T


def pack(where, x, chips):
    tokens, features = x.shape
    return pl.pallas_call(
        pack_kernel,
        grid=(2,),
        out_shape=(pltpu.HBM((features // chips, tokens), x.dtype),) * chips,
        in_specs=[SMEM, whole(x)],
        out_specs=(pl.BlockSpec((features // chips // 2, tokens), lambda i: (i, 0)),) * chips,
        compiler_params=pltpu.CompilerParams(vmem_limit_bytes=60 * MIB),
        cost_estimate=SMALL,
        name="pack",
    )(where, x)


def kv_kernel(x_ref, w_ref, kv_ref, acc_ref):
    step = pl.program_id(0)
    part = nn(x_ref[...], w_ref[...])

    @pl.when(step == 0)
    def _():
        acc_ref[...] = part

    @pl.when(step > 0)
    def _():
        acc_ref[...] += part

    @pl.when(step == pl.num_programs(0) - 1)
    def _():
        low = acc_ref[...].astype(jnp.bfloat16)
        for i in range(kv_ref.shape[0]):
            kv_ref[i] = low


def project_kv(x, w, copies):
    tokens, features = x.shape
    width = 2 * HD
    depth = features // 2
    return pl.pallas_call(
        kv_kernel,
        grid=(features // depth,),
        out_shape=pltpu.HBM((copies, tokens, width), jnp.bfloat16),
        in_specs=[
            pl.BlockSpec((tokens, depth), lambda i: (0, i)),
            pl.BlockSpec((depth, width), lambda i: (i, HQ // 2)),
        ],
        out_specs=pl.BlockSpec((copies, tokens, width), lambda i: (0, 0, 0)),
        scratch_shapes=[pltpu.VMEM((tokens, width), jnp.float32)],
        compiler_params=pltpu.CompilerParams(vmem_limit_bytes=60 * MIB),
        cost_estimate=SMALL,
        name="project_kv",
    )(x, w)


def query_kernel(x_ref, w_ref, out_ref):
    out_ref[...] = nn(x_ref[...], w_ref[...]).astype(jnp.bfloat16)


def project_query(x, w):
    tokens, features = x.shape
    width = 2 * HD
    return pl.pallas_call(
        query_kernel,
        grid=(HQ // 2,),
        out_shape=pltpu.HBM((tokens, HQ * HD), jnp.bfloat16),
        in_specs=[pl.BlockSpec((tokens, features), lambda i: (0, 0)), pl.BlockSpec((features, width), lambda i: (0, i))],
        out_specs=pl.BlockSpec((tokens, width), lambda i: (0, i)),
        compiler_params=pltpu.CompilerParams(vmem_limit_bytes=60 * MIB),
        cost_estimate=SMALL,
        name="project_query",
    )(x, w)


def halves_kernel(where_ref, *refs):
    pieces, own_ref, send_ref = refs[:-2], refs[-2], refs[-1]
    half, tokens = own_ref.shape[0], pieces[0].shape[1]
    own = pl.multiple_of(where_ref[1] * half, half)
    send = pl.multiple_of((1 - where_ref[1]) * half, half)
    for i, piece in enumerate(pieces):
        own_ref[:, i * tokens : (i + 1) * tokens] = piece[pl.ds(own, half), :]
        send_ref[:, i * tokens : (i + 1) * tokens] = piece[pl.ds(send, half), :]


def halves(where, pieces):
    rows, tokens = pieces[0].shape
    shape = (rows // 2, len(pieces) * tokens)
    return pl.pallas_call(
        halves_kernel,
        grid=(1,),
        out_shape=(pltpu.HBM(shape, jnp.bfloat16),) * 2,
        in_specs=[SMEM] + [whole(piece) for piece in pieces],
        out_specs=(pl.BlockSpec(shape, lambda i: (0, 0)),) * 2,
        compiler_params=pltpu.CompilerParams(vmem_limit_bytes=20 * MIB),
        cost_estimate=SMALL,
        name="halves",
    )(where, *pieces)


def attention_kernel(where_ref, order_ref, lens_ref, q_ref, do_ref, kv_ref, dq_ref, dkv_ref, bias_ref, dk_ref, dv_ref):
    scale = HD ** (-0.5)
    spans = order_ref.shape[1]
    docs = lens_ref.shape[1]
    place = where_ref[2]
    lane = lax.broadcasted_iota(jnp.int32, (1, 2 * SPAN), 1)
    pos_q = jnp.where(
        lane < SPAN,
        order_ref[0, 2 * place] * SPAN + lane,
        order_ref[0, 2 * place + 1] * SPAN + lane - SPAN,
    )
    start = jnp.zeros_like(pos_q)
    end = jnp.int32(0)
    for i in range(docs):
        end = end + lens_ref[0, i]
        start = jnp.where(pos_q >= end, end, start)
    row = lax.broadcasted_iota(jnp.int32, (SPAN, 2 * SPAN), 0)
    for s in range(spans):
        pos_k = order_ref[0, s] * SPAN + row
        allowed = (pos_k <= pos_q) & (pos_k >= start)
        bias_ref[s * SPAN : (s + 1) * SPAN, :] = jnp.where(allowed, 0.0, -jnp.inf)
    k = kv_ref[:, :HD]
    v = kv_ref[:, HD:]
    for h in range(0, HQ, 2):
        a, b, c = h * HD, (h + 1) * HD, (h + 2) * HD
        q2 = jnp.concatenate([q_ref[:, a:b], q_ref[:, b:c]], axis=0)
        d2 = jnp.concatenate([do_ref[:, a:b], do_ref[:, b:c]], axis=0)
        bias = bias_ref[...]
        s2 = nt(k, q2) + jnp.concatenate([bias, bias], axis=1)
        peak = jnp.max(s2, axis=0, keepdims=True)
        expo = jnp.exp2((s2 - peak) * (scale * LOG2E))
        inverse = 1.0 / jnp.sum(expo, axis=0, keepdims=True)
        probs = expo * inverse
        low = probs.astype(jnp.bfloat16)
        dp = nt(v, d2)
        delta = jnp.sum(low.astype(jnp.float32) * dp, axis=0, keepdims=True)
        ds = (probs * ((dp - delta) * scale)).astype(jnp.bfloat16)
        dq = tn(ds, k).astype(jnp.bfloat16)
        dq_ref[:, a:b] = dq[:HD]
        dq_ref[:, b:c] = dq[HD:]
        dv = nn(low, d2)
        dk = nn(ds, q2)
        if h > 0:
            dv += dv_ref[...]
            dk += dk_ref[...]
        if h < HQ - 2:
            dv_ref[...] = dv
            dk_ref[...] = dk
        else:
            dkv_ref[:, :HD] = dk.astype(jnp.bfloat16)
            dkv_ref[:, HD:] = dv.astype(jnp.bfloat16)


def attention(where, order, lens, query, grad, key_value):
    tokens = query.shape[0]
    total = key_value.shape[0]
    work = HQ * tokens * total
    return pl.pallas_call(
        attention_kernel,
        out_shape=(
            pltpu.HBM((tokens, HQ * HD), jnp.bfloat16),
            pltpu.HBM((total, 2 * HD), jnp.bfloat16),
        ),
        grid=(1,),
        in_specs=[SMEM, SMEM, SMEM] + [whole(v) for v in (query, grad, key_value)],
        out_specs=(whole(query), whole(key_value)),
        scratch_shapes=[
            pltpu.VMEM((total, tokens), jnp.float32),
            pltpu.VMEM((total, HD), jnp.float32),
            pltpu.VMEM((total, HD), jnp.float32),
        ],
        compiler_params=pltpu.CompilerParams(vmem_limit_bytes=24 * MIB),
        cost_estimate=SMALL,
        name="attention",
    )(where, order, lens, query, grad, key_value)


def both(x_own, x_other, pieces, at, width):
    n = len(pieces) // 2
    near = jnp.concatenate([g[:, pl.ds(at, width)] for g in pieces[:n]], axis=0)
    far = jnp.concatenate([g[:, pl.ds(at, width)] for g in pieces[n:]], axis=0)
    return nn(x_own, near) + nn(x_other, far)


def term_query_kernel(own_ref, other_ref, *refs):
    pieces, out_ref, done_ref = refs[:-2], refs[-2], refs[-1]
    step = pl.program_id(0)
    width = out_ref.shape[2]
    at = pl.multiple_of(step * width, width)
    part = both(own_ref[...], other_ref[...], pieces, at, width).astype(out_ref.dtype)
    blocks = out_ref.shape[0]
    rows = own_ref.shape[0] // (blocks * blocks)

    @pl.when(step < FIRST // (2 * HD))
    def _():
        for i in range(blocks):
            for y in range(blocks):
                here = (i * blocks + y) * rows
                out_ref[y, i * rows : (i + 1) * rows, :] = part[here : here + rows]

    @pl.when(step >= FIRST // (2 * HD))
    def _():
        done_ref[...] = part


def term_query(own, other, pieces, blocks):
    half, depth = own.shape
    width = pieces[0].shape[1]
    step = 2 * HD
    first = FIRST // step
    return pl.pallas_call(
        term_query_kernel,
        grid=(width // step,),
        out_shape=(
            pltpu.HBM((blocks, half // blocks, FIRST), jnp.bfloat16),
            pltpu.HBM((half, width - FIRST), jnp.bfloat16),
        ),
        in_specs=[whole(own), whole(other)] + [VMEM] * len(pieces),
        out_specs=(
            pl.BlockSpec((blocks, half // blocks, step), lambda j: (0, 0, jnp.minimum(j, first - 1))),
            pl.BlockSpec((half, step), lambda j: (0, jnp.maximum(j - first, 0))),
        ),
        compiler_params=pltpu.CompilerParams(vmem_limit_bytes=20 * MIB),
        cost_estimate=SMALL,
        name="term_query",
    )(own, other, *pieces)


def ring_block(where_ref, s):
    place = lax.rem(where_ref[3] + s, 4)
    return 2 * lax.rem(place, 2) + place // 2


def term_second_kernel(where_ref, own_ref, other_ref, done_ref, *refs):
    pieces, outs = refs[:-4], refs[-4:]
    rows = outs[0].shape[0]
    done = done_ref.shape[1]
    for s in range(4):
        at = pl.multiple_of(ring_block(where_ref, s) * rows, rows)
        outs[s][:, :done] = done_ref[pl.ds(at, rows), :]
        part = both(own_ref[pl.ds(at, rows), :], other_ref[pl.ds(at, rows), :], pieces, 0, pieces[0].shape[1])
        outs[s][:, done:] = part.astype(outs[s].dtype)


def term_second(where, own, other, done, pieces):
    half, depth = own.shape
    width = pieces[0].shape[1]
    out = pltpu.HBM((half // 4, done.shape[1] + width), jnp.bfloat16)
    return pl.pallas_call(
        term_second_kernel,
        grid=(1,),
        out_shape=(out,) * 4,
        in_specs=[SMEM] + [whole(value) for value in (own, other, done)] + [VMEM] * len(pieces),
        out_specs=(pl.BlockSpec(out.shape, lambda i: (0, 0)),) * 4,
        compiler_params=pltpu.CompilerParams(vmem_limit_bytes=20 * MIB),
        cost_estimate=SMALL,
        name="term_second",
    )(where, own, other, done, *pieces)


def middle_kernel(along_z, where_ref, *refs):
    parts, outs = refs[:-4], refs[-4:]
    rows = outs[0].shape[0]
    for s in range(4):
        block = ring_block(where_ref, s) if along_z else lax.rem(where_ref[4] + s, 4)
        at = pl.multiple_of(block * rows, rows)
        total = sum(part[pl.ds(at, rows), :].astype(jnp.float32) for part in parts)
        outs[s][...] = total.astype(outs[s].dtype)


def middle_stacked_kernel(where_ref, stack_ref, *outs):
    middle_kernel(True, where_ref, *[stack_ref.at[i] for i in range(stack_ref.shape[0])], *outs)


def middle(where, parts, along_z):
    stacked = len(parts) == 1
    rows, width = parts[0].shape[-2:]
    return pl.pallas_call(
        middle_stacked_kernel if stacked else lambda *refs: middle_kernel(along_z, *refs),
        grid=(1,),
        out_shape=(pltpu.HBM((rows // 4, width), jnp.float32),) + (pltpu.HBM((rows // 4, width), jnp.bfloat16),) * 3,
        in_specs=[SMEM] + [whole(part) for part in parts],
        out_specs=(pl.BlockSpec((rows // 4, width), lambda i: (0, 0)),) * 4,
        compiler_params=pltpu.CompilerParams(vmem_limit_bytes=14 * MIB),
        cost_estimate=SMALL,
        name="middle_z" if along_z else "middle_y",
    )(where, *parts)


def final_kernel(*refs):
    out_ref = refs[-1]
    out_ref[:, :FIRST] = sum(part[...].astype(jnp.float32) for part in refs[:4])
    out_ref[:, FIRST:] = sum(part[...].astype(jnp.float32) for part in refs[4:8])


def final(parts):
    rows = parts[0].shape[0]
    width = FIRST + parts[4].shape[1]
    return pl.pallas_call(
        final_kernel,
        out_shape=jax.ShapeDtypeStruct((rows, width), jnp.float32),
        in_specs=[VMEM] * 8,
        out_specs=VMEM,
        compiler_params=pltpu.CompilerParams(vmem_limit_bytes=8 * MIB),
        cost_estimate=SMALL,
        name="final",
    )(*parts)


def shifted(value, s):
    n = lax.axis_size("x")
    return lax.ppermute(value, "x", [(i, (i + s) % n) for i in range(n)])


def swapped(value):
    return lax.ppermute(value, "core", [(0, 1), (1, 0)])


def gather_chips(value):
    own = [value] + [shifted(value, s) for s in range(1, lax.axis_size("x"))]
    return own, [swapped(piece) for piece in own]


def after(value, *others):
    return lax.optimization_barrier((value,) + others)[0]


def ring_index(place):
    return 2 * (place % 2) + place // 2


def shifted_z(value, s):
    return lax.ppermute(value, DEPTH, [(ring_index(i), ring_index((i + s) % 4)) for i in range(4)])


def shifted_y(value, s):
    return lax.ppermute(value, "y", [(i, (i + s) % 4) for i in range(4)])


def local(layer_input, w_qkv, d_out, span_order, doc_lengths):
    rows = layer_input[0]
    tokens = rows.shape[0]
    chips = lax.axis_size("x")
    seq = lax.axis_size("zhi") * lax.axis_size("y")
    at_zlo, at_zhi, at_y = lax.axis_index("zlo"), lax.axis_index("zhi"), lax.axis_index("y")
    where = jnp.stack(
        [lax.axis_index("x"), lax.axis_index("core"), at_zhi * lax.axis_size("y") + at_y, at_zhi * 2 + at_zlo, at_y]
    ).astype(jnp.int32)

    packed = pack(where, rows, chips)
    rows = after(rows, packed[0])
    copies = project_kv(rows, w_qkv, seq)
    gathered = lax.all_to_all(copies, SEQ, 0, 0, tiled=True).reshape(seq * tokens, 2 * HD)
    pieces = [packed[0]] + [shifted(packed[s], s) for s in range(1, chips)]
    query = project_query(after(rows, copies), w_qkv)
    d_query, terms = attention(where, span_order, doc_lengths, query, d_out[0], gathered)
    own_q, other_q = gather_chips(d_query)
    arrived = lax.all_to_all(terms.reshape(seq, tokens, 2 * HD), SEQ, 0, 0, tiled=True)
    pieces = [after(piece, terms) for piece in pieces]
    x_own, x_send = halves(where, pieces)
    x_other = swapped(x_send)

    stacked, done = term_query(x_own, x_other, own_q + other_q, lax.axis_size("y"))
    group_y = lax.all_to_all(stacked, "y", 0, 0, tiled=True)
    owned = jnp.sum(arrived.astype(jnp.float32), axis=0).astype(jnp.bfloat16)
    own_kv, other_kv = gather_chips(owned)
    parts = term_second(where, x_own, x_other, done, own_kv + other_kv)
    d_qkv = jnp.concatenate([d_query, owned], axis=1)
    d_rows = nt(d_qkv, w_qkv).astype(jnp.bfloat16)
    group_z = [parts[0]] + [after(shifted_z(parts[s], s), d_rows) for s in range(1, 4)]

    sums_z = middle(where, [group_y], True)
    sums_y = middle(where, group_z, False)
    last = [sums_z[0]] + [shifted_z(sums_z[s], s) for s in range(1, 4)]
    last += [sums_y[0]] + [shifted_y(sums_y[s], s) for s in range(1, 4)]
    d_w = final(last)
    return (d_rows[None], d_w)


def solution(mesh):
    fine = Mesh(mesh.devices.reshape(2, 4, 2, 2, 4), ("zlo", "x", "core", "zhi", "y"))
    dp, ctx = ("zlo", "x", "core"), ("zhi", "y")
    placed = (P(dp, ctx, None), P(), P(dp, ctx, None), P(dp, None), P(dp, None))
    return jax.shard_map(
        local,
        mesh=fine,
        in_specs=placed,
        out_specs=(P(dp, ctx, None), P(dp + ctx, None)),
        check_vma=False,
    )
```

```python
import jax
import jax.numpy as jnp
from jax import lax
from jax.experimental import pallas as pl
from jax.experimental.pallas import tpu as pltpu
from jax.sharding import Mesh, PartitionSpec as P

HD = 128
HQ = 8
SPAN = 64
LOG2E = 1.4426950408889634
FIRST = 768
SEQ = ("zhi", "y")
DEPTH = ("zlo", "zhi")


def nt(a, b):
    return lax.dot_general(a, b, (((1,), (1,)), ((), ())), preferred_element_type=jnp.float32)


def tn(a, b):
    return lax.dot_general(a, b, (((0,), (0,)), ((), ())), preferred_element_type=jnp.float32)


def nn(a, b):
    return jnp.dot(a, b, preferred_element_type=jnp.float32)


SMEM = pl.BlockSpec(memory_space=pltpu.SMEM)
VMEM = pl.BlockSpec(memory_space=pltpu.VMEM)
MIB = 1024 * 1024
SMALL = pl.CostEstimate(flops=1, bytes_accessed=1, transcendentals=0)


def whole(value):
    return pl.BlockSpec(value.shape, lambda i: (0,) * value.ndim)


def pack_kernel(where_ref, x_ref, *out_refs):
    chips = len(out_refs)
    step = pl.program_id(0)
    features = x_ref.shape[1]
    width = features // (4 * chips)
    for s in range(chips):
        chip = lax.rem(where_ref[0] + s, chips)
        for z in range(2):
            at = pl.multiple_of(z * (features // 2) + chip * 2 * width + step * width, width)
            out_refs[s][z * width : (z + 1) * width, :] = x_ref[:, pl.ds(at, width)].T


def pack(where, x, chips):
    tokens, features = x.shape
    return pl.pallas_call(
        pack_kernel,
        grid=(2,),
        out_shape=(pltpu.HBM((features // chips, tokens), x.dtype),) * chips,
        in_specs=[SMEM, whole(x)],
        out_specs=(pl.BlockSpec((features // chips // 2, tokens), lambda i: (i, 0)),) * chips,
        compiler_params=pltpu.CompilerParams(vmem_limit_bytes=60 * MIB),
        cost_estimate=SMALL,
        name="pack",
    )(where, x)


def kv_kernel(x_ref, w_ref, kv_ref, acc_ref):
    step = pl.program_id(0)
    part = nn(x_ref[...], w_ref[...])

    @pl.when(step == 0)
    def _():
        acc_ref[...] = part

    @pl.when(step > 0)
    def _():
        acc_ref[...] += part

    @pl.when(step == pl.num_programs(0) - 1)
    def _():
        low = acc_ref[...].astype(jnp.bfloat16)
        for i in range(kv_ref.shape[0]):
            kv_ref[i] = low


def project_kv(x, w, copies):
    tokens, features = x.shape
    width = 2 * HD
    depth = features // 2
    return pl.pallas_call(
        kv_kernel,
        grid=(features // depth,),
        out_shape=pltpu.HBM((copies, tokens, width), jnp.bfloat16),
        in_specs=[
            pl.BlockSpec((tokens, depth), lambda i: (0, i)),
            pl.BlockSpec((depth, width), lambda i: (i, HQ // 2)),
        ],
        out_specs=pl.BlockSpec((copies, tokens, width), lambda i: (0, 0, 0)),
        scratch_shapes=[pltpu.VMEM((tokens, width), jnp.float32)],
        compiler_params=pltpu.CompilerParams(vmem_limit_bytes=60 * MIB),
        cost_estimate=SMALL,
        name="project_kv",
    )(x, w)


def query_kernel(x_ref, w_ref, out_ref):
    out_ref[...] = nn(x_ref[...], w_ref[...]).astype(jnp.bfloat16)


def project_query(x, w):
    tokens, features = x.shape
    width = 2 * HD
    return pl.pallas_call(
        query_kernel,
        grid=(HQ // 2,),
        out_shape=jax.ShapeDtypeStruct((tokens, HQ * HD), jnp.bfloat16),
        in_specs=[pl.BlockSpec((tokens, features), lambda i: (0, 0)), pl.BlockSpec((features, width), lambda i: (0, i))],
        out_specs=pl.BlockSpec((tokens, width), lambda i: (0, i)),
        compiler_params=pltpu.CompilerParams(vmem_limit_bytes=44 * MIB),
        cost_estimate=SMALL,
        name="project_query",
    )(x, w)


def halves(where_ref, pieces, own_ref, send_ref):
    half, tokens = own_ref.shape[0], pieces[0].shape[1]
    own = pl.multiple_of(where_ref[1] * half, half)
    send = pl.multiple_of((1 - where_ref[1]) * half, half)
    for i, piece in enumerate(pieces):
        own_ref[:, i * tokens : (i + 1) * tokens] = piece[pl.ds(own, half), :]
        send_ref[:, i * tokens : (i + 1) * tokens] = piece[pl.ds(send, half), :]


def attention_kernel(where_ref, order_ref, lens_ref, q_ref, do_ref, kv_ref, *refs):
    pieces, (dq_ref, dkv_ref, own_ref, send_ref, bias_ref, dk_ref, dv_ref) = refs[:-7], refs[-7:]
    halves(where_ref, pieces, own_ref, send_ref)
    scale = HD ** (-0.5)
    spans = order_ref.shape[1]
    docs = lens_ref.shape[1]
    place = where_ref[2]
    lane = lax.broadcasted_iota(jnp.int32, (1, 2 * SPAN), 1)
    pos_q = jnp.where(
        lane < SPAN,
        order_ref[0, 2 * place] * SPAN + lane,
        order_ref[0, 2 * place + 1] * SPAN + lane - SPAN,
    )
    start = jnp.zeros_like(pos_q)
    end = jnp.int32(0)
    for i in range(docs):
        end = end + lens_ref[0, i]
        start = jnp.where(pos_q >= end, end, start)
    row = lax.broadcasted_iota(jnp.int32, (SPAN, 2 * SPAN), 0)
    for s in range(spans):
        pos_k = order_ref[0, s] * SPAN + row
        allowed = (pos_k <= pos_q) & (pos_k >= start)
        bias_ref[s * SPAN : (s + 1) * SPAN, :] = jnp.where(allowed, 0.0, -jnp.inf)
    k = kv_ref[:, :HD]
    v = kv_ref[:, HD:]
    for h in range(0, HQ, 2):
        a, b, c = h * HD, (h + 1) * HD, (h + 2) * HD
        q2 = jnp.concatenate([q_ref[:, a:b], q_ref[:, b:c]], axis=0)
        d2 = jnp.concatenate([do_ref[:, a:b], do_ref[:, b:c]], axis=0)
        bias = bias_ref[...]
        s2 = nt(k, q2) + jnp.concatenate([bias, bias], axis=1)
        peak = jnp.max(s2, axis=0, keepdims=True)
        expo = jnp.exp2((s2 - peak) * (scale * LOG2E))
        inverse = 1.0 / jnp.sum(expo, axis=0, keepdims=True)
        probs = expo * inverse
        low = probs.astype(jnp.bfloat16)
        dp = nt(v, d2)
        delta = jnp.sum(low.astype(jnp.float32) * dp, axis=0, keepdims=True)
        ds = (probs * ((dp - delta) * scale)).astype(jnp.bfloat16)
        dq = tn(ds, k).astype(jnp.bfloat16)
        dq_ref[:, a:b] = dq[:HD]
        dq_ref[:, b:c] = dq[HD:]
        dv = nn(low, d2)
        dk = nn(ds, q2)
        if h > 0:
            dv += dv_ref[...]
            dk += dk_ref[...]
        if h < HQ - 2:
            dv_ref[...] = dv
            dk_ref[...] = dk
        else:
            dkv_ref[:, :HD] = dk.astype(jnp.bfloat16)
            dkv_ref[:, HD:] = dv.astype(jnp.bfloat16)


def attention(where, order, lens, query, grad, key_value, pieces):
    rows, width = pieces[0].shape
    half = jax.ShapeDtypeStruct((rows // 2, width * len(pieces)), jnp.bfloat16)
    tokens = query.shape[0]
    total = key_value.shape[0]
    return pl.pallas_call(
        attention_kernel,
        out_shape=(
            pltpu.HBM((tokens, HQ * HD), jnp.bfloat16),
            pltpu.HBM((total, 2 * HD), jnp.bfloat16),
            pltpu.HBM(half.shape, half.dtype),
            pltpu.HBM(half.shape, half.dtype),
        ),
        grid=(1,),
        in_specs=[SMEM] * 3 + [VMEM] * (3 + len(pieces)),
        out_specs=(whole(query), whole(key_value), whole(half), whole(half)),
        scratch_shapes=[
            pltpu.VMEM((total, tokens), jnp.float32),
            pltpu.VMEM((total, HD), jnp.float32),
            pltpu.VMEM((total, HD), jnp.float32),
        ],
        compiler_params=pltpu.CompilerParams(vmem_limit_bytes=30 * MIB),
        cost_estimate=SMALL,
        name="attention",
    )(where, order, lens, query, grad, key_value, *pieces)


def both(x_own, x_other, pieces, at, width):
    n = len(pieces) // 2
    near = jnp.concatenate([g[:, pl.ds(at, width)] for g in pieces[:n]], axis=0)
    far = jnp.concatenate([g[:, pl.ds(at, width)] for g in pieces[n:]], axis=0)
    return nn(x_own, near) + nn(x_other, far)


def term_query_kernel(own_ref, other_ref, *refs):
    pieces, out_ref, done_ref = refs[:-2], refs[-2], refs[-1]
    step = pl.program_id(0)
    width = out_ref.shape[2]
    at = pl.multiple_of(step * width, width)
    part = both(own_ref[...], other_ref[...], pieces, at, width).astype(out_ref.dtype)
    blocks = out_ref.shape[0]
    rows = own_ref.shape[0] // (blocks * blocks)

    @pl.when(step < FIRST // (2 * HD))
    def _():
        for i in range(blocks):
            for y in range(blocks):
                here = (i * blocks + y) * rows
                out_ref[y, i * rows : (i + 1) * rows, :] = part[here : here + rows]

    @pl.when(step >= FIRST // (2 * HD))
    def _():
        done_ref[...] = part


def term_query(own, other, pieces, blocks):
    half, depth = own.shape
    width = pieces[0].shape[1]
    step = 2 * HD
    first = FIRST // step
    return pl.pallas_call(
        term_query_kernel,
        grid=(width // step,),
        out_shape=(
            pltpu.HBM((blocks, half // blocks, FIRST), jnp.bfloat16),
            pltpu.HBM((half, width - FIRST), jnp.bfloat16),
        ),
        in_specs=[VMEM] * (2 + len(pieces)),
        out_specs=(
            pl.BlockSpec((blocks, half // blocks, step), lambda j: (0, 0, jnp.minimum(j, first - 1))),
            pl.BlockSpec((half, step), lambda j: (0, jnp.maximum(j - first, 0))),
        ),
        compiler_params=pltpu.CompilerParams(vmem_limit_bytes=20 * MIB),
        cost_estimate=SMALL,
        name="term_query",
    )(own, other, *pieces)


def ring_block(where_ref, s):
    place = lax.rem(where_ref[3] + s, 4)
    return 2 * lax.rem(place, 2) + place // 2


def term_second_kernel(where_ref, own_ref, other_ref, done_ref, *refs):
    pieces, outs = refs[:-4], refs[-4:]
    rows = outs[0].shape[0]
    done = done_ref.shape[1]
    for s in range(4):
        at = pl.multiple_of(ring_block(where_ref, s) * rows, rows)
        outs[s][:, :done] = done_ref[pl.ds(at, rows), :]
        part = both(own_ref[pl.ds(at, rows), :], other_ref[pl.ds(at, rows), :], pieces, 0, pieces[0].shape[1])
        outs[s][:, done:] = part.astype(outs[s].dtype)


def term_second(where, own, other, done, pieces):
    half, depth = own.shape
    width = pieces[0].shape[1]
    out = pltpu.HBM((half // 4, done.shape[1] + width), jnp.bfloat16)
    return pl.pallas_call(
        term_second_kernel,
        grid=(1,),
        out_shape=(out,) * 4,
        in_specs=[SMEM] + [VMEM] * (3 + len(pieces)),
        out_specs=(pl.BlockSpec(out.shape, lambda i: (0, 0)),) * 4,
        compiler_params=pltpu.CompilerParams(vmem_limit_bytes=20 * MIB),
        cost_estimate=SMALL,
        name="term_second",
    )(where, own, other, done, *pieces)


def middle_kernel(along_z, where_ref, *refs):
    parts, outs = refs[:-4], refs[-4:]
    rows = outs[0].shape[0]
    for s in range(4):
        block = ring_block(where_ref, s) if along_z else lax.rem(where_ref[4] + s, 4)
        at = pl.multiple_of(block * rows, rows)
        total = sum(part[pl.ds(at, rows), :].astype(jnp.float32) for part in parts)
        outs[s][...] = total.astype(outs[s].dtype)


def middle_stacked_kernel(where_ref, stack_ref, *outs):
    middle_kernel(True, where_ref, *[stack_ref.at[i] for i in range(stack_ref.shape[0])], *outs)


def middle(where, parts, along_z):
    stacked = len(parts) == 1
    rows, width = parts[0].shape[-2:]
    return pl.pallas_call(
        middle_stacked_kernel if stacked else lambda *refs: middle_kernel(along_z, *refs),
        grid=(1,),
        out_shape=(jax.ShapeDtypeStruct((rows // 4, width), jnp.float32),) + (pltpu.HBM((rows // 4, width), jnp.bfloat16),) * 3,
        in_specs=[SMEM] + [VMEM] * len(parts),
        out_specs=(VMEM,) + (pl.BlockSpec((rows // 4, width), lambda i: (0, 0)),) * 3,
        compiler_params=pltpu.CompilerParams(vmem_limit_bytes=14 * MIB),
        cost_estimate=SMALL,
        name="middle_z" if along_z else "middle_y",
    )(where, *parts)


def final_kernel(*refs):
    out_ref = refs[-1]
    out_ref[:, :FIRST] = sum(part[...].astype(jnp.float32) for part in refs[:4])
    out_ref[:, FIRST:] = sum(part[...].astype(jnp.float32) for part in refs[4:8])


def final(parts):
    rows = parts[0].shape[0]
    width = FIRST + parts[4].shape[1]
    return pl.pallas_call(
        final_kernel,
        out_shape=jax.ShapeDtypeStruct((rows, width), jnp.float32),
        in_specs=[VMEM] * 8,
        out_specs=VMEM,
        compiler_params=pltpu.CompilerParams(vmem_limit_bytes=8 * MIB),
        cost_estimate=SMALL,
        name="final",
    )(*parts)


def shifted(value, s):
    n = lax.axis_size("x")
    return lax.ppermute(value, "x", [(i, (i + s) % n) for i in range(n)])


def swapped(value):
    return lax.ppermute(value, "core", [(0, 1), (1, 0)])


def gather_chips(value, *others):
    own = [value] + [shifted(value, s) for s in range(1, lax.axis_size("x"))]
    return own, [swapped(after(piece, *others)) for piece in own]


def after(value, *others):
    if not others:
        return value
    return lax.optimization_barrier((value,) + others)[0]


def ring_index(place):
    return 2 * (place % 2) + place // 2


def shifted_z(value, s):
    return lax.ppermute(value, DEPTH, [(ring_index(i), ring_index((i + s) % 4)) for i in range(4)])


def shifted_y(value, s):
    return lax.ppermute(value, "y", [(i, (i + s) % 4) for i in range(4)])


def local(layer_input, w_qkv, d_out, span_order, doc_lengths):
    rows = layer_input[0]
    tokens = rows.shape[0]
    chips = lax.axis_size("x")
    seq = lax.axis_size("zhi") * lax.axis_size("y")
    at_zlo, at_zhi, at_y = lax.axis_index("zlo"), lax.axis_index("zhi"), lax.axis_index("y")
    where = jnp.stack(
        [lax.axis_index("x"), lax.axis_index("core"), at_zhi * lax.axis_size("y") + at_y, at_zhi * 2 + at_zlo, at_y]
    ).astype(jnp.int32)

    packed = pack(where, rows, chips)
    rows = after(rows, packed[0])
    copies = project_kv(rows, w_qkv, seq)
    gathered = lax.all_to_all(copies, SEQ, 0, 0, tiled=True).reshape(seq * tokens, 2 * HD)
    pieces = [packed[0]] + [shifted(packed[s], s) for s in range(1, chips)]
    query = project_query(after(rows, copies), w_qkv)
    d_query, terms, x_own, x_send = attention(where, span_order, doc_lengths, query, d_out[0], gathered, pieces)
    own_q, other_q = gather_chips(d_query)
    arrived = lax.all_to_all(after(terms, other_q[0]).reshape(seq, tokens, 2 * HD), SEQ, 0, 0, tiled=True)
    x_other = swapped(x_send)

    stacked, done = term_query(x_own, x_other, own_q + other_q, lax.axis_size("y"))
    group_y = lax.all_to_all(stacked, "y", 0, 0, tiled=True)
    owned = jnp.sum(arrived.astype(jnp.float32), axis=0).astype(jnp.bfloat16)
    own_kv, other_kv = gather_chips(after(owned, *other_q), done)
    parts = term_second(where, x_own, x_other, done, own_kv + other_kv)
    d_qkv = jnp.concatenate([d_query, owned], axis=1)
    d_rows = nt(d_qkv, w_qkv).astype(jnp.bfloat16)
    group_z = [parts[0]] + [after(shifted_z(parts[s], s), d_rows) for s in range(1, 4)]

    sums_z = middle(where, [group_y], True)
    sums_y = middle(where, group_z, False)
    last = [sums_z[0]] + [shifted_z(sums_z[s], s) for s in range(1, 4)]
    last += [sums_y[0]] + [shifted_y(sums_y[s], s) for s in range(1, 4)]
    d_w = final(last)
    return (d_rows[None], d_w)


def solution(mesh):
    fine = Mesh(mesh.devices.reshape(2, 4, 2, 2, 4), ("zlo", "x", "core", "zhi", "y"))
    dp, ctx = ("zlo", "x", "core"), ("zhi", "y")
    placed = (P(dp, ctx, None), P(), P(dp, ctx, None), P(dp, None), P(dp, None))
    return jax.shard_map(
        local,
        mesh=fine,
        in_specs=placed,
        out_specs=(P(dp, ctx, None), P(dp + ctx, None)),
        check_vma=False,
    )
```

```python
import jax
import jax.numpy as jnp
from jax import lax
from jax.experimental import pallas as pl
from jax.experimental.pallas import tpu as pltpu
from jax.sharding import Mesh, PartitionSpec as P

HD = 128
HQ = 8
SPAN = 64
LOG2E = 1.4426950408889634
FIRST = 768
SEQ = ("zhi", "y")
DEPTH = ("zlo", "zhi")


def nt(a, b):
    return lax.dot_general(a, b, (((1,), (1,)), ((), ())), preferred_element_type=jnp.float32)


def tn(a, b):
    return lax.dot_general(a, b, (((0,), (0,)), ((), ())), preferred_element_type=jnp.float32)


def nn(a, b):
    return jnp.dot(a, b, preferred_element_type=jnp.float32)


SMEM = pl.BlockSpec(memory_space=pltpu.SMEM)
VMEM = pl.BlockSpec(memory_space=pltpu.VMEM)
MIB = 1024 * 1024
SMALL = pl.CostEstimate(flops=1, bytes_accessed=1, transcendentals=0)


def whole(value):
    return pl.BlockSpec(value.shape, lambda i: (0,) * value.ndim)


def pack_kernel(where_ref, x_ref, *out_refs):
    chips = len(out_refs)
    step = pl.program_id(0)
    features = x_ref.shape[1]
    width = features // (4 * chips)
    for s in range(chips):
        chip = lax.rem(where_ref[0] + s, chips)
        for z in range(2):
            at = pl.multiple_of(z * (features // 2) + chip * 2 * width + step * width, width)
            out_refs[s][z * width : (z + 1) * width, :] = x_ref[:, pl.ds(at, width)].T


def pack(where, x, chips):
    tokens, features = x.shape
    return pl.pallas_call(
        pack_kernel,
        grid=(2,),
        out_shape=(pltpu.HBM((features // chips, tokens), x.dtype),) * chips,
        in_specs=[SMEM, whole(x)],
        out_specs=(pl.BlockSpec((features // chips // 2, tokens), lambda i: (i, 0)),) * chips,
        compiler_params=pltpu.CompilerParams(vmem_limit_bytes=60 * MIB),
        cost_estimate=SMALL,
        name="pack",
    )(where, x)


def kv_kernel(x_ref, w_ref, kv_ref, acc_ref):
    step = pl.program_id(0)
    part = nn(x_ref[...], w_ref[...])

    @pl.when(step == 0)
    def _():
        acc_ref[...] = part

    @pl.when(step > 0)
    def _():
        acc_ref[...] += part

    @pl.when(step == pl.num_programs(0) - 1)
    def _():
        low = acc_ref[...].astype(jnp.bfloat16)
        for i in range(kv_ref.shape[0]):
            kv_ref[i] = low


def project_kv(x, w, copies):
    tokens, features = x.shape
    width = 2 * HD
    depth = features // 2
    return pl.pallas_call(
        kv_kernel,
        grid=(features // depth,),
        out_shape=pltpu.HBM((copies, tokens, width), jnp.bfloat16),
        in_specs=[
            pl.BlockSpec((tokens, depth), lambda i: (0, i)),
            pl.BlockSpec((depth, width), lambda i: (i, HQ // 2)),
        ],
        out_specs=pl.BlockSpec((copies, tokens, width), lambda i: (0, 0, 0)),
        scratch_shapes=[pltpu.VMEM((tokens, width), jnp.float32)],
        compiler_params=pltpu.CompilerParams(vmem_limit_bytes=60 * MIB),
        cost_estimate=SMALL,
        name="project_kv",
    )(x, w)


def query_kernel(x_ref, w_ref, out_ref):
    out_ref[...] = nn(x_ref[...], w_ref[...]).astype(jnp.bfloat16)


def project_query(x, w):
    tokens, features = x.shape
    width = 2 * HD
    return pl.pallas_call(
        query_kernel,
        grid=(HQ // 2,),
        out_shape=jax.ShapeDtypeStruct((tokens, HQ * HD), jnp.bfloat16),
        in_specs=[pl.BlockSpec((tokens, features), lambda i: (0, 0)), pl.BlockSpec((features, width), lambda i: (0, i))],
        out_specs=pl.BlockSpec((tokens, width), lambda i: (0, i)),
        compiler_params=pltpu.CompilerParams(vmem_limit_bytes=44 * MIB),
        cost_estimate=SMALL,
        name="project_query",
    )(x, w)


def halves_kernel(where_ref, *refs):
    pieces, own_ref, send_ref = refs[:-2], refs[-2], refs[-1]
    half, tokens = own_ref.shape[0], pieces[0].shape[1]
    own = pl.multiple_of(where_ref[1] * half, half)
    send = pl.multiple_of((1 - where_ref[1]) * half, half)
    for i, piece in enumerate(pieces):
        own_ref[:, i * tokens : (i + 1) * tokens] = piece[pl.ds(own, half), :]
        send_ref[:, i * tokens : (i + 1) * tokens] = piece[pl.ds(send, half), :]


def halves(where, pieces):
    rows, tokens = pieces[0].shape
    n = len(pieces)
    shape = (rows // 2, n * tokens)
    return pl.pallas_call(
        halves_kernel,
        grid=(1,),
        out_shape=(pltpu.HBM(shape, jnp.bfloat16),) * 2,
        in_specs=[SMEM] + [VMEM] * n,
        out_specs=(pl.BlockSpec(shape, lambda i: (0, 0)),) * 2,
        compiler_params=pltpu.CompilerParams(vmem_limit_bytes=20 * MIB),
        cost_estimate=SMALL,
        name="halves",
    )(where, *pieces)


def attention_kernel(where_ref, order_ref, lens_ref, q_ref, do_ref, kv_ref, *refs):
    dq_ref, dkv_ref, bias_ref, dk_ref, dv_ref = refs
    scale = HD ** (-0.5)
    spans = order_ref.shape[1]
    docs = lens_ref.shape[1]
    place = where_ref[2]
    lane = lax.broadcasted_iota(jnp.int32, (1, 2 * SPAN), 1)
    pos_q = jnp.where(
        lane < SPAN,
        order_ref[0, 2 * place] * SPAN + lane,
        order_ref[0, 2 * place + 1] * SPAN + lane - SPAN,
    )
    start = jnp.zeros_like(pos_q)
    end = jnp.int32(0)
    for i in range(docs):
        end = end + lens_ref[0, i]
        start = jnp.where(pos_q >= end, end, start)
    row = lax.broadcasted_iota(jnp.int32, (SPAN, 2 * SPAN), 0)
    for s in range(spans):
        pos_k = order_ref[0, s] * SPAN + row
        allowed = (pos_k <= pos_q) & (pos_k >= start)
        bias_ref[s * SPAN : (s + 1) * SPAN, :] = jnp.where(allowed, 0.0, -jnp.inf)
    k = kv_ref[:, :HD]
    v = kv_ref[:, HD:]
    for h in range(0, HQ, 2):
        a, b, c = h * HD, (h + 1) * HD, (h + 2) * HD
        q2 = jnp.concatenate([q_ref[:, a:b], q_ref[:, b:c]], axis=0)
        d2 = jnp.concatenate([do_ref[:, a:b], do_ref[:, b:c]], axis=0)
        bias = bias_ref[...]
        s2 = nt(k, q2) + jnp.concatenate([bias, bias], axis=1)
        peak = jnp.max(s2, axis=0, keepdims=True)
        expo = jnp.exp2((s2 - peak) * (scale * LOG2E))
        inverse = 1.0 / jnp.sum(expo, axis=0, keepdims=True)
        probs = expo * inverse
        low = probs.astype(jnp.bfloat16)
        dp = nt(v, d2)
        delta = jnp.sum(low.astype(jnp.float32) * dp, axis=0, keepdims=True)
        ds = (probs * ((dp - delta) * scale)).astype(jnp.bfloat16)
        dq = tn(ds, k).astype(jnp.bfloat16)
        dq_ref[:, a:b] = dq[:HD]
        dq_ref[:, b:c] = dq[HD:]
        dv = nn(low, d2)
        dk = nn(ds, q2)
        if h > 0:
            dv += dv_ref[...]
            dk += dk_ref[...]
        if h < HQ - 2:
            dv_ref[...] = dv
            dk_ref[...] = dk
        else:
            dkv_ref[:, :HD] = dk.astype(jnp.bfloat16)
            dkv_ref[:, HD:] = dv.astype(jnp.bfloat16)


def attention(where, order, lens, query, grad, key_value):
    tokens = query.shape[0]
    total = key_value.shape[0]
    return pl.pallas_call(
        attention_kernel,
        out_shape=(
            pltpu.HBM((tokens, HQ * HD), jnp.bfloat16),
            pltpu.HBM((total, 2 * HD), jnp.bfloat16),
        ),
        grid=(1,),
        in_specs=[SMEM] * 3 + [VMEM] * 3,
        out_specs=(whole(query), whole(key_value)),
        scratch_shapes=[
            pltpu.VMEM((total, tokens), jnp.float32),
            pltpu.VMEM((total, HD), jnp.float32),
            pltpu.VMEM((total, HD), jnp.float32),
        ],
        compiler_params=pltpu.CompilerParams(vmem_limit_bytes=30 * MIB),
        cost_estimate=SMALL,
        name="attention",
    )(where, order, lens, query, grad, key_value)


def term_query_kernel(*refs):
    parts, pieces, out_ref, done_ref = refs[:2], refs[2:-2], refs[-2], refs[-1]
    step = pl.program_id(0)
    width = out_ref.shape[2]
    at = pl.multiple_of(step * width, width)
    left = jnp.concatenate([part[...] for part in parts], axis=1)
    right = jnp.concatenate([g[:, pl.ds(at, width)] for g in pieces], axis=0)
    part = nn(left, right).astype(out_ref.dtype)
    blocks = out_ref.shape[0]
    rows = left.shape[0] // (blocks * blocks)

    @pl.when(step < FIRST // (2 * HD))
    def _():
        for i in range(blocks):
            for y in range(blocks):
                here = (i * blocks + y) * rows
                out_ref[y, i * rows : (i + 1) * rows, :] = part[here : here + rows]

    @pl.when(step >= FIRST // (2 * HD))
    def _():
        done_ref[...] = part


def term_query(parts, pieces, blocks):
    half = parts[0].shape[0]
    width = pieces[0].shape[1]
    step = 2 * HD
    first = FIRST // step
    return pl.pallas_call(
        term_query_kernel,
        grid=(width // step,),
        out_shape=(
            pltpu.HBM((blocks, half // blocks, FIRST), jnp.bfloat16),
            pltpu.HBM((half, width - FIRST), jnp.bfloat16),
        ),
        in_specs=[VMEM] * (len(parts) + len(pieces)),
        out_specs=(
            pl.BlockSpec((blocks, half // blocks, step), lambda j: (0, 0, jnp.minimum(j, first - 1))),
            pl.BlockSpec((half, step), lambda j: (0, jnp.maximum(j - first, 0))),
        ),
        compiler_params=pltpu.CompilerParams(vmem_limit_bytes=20 * MIB),
        cost_estimate=SMALL,
        name="term_query",
    )(*parts, *pieces)


def ring_block(where_ref, s):
    place = lax.rem(where_ref[3] + s, 4)
    return 2 * lax.rem(place, 2) + place // 2


def term_second_kernel(where_ref, *refs):
    parts, done_ref, pieces, outs = refs[:2], refs[2], refs[3:-4], refs[-4:]
    rows = outs[0].shape[0]
    done = done_ref.shape[1]
    right = jnp.concatenate([g[...] for g in pieces], axis=0)
    for s in range(4):
        at = pl.multiple_of(ring_block(where_ref, s) * rows, rows)
        left = jnp.concatenate([part[pl.ds(at, rows), :] for part in parts], axis=1)
        outs[s][:, :done] = done_ref[pl.ds(at, rows), :]
        outs[s][:, done:] = nn(left, right).astype(outs[s].dtype)


def term_second(where, parts, done, pieces):
    half = parts[0].shape[0]
    width = pieces[0].shape[1]
    out = pltpu.HBM((half // 4, done.shape[1] + width), jnp.bfloat16)
    return pl.pallas_call(
        term_second_kernel,
        grid=(1,),
        out_shape=(out,) * 4,
        in_specs=[SMEM] + [VMEM] * (1 + len(parts) + len(pieces)),
        out_specs=(pl.BlockSpec(out.shape, lambda i: (0, 0)),) * 4,
        compiler_params=pltpu.CompilerParams(vmem_limit_bytes=60 * MIB),
        cost_estimate=SMALL,
        name="term_second",
    )(where, *parts, done, *pieces)


def middle_z_kernel(stack_ref, out_ref):
    rows = out_ref.shape[1]
    for i in range(out_ref.shape[0]):
        parts = [stack_ref[j, i * rows : (i + 1) * rows, :].astype(jnp.float32) for j in range(stack_ref.shape[0])]
        out_ref[i] = sum(parts).astype(out_ref.dtype)


def middle_z(stack):
    blocks, rows, width = stack.shape
    out = pltpu.HBM((blocks, rows // blocks, width), jnp.bfloat16)
    return pl.pallas_call(
        middle_z_kernel,
        grid=(1,),
        out_shape=out,
        in_specs=[VMEM],
        out_specs=pl.BlockSpec(out.shape, lambda i: (0, 0, 0)),
        compiler_params=pltpu.CompilerParams(vmem_limit_bytes=14 * MIB),
        cost_estimate=SMALL,
        name="middle_z",
    )(stack)


def middle_y_kernel(where_ref, *refs):
    parts, outs = refs[:-4], refs[-4:]
    rows = outs[0].shape[0]
    for s in range(4):
        at = pl.multiple_of(lax.rem(where_ref[4] + s, 4) * rows, rows)
        total = sum(part[pl.ds(at, rows), :].astype(jnp.float32) for part in parts)
        outs[s][...] = total.astype(outs[s].dtype)


def middle_y(where, parts):
    rows, width = parts[0].shape
    return pl.pallas_call(
        middle_y_kernel,
        grid=(1,),
        out_shape=(jax.ShapeDtypeStruct((rows // 4, width), jnp.float32),) + (pltpu.HBM((rows // 4, width), jnp.bfloat16),) * 3,
        in_specs=[SMEM] + [VMEM] * len(parts),
        out_specs=(VMEM,) + (pl.BlockSpec((rows // 4, width), lambda i: (0, 0)),) * 3,
        compiler_params=pltpu.CompilerParams(vmem_limit_bytes=14 * MIB),
        cost_estimate=SMALL,
        name="middle_y",
    )(where, *parts)


def final_kernel(stack_ref, *refs):
    parts, out_ref = refs[:-1], refs[-1]
    out_ref[:, :FIRST] = sum(stack_ref[i].astype(jnp.float32) for i in range(stack_ref.shape[0]))
    out_ref[:, FIRST:] = sum(part[...].astype(jnp.float32) for part in parts)


def final(stack, parts):
    rows = stack.shape[1]
    width = FIRST + parts[0].shape[1]
    return pl.pallas_call(
        final_kernel,
        out_shape=jax.ShapeDtypeStruct((rows, width), jnp.float32),
        in_specs=[VMEM] * 5,
        out_specs=VMEM,
        compiler_params=pltpu.CompilerParams(vmem_limit_bytes=8 * MIB),
        cost_estimate=SMALL,
        name="final",
    )(stack, *parts)


def shifted(value, s):
    n = lax.axis_size("x")
    return lax.ppermute(value, "x", [(i, (i + s) % n) for i in range(n)])


def swapped(value):
    return lax.ppermute(value, "core", [(0, 1), (1, 0)])


def gather_chips(value, *others):
    own = [value] + [shifted(value, s) for s in range(1, lax.axis_size("x"))]
    return own, [swapped(after(piece, *others)) for piece in own]


def after(value, *others):
    if not others:
        return value
    return lax.optimization_barrier((value,) + others)[0]


def ring_index(place):
    return 2 * (place % 2) + place // 2


def shifted_z(value, s):
    return lax.ppermute(value, DEPTH, [(ring_index(i), ring_index((i + s) % 4)) for i in range(4)])


def shifted_y(value, s):
    return lax.ppermute(value, "y", [(i, (i + s) % 4) for i in range(4)])


def local(layer_input, w_qkv, d_out, span_order, doc_lengths):
    rows = layer_input[0]
    tokens = rows.shape[0]
    chips = lax.axis_size("x")
    seq = lax.axis_size("zhi") * lax.axis_size("y")
    at_zlo, at_zhi, at_y = lax.axis_index("zlo"), lax.axis_index("zhi"), lax.axis_index("y")
    where = jnp.stack(
        [lax.axis_index("x"), lax.axis_index("core"), at_zhi * lax.axis_size("y") + at_y, at_zhi * 2 + at_zlo, at_y]
    ).astype(jnp.int32)

    packed = pack(where, rows, chips)
    rows = after(rows, packed[0])
    copies = project_kv(rows, w_qkv, seq)
    gathered = lax.all_to_all(copies, SEQ, 0, 0, tiled=True).reshape(seq * tokens, 2 * HD)
    pieces = [packed[0]] + [shifted(packed[s], s) for s in range(1, chips)]
    query = project_query(after(rows, copies), w_qkv)
    d_query, terms = attention(where, span_order, doc_lengths, query, d_out[0], gathered)
    own_q, other_q = gather_chips(d_query)
    arrived = lax.all_to_all(after(terms, other_q[0]).reshape(seq, tokens, 2 * HD), SEQ, 0, 0, tiled=True)
    x_own, x_send = halves(where, [after(piece, terms) for piece in pieces])
    columns = [x_own, swapped(x_send)]

    stacked, done = term_query(columns, own_q + other_q, lax.axis_size("y"))
    group_y = lax.all_to_all(stacked, "y", 0, 0, tiled=True)
    owned = jnp.sum(arrived.astype(jnp.float32), axis=0).astype(jnp.bfloat16)
    own_kv, other_kv = gather_chips(after(owned, done))
    parts = term_second(where, columns, done, own_kv + other_kv)
    second_z = lax.all_to_all(middle_z(group_y), DEPTH, 0, 0, tiled=True)
    d_qkv = after(jnp.concatenate([d_query, owned], axis=1), group_y)
    d_rows = nt(d_qkv, w_qkv).astype(jnp.bfloat16)
    group_z = [parts[0]] + [after(shifted_z(parts[s], s), d_rows) for s in range(1, 4)]
    sums = middle_y(where, group_z)
    d_w = final(second_z, [sums[0]] + [shifted_y(sums[s], s) for s in range(1, 4)])
    return (d_rows[None], d_w)


def solution(mesh):
    fine = Mesh(mesh.devices.reshape(2, 4, 2, 2, 4), ("zlo", "x", "core", "zhi", "y"))
    dp, ctx = ("zlo", "x", "core"), ("zhi", "y")
    placed = (P(dp, ctx, None), P(), P(dp, ctx, None), P(dp, None), P(dp, None))
    return jax.shard_map(
        local,
        mesh=fine,
        in_specs=placed,
        out_specs=(P(dp, ctx, None), P(dp + ctx, None)),
        check_vma=False,
    )
```

```python
import jax
import jax.numpy as jnp
from jax import lax
from jax.experimental import pallas as pl
from jax.experimental.pallas import tpu as pltpu
from jax.sharding import Mesh, PartitionSpec as P

HD = 128
HQ = 8
SPAN = 64
LOG2E = 1.4426950408889634
SEQ = ("zhi", "y")
DEPTH = ("zlo", "zhi")


def nt(a, b):
    return lax.dot_general(a, b, (((1,), (1,)), ((), ())), preferred_element_type=jnp.float32)


def tn(a, b):
    return lax.dot_general(a, b, (((0,), (0,)), ((), ())), preferred_element_type=jnp.float32)


def nn(a, b):
    return jnp.dot(a, b, preferred_element_type=jnp.float32)


SMEM = pl.BlockSpec(memory_space=pltpu.SMEM)
VMEM = pl.BlockSpec(memory_space=pltpu.VMEM)
MIB = 1024 * 1024
SMALL = pl.CostEstimate(flops=1, bytes_accessed=1, transcendentals=0)


def whole(value):
    return pl.BlockSpec(value.shape, lambda i: (0,) * value.ndim)


def first_kernel(where_ref, x_hbm, w_hbm, kv_hbm, *refs):
    chips = len(refs) - 7
    out_hbm = refs[:chips]
    x_ref, w_ref, piece_ref, kv_ref, in_sem, piece_sem, kv_sem = refs[chips:]
    features = x_ref.shape[1]
    width = features // (4 * chips)
    chunks = in_sem.shape[0] - 1
    depth = features // chunks
    load_x = pltpu.make_async_copy(x_hbm, x_ref, in_sem.at[chunks])
    load_x.start()
    loads = []
    for i in range(chunks):
        rows = pl.ds(i * depth, depth)
        loads.append(pltpu.make_async_copy(w_hbm.at[rows, pl.ds(HQ * HD, 2 * HD)], w_ref.at[rows, :], in_sem.at[i]))
        loads[i].start()
    load_x.wait()
    stores = []
    for s in range(chips):
        chip = lax.rem(where_ref[0] + s, chips)
        for c in range(2):
            for z in range(2):
                at = pl.multiple_of(z * (features // 2) + chip * 2 * width + c * width, width)
                piece_ref[s, (2 * c + z) * width : (2 * c + z + 1) * width, :] = x_ref[:, pl.ds(at, width)].T
        stores.append(pltpu.make_async_copy(piece_ref.at[s], out_hbm[s], piece_sem.at[s]))
        stores[s].start()
    total = None
    for i in range(chunks):
        loads[i].wait()
        part = nn(x_ref[:, i * depth : (i + 1) * depth], w_ref[i * depth : (i + 1) * depth, :])
        total = part if total is None else total + part
    kv_ref[...] = total.astype(jnp.bfloat16)
    copies = kv_hbm.shape[0]
    for i in range(copies):
        stores.append(pltpu.make_async_copy(kv_ref, kv_hbm.at[i], kv_sem.at[i]))
        stores[-1].start()
    for store in stores:
        store.wait()


def first(where, x, w, copies, chips):
    tokens, features = x.shape
    width = 2 * HD
    anywhere = pl.BlockSpec(memory_space=pltpu.HBM)
    return pl.pallas_call(
        first_kernel,
        out_shape=(pltpu.HBM((copies, tokens, width), jnp.bfloat16),)
        + (pltpu.HBM((features // chips, tokens), x.dtype),) * chips,
        in_specs=[SMEM, anywhere, anywhere],
        out_specs=(anywhere,) * (chips + 1),
        scratch_shapes=[
            pltpu.VMEM((tokens, features), x.dtype),
            pltpu.VMEM((features, width), x.dtype),
            pltpu.VMEM((chips, features // chips, tokens), x.dtype),
            pltpu.VMEM((tokens, width), jnp.bfloat16),
            pltpu.SemaphoreType.DMA((5,)),
            pltpu.SemaphoreType.DMA((chips,)),
            pltpu.SemaphoreType.DMA((copies,)),
        ],
        compiler_params=pltpu.CompilerParams(vmem_limit_bytes=60 * MIB),
        cost_estimate=SMALL,
        name="first",
    )(where, x, w)


def query_kernel(x_ref, w_ref, out_ref):
    out_ref[...] = nn(x_ref[...], w_ref[...]).astype(jnp.bfloat16)


def project_query(x, w):
    tokens, features = x.shape
    width = 2 * HD
    return pl.pallas_call(
        query_kernel,
        grid=(HQ // 2,),
        out_shape=jax.ShapeDtypeStruct((tokens, HQ * HD), jnp.bfloat16),
        in_specs=[pl.BlockSpec((tokens, features), lambda i: (0, 0)), pl.BlockSpec((features, width), lambda i: (0, i))],
        out_specs=pl.BlockSpec((tokens, width), lambda i: (0, i)),
        compiler_params=pltpu.CompilerParams(vmem_limit_bytes=44 * MIB),
        cost_estimate=SMALL,
        name="project_query",
    )(x, w)


def halves_kernel(where_ref, *refs):
    pieces, own_ref, send_ref = refs[:-2], refs[-2], refs[-1]
    half, tokens = own_ref.shape[0], pieces[0].shape[1]
    own = pl.multiple_of(where_ref[1] * half, half)
    send = pl.multiple_of((1 - where_ref[1]) * half, half)
    for i, piece in enumerate(pieces):
        own_ref[:, i * tokens : (i + 1) * tokens] = piece[pl.ds(own, half), :]
        send_ref[:, i * tokens : (i + 1) * tokens] = piece[pl.ds(send, half), :]


def halves(where, pieces):
    rows, tokens = pieces[0].shape
    n = len(pieces)
    shape = (rows // 2, n * tokens)
    return pl.pallas_call(
        halves_kernel,
        grid=(1,),
        out_shape=(pltpu.HBM(shape, jnp.bfloat16),) * 2,
        in_specs=[SMEM] + [VMEM] * n,
        out_specs=(pl.BlockSpec(shape, lambda i: (0, 0)),) * 2,
        compiler_params=pltpu.CompilerParams(vmem_limit_bytes=60 * MIB),
        cost_estimate=SMALL,
        name="halves",
    )(where, *pieces)


def attention_kernel(where_ref, order_ref, lens_ref, q_ref, do_ref, kv_ref, *refs):
    dq_ref, dkv_ref, bias_ref, dk_ref, dv_ref = refs
    scale = HD ** (-0.5)
    spans = order_ref.shape[1]
    docs = lens_ref.shape[1]
    place = where_ref[2]
    lane = lax.broadcasted_iota(jnp.int32, (1, 2 * SPAN), 1)
    pos_q = jnp.where(
        lane < SPAN,
        order_ref[0, 2 * place] * SPAN + lane,
        order_ref[0, 2 * place + 1] * SPAN + lane - SPAN,
    )
    start = jnp.zeros_like(pos_q)
    end = jnp.int32(0)
    for i in range(docs):
        end = end + lens_ref[0, i]
        start = jnp.where(pos_q >= end, end, start)
    row = lax.broadcasted_iota(jnp.int32, (SPAN, 2 * SPAN), 0)
    for s in range(spans):
        pos_k = order_ref[0, s] * SPAN + row
        allowed = (pos_k <= pos_q) & (pos_k >= start)
        bias_ref[s * SPAN : (s + 1) * SPAN, :] = jnp.where(allowed, 0.0, -jnp.inf)
    k = kv_ref[:, :HD]
    v = kv_ref[:, HD:]
    for h in range(0, HQ, 2):
        a, b, c = h * HD, (h + 1) * HD, (h + 2) * HD
        q2 = jnp.concatenate([q_ref[:, a:b], q_ref[:, b:c]], axis=0)
        d2 = jnp.concatenate([do_ref[:, a:b], do_ref[:, b:c]], axis=0)
        bias = bias_ref[...]
        s2 = nt(k, q2) + jnp.concatenate([bias, bias], axis=1)
        peak = jnp.max(s2, axis=0, keepdims=True)
        expo = jnp.exp2((s2 - peak) * (scale * LOG2E))
        inverse = 1.0 / jnp.sum(expo, axis=0, keepdims=True)
        probs = expo * inverse
        low = probs.astype(jnp.bfloat16)
        dp = nt(v, d2)
        delta = jnp.sum(low.astype(jnp.float32) * dp, axis=0, keepdims=True)
        ds = (probs * ((dp - delta) * scale)).astype(jnp.bfloat16)
        dq = tn(ds, k).astype(jnp.bfloat16)
        dq_ref[:, a:b] = dq[:HD]
        dq_ref[:, b:c] = dq[HD:]
        dv = nn(low, d2)
        dk = nn(ds, q2)
        if h > 0:
            dv += dv_ref[...]
            dk += dk_ref[...]
        if h < HQ - 2:
            dv_ref[...] = dv
            dk_ref[...] = dk
        else:
            dkv_ref[:, :HD] = dk.astype(jnp.bfloat16)
            dkv_ref[:, HD:] = dv.astype(jnp.bfloat16)


def attention(where, order, lens, query, grad, key_value):
    tokens = query.shape[0]
    total = key_value.shape[0]
    return pl.pallas_call(
        attention_kernel,
        out_shape=(
            pltpu.HBM((tokens, HQ * HD), jnp.bfloat16),
            pltpu.HBM((total, 2 * HD), jnp.bfloat16),
        ),
        grid=(1,),
        in_specs=[SMEM] * 3 + [VMEM] * 3,
        out_specs=(whole(query), whole(key_value)),
        scratch_shapes=[
            pltpu.VMEM((total, tokens), jnp.float32),
            pltpu.VMEM((total, HD), jnp.float32),
            pltpu.VMEM((total, HD), jnp.float32),
        ],
        compiler_params=pltpu.CompilerParams(vmem_limit_bytes=30 * MIB),
        cost_estimate=SMALL,
        name="attention",
    )(where, order, lens, query, grad, key_value)


def term_query_kernel(*refs):
    parts, pieces, out_ref = refs[:2], refs[2:-1], refs[-1]
    step = pl.program_id(0)
    width = out_ref.shape[2]
    at = pl.multiple_of(step * width, width)
    left = jnp.concatenate([part[...] for part in parts], axis=1)
    right = jnp.concatenate([g[:, pl.ds(at, width)] for g in pieces], axis=0)
    part = nn(left, right).astype(out_ref.dtype)
    blocks = out_ref.shape[0]
    rows = left.shape[0] // (blocks * blocks)
    for i in range(blocks):
        for y in range(blocks):
            here = (i * blocks + y) * rows
            out_ref[y, i * rows : (i + 1) * rows, :] = part[here : here + rows]


def term_query(parts, pieces, blocks):
    half = parts[0].shape[0]
    width = pieces[0].shape[1]
    step = 2 * HD
    return pl.pallas_call(
        term_query_kernel,
        grid=(width // step,),
        out_shape=pltpu.HBM((blocks, half // blocks, width), jnp.bfloat16),
        in_specs=[VMEM] * (len(parts) + len(pieces)),
        out_specs=pl.BlockSpec((blocks, half // blocks, step), lambda j: (0, 0, j)),
        compiler_params=pltpu.CompilerParams(vmem_limit_bytes=20 * MIB),
        cost_estimate=SMALL,
        name="term_query",
    )(*parts, *pieces)


def ring_block(where_ref, s):
    place = lax.rem(where_ref[3] + s, 4)
    return 2 * lax.rem(place, 2) + place // 2


def term_second_kernel(where_ref, *refs):
    parts, pieces, outs = refs[:2], refs[2:-4], refs[-4:]
    rows = outs[0].shape[0]
    right = jnp.concatenate([g[...] for g in pieces], axis=0)
    for s in range(4):
        at = pl.multiple_of(ring_block(where_ref, s) * rows, rows)
        left = jnp.concatenate([part[pl.ds(at, rows), :] for part in parts], axis=1)
        outs[s][...] = nn(left, right).astype(outs[s].dtype)


def term_second(where, parts, pieces):
    half = parts[0].shape[0]
    width = pieces[0].shape[1]
    out = pltpu.HBM((half // 4, width), jnp.bfloat16)
    return pl.pallas_call(
        term_second_kernel,
        grid=(1,),
        out_shape=(out,) * 4,
        in_specs=[SMEM] + [VMEM] * (len(parts) + len(pieces)),
        out_specs=(pl.BlockSpec(out.shape, lambda i: (0, 0)),) * 4,
        compiler_params=pltpu.CompilerParams(vmem_limit_bytes=60 * MIB),
        cost_estimate=SMALL,
        name="term_second",
    )(where, *parts, *pieces)


def middle_z_kernel(stack_ref, out_ref):
    rows = out_ref.shape[1]
    for i in range(out_ref.shape[0]):
        parts = [stack_ref[j, i * rows : (i + 1) * rows, :].astype(jnp.float32) for j in range(stack_ref.shape[0])]
        out_ref[i] = sum(parts).astype(out_ref.dtype)


def middle_z(stack):
    blocks, rows, width = stack.shape
    out = pltpu.HBM((blocks, rows // blocks, width), jnp.bfloat16)
    return pl.pallas_call(
        middle_z_kernel,
        grid=(1,),
        out_shape=out,
        in_specs=[VMEM],
        out_specs=pl.BlockSpec(out.shape, lambda i: (0, 0, 0)),
        compiler_params=pltpu.CompilerParams(vmem_limit_bytes=14 * MIB),
        cost_estimate=SMALL,
        name="middle_z",
    )(stack)


def middle_y_kernel(where_ref, *refs):
    parts, outs = refs[:-4], refs[-4:]
    rows = outs[0].shape[0]
    for s in range(4):
        at = pl.multiple_of(lax.rem(where_ref[4] + s, 4) * rows, rows)
        total = sum(part[pl.ds(at, rows), :].astype(jnp.float32) for part in parts)
        outs[s][...] = total.astype(outs[s].dtype)


def middle_y(where, parts):
    rows, width = parts[0].shape
    return pl.pallas_call(
        middle_y_kernel,
        grid=(1,),
        out_shape=(jax.ShapeDtypeStruct((rows // 4, width), jnp.float32),) + (pltpu.HBM((rows // 4, width), jnp.bfloat16),) * 3,
        in_specs=[SMEM] + [VMEM] * len(parts),
        out_specs=(VMEM,) + (pl.BlockSpec((rows // 4, width), lambda i: (0, 0)),) * 3,
        compiler_params=pltpu.CompilerParams(vmem_limit_bytes=14 * MIB),
        cost_estimate=SMALL,
        name="middle_y",
    )(where, *parts)


def final_kernel(stack_ref, *refs):
    parts, out_ref = refs[:-1], refs[-1]
    first = stack_ref.shape[2]
    out_ref[:, :first] = sum(stack_ref[i].astype(jnp.float32) for i in range(stack_ref.shape[0]))
    out_ref[:, first:] = sum(part[...].astype(jnp.float32) for part in parts)


def final(stack, parts):
    rows = stack.shape[1]
    width = stack.shape[2] + parts[0].shape[1]
    return pl.pallas_call(
        final_kernel,
        out_shape=jax.ShapeDtypeStruct((rows, width), jnp.float32),
        in_specs=[VMEM] * 5,
        out_specs=VMEM,
        compiler_params=pltpu.CompilerParams(vmem_limit_bytes=8 * MIB),
        cost_estimate=SMALL,
        name="final",
    )(stack, *parts)


def shifted(value, s):
    n = lax.axis_size("x")
    return lax.ppermute(value, "x", [(i, (i + s) % n) for i in range(n)])


def swapped(value):
    return lax.ppermute(value, "core", [(0, 1), (1, 0)])


def gather_chips(value, *others):
    own = [value] + [shifted(value, s) for s in range(1, lax.axis_size("x"))]
    return own, [swapped(after(piece, *others)) for piece in own]


def after(value, *others):
    if not others:
        return value
    return lax.optimization_barrier((value,) + others)[0]


def ring_index(place):
    return 2 * (place % 2) + place // 2


def shifted_z(value, s):
    return lax.ppermute(value, DEPTH, [(ring_index(i), ring_index((i + s) % 4)) for i in range(4)])


def shifted_y(value, s):
    return lax.ppermute(value, "y", [(i, (i + s) % 4) for i in range(4)])


def local(layer_input, w_qkv, d_out, span_order, doc_lengths):
    rows = layer_input[0]
    tokens = rows.shape[0]
    chips = lax.axis_size("x")
    seq = lax.axis_size("zhi") * lax.axis_size("y")
    at_zlo, at_zhi, at_y = lax.axis_index("zlo"), lax.axis_index("zhi"), lax.axis_index("y")
    where = jnp.stack(
        [lax.axis_index("x"), lax.axis_index("core"), at_zhi * lax.axis_size("y") + at_y, at_zhi * 2 + at_zlo, at_y]
    ).astype(jnp.int32)

    copies, *packed = first(where, rows, w_qkv, seq, chips)
    gathered = lax.all_to_all(copies, SEQ, 0, 0, tiled=True).reshape(seq * tokens, 2 * HD)
    pieces = [packed[0]] + [shifted(packed[s], s) for s in range(1, chips)]
    query = project_query(after(rows, copies), w_qkv)
    d_query, terms = attention(where, span_order, doc_lengths, query, d_out[0], gathered)
    own_q, other_q = gather_chips(d_query)
    arrived = lax.all_to_all(after(terms, other_q[0]).reshape(seq, tokens, 2 * HD), SEQ, 0, 0, tiled=True)
    x_own, x_send = halves(where, [after(piece, terms) for piece in pieces])
    columns = [x_own, swapped(x_send)]

    stacked = term_query(columns, own_q + other_q, lax.axis_size("y"))
    group_y = lax.all_to_all(stacked, "y", 0, 0, tiled=True)
    owned = jnp.sum(arrived.astype(jnp.float32), axis=0).astype(jnp.bfloat16)
    own_kv, other_kv = gather_chips(after(owned, stacked))
    parts = term_second(where, columns, own_kv + other_kv)
    d_qkv = after(jnp.concatenate([d_query, owned], axis=1), parts[0])
    d_rows = nt(d_qkv, w_qkv).astype(jnp.bfloat16)
    group_z = [parts[0]] + [after(shifted_z(parts[s], s), d_rows) for s in range(1, 4)]
    sums = middle_y(where, group_z)
    second_z = lax.all_to_all(middle_z(after(group_y, sums[1])), DEPTH, 0, 0, tiled=True)
    d_w = final(second_z, [sums[0]] + [shifted_y(sums[s], s) for s in range(1, 4)])
    return (d_rows[None], d_w)


def solution(mesh):
    fine = Mesh(mesh.devices.reshape(2, 4, 2, 2, 4), ("zlo", "x", "core", "zhi", "y"))
    dp, ctx = ("zlo", "x", "core"), ("zhi", "y")
    placed = (P(dp, ctx, None), P(), P(dp, ctx, None), P(dp, None), P(dp, None))
    return jax.shard_map(
        local,
        mesh=fine,
        in_specs=placed,
        out_specs=(P(dp, ctx, None), P(dp + ctx, None)),
        check_vma=False,
    )
```

```python
import jax
import jax.numpy as jnp
from jax import lax
from jax.experimental import pallas as pl
from jax.experimental.pallas import tpu as pltpu
from jax.sharding import Mesh, PartitionSpec as P

HD = 128
HQ = 8
SPAN = 64
LOG2E = 1.4426950408889634
SEQ = ("zhi", "y")
OWN = ("zlo", "zhi", "y")


def nt(a, b):
    return lax.dot_general(a, b, (((1,), (1,)), ((), ())), preferred_element_type=jnp.float32)


def tn(a, b):
    return lax.dot_general(a, b, (((0,), (0,)), ((), ())), preferred_element_type=jnp.float32)


def nn(a, b):
    return jnp.dot(a, b, preferred_element_type=jnp.float32)


SMEM = pl.BlockSpec(memory_space=pltpu.SMEM)
VMEM = pl.BlockSpec(memory_space=pltpu.VMEM)
MIB = 1024 * 1024
SMALL = pl.CostEstimate(flops=1, bytes_accessed=1, transcendentals=0)


def whole(value):
    return pl.BlockSpec(value.shape, lambda i: (0,) * value.ndim)


def first_kernel(where_ref, x_hbm, w_hbm, kv_hbm, *refs):
    chips = len(refs) - 7
    out_hbm = refs[:chips]
    x_ref, w_ref, piece_ref, kv_ref, in_sem, piece_sem, kv_sem = refs[chips:]
    features = x_ref.shape[1]
    width = features // (4 * chips)
    chunks = in_sem.shape[0] - 1
    depth = features // chunks
    load_x = pltpu.make_async_copy(x_hbm, x_ref, in_sem.at[chunks])
    load_x.start()
    loads = []
    for i in range(chunks):
        rows = pl.ds(i * depth, depth)
        loads.append(pltpu.make_async_copy(w_hbm.at[rows, pl.ds(HQ * HD, 2 * HD)], w_ref.at[rows, :], in_sem.at[i]))
        loads[i].start()
    load_x.wait()
    stores = []
    for s in range(chips):
        chip = lax.rem(where_ref[0] + s, chips)
        for c in range(2):
            core = where_ref[1] if c == 0 else 1 - where_ref[1]
            for z in range(2):
                at = pl.multiple_of(z * (features // 2) + chip * 2 * width + core * width, width)
                piece_ref[s, (2 * c + z) * width : (2 * c + z + 1) * width, :] = x_ref[:, pl.ds(at, width)].T
        stores.append(pltpu.make_async_copy(piece_ref.at[s], out_hbm[s], piece_sem.at[s]))
        stores[s].start()
    total = None
    for i in range(chunks):
        loads[i].wait()
        part = nn(x_ref[:, i * depth : (i + 1) * depth], w_ref[i * depth : (i + 1) * depth, :])
        total = part if total is None else total + part
    kv_ref[...] = total.astype(jnp.bfloat16)
    copies = kv_hbm.shape[0]
    for i in range(copies):
        stores.append(pltpu.make_async_copy(kv_ref, kv_hbm.at[i], kv_sem.at[i]))
        stores[-1].start()
    for store in stores:
        store.wait()


def first(where, x, w, copies, chips):
    tokens, features = x.shape
    width = 2 * HD
    anywhere = pl.BlockSpec(memory_space=pltpu.HBM)
    return pl.pallas_call(
        first_kernel,
        out_shape=(pltpu.HBM((copies, tokens, width), jnp.bfloat16),)
        + (pltpu.HBM((features // chips, tokens), x.dtype),) * chips,
        in_specs=[SMEM, anywhere, anywhere],
        out_specs=(anywhere,) * (chips + 1),
        scratch_shapes=[
            pltpu.VMEM((tokens, features), x.dtype),
            pltpu.VMEM((features, width), x.dtype),
            pltpu.VMEM((chips, features // chips, tokens), x.dtype),
            pltpu.VMEM((tokens, width), jnp.bfloat16),
            pltpu.SemaphoreType.DMA((5,)),
            pltpu.SemaphoreType.DMA((chips,)),
            pltpu.SemaphoreType.DMA((copies,)),
        ],
        compiler_params=pltpu.CompilerParams(vmem_limit_bytes=60 * MIB),
        cost_estimate=SMALL,
        name="first",
    )(where, x, w)


def query_kernel(x_ref, w_ref, out_ref):
    out_ref[...] = nn(x_ref[...], w_ref[...]).astype(jnp.bfloat16)


def project_query(x, w):
    tokens, features = x.shape
    width = 2 * HD
    return pl.pallas_call(
        query_kernel,
        grid=(HQ // 2,),
        out_shape=jax.ShapeDtypeStruct((tokens, HQ * HD), jnp.bfloat16),
        in_specs=[pl.BlockSpec((tokens, features), lambda i: (0, 0)), pl.BlockSpec((features, width), lambda i: (0, i))],
        out_specs=pl.BlockSpec((tokens, width), lambda i: (0, i)),
        compiler_params=pltpu.CompilerParams(vmem_limit_bytes=44 * MIB),
        cost_estimate=SMALL,
        name="project_query",
    )(x, w)


def half_of(piece, at):
    return pl.BlockSpec((piece.shape[0] // 2, piece.shape[1]), lambda i: (at, 0))


def forward_kernel(*refs):
    pieces, out_ref = refs[:-1], refs[-1]
    tokens = pieces[0].shape[1]
    for i, piece in enumerate(pieces):
        out_ref[:, i * tokens : (i + 1) * tokens] = piece[...]


def forward(pieces):
    rows, tokens = pieces[0].shape
    out = pltpu.HBM((rows // 2, len(pieces) * tokens), jnp.bfloat16)
    return pl.pallas_call(
        forward_kernel,
        grid=(1,),
        out_shape=out,
        in_specs=[half_of(piece, 1) for piece in pieces],
        out_specs=pl.BlockSpec(out.shape, lambda i: (0, 0)),
        compiler_params=pltpu.CompilerParams(vmem_limit_bytes=60 * MIB),
        cost_estimate=SMALL,
        name="forward",
    )(*pieces)


def attention_kernel(where_ref, order_ref, lens_ref, q_ref, do_ref, kv_ref, *refs):
    dq_ref, dkv_ref, bias_ref, dk_ref, dv_ref = refs
    scale = HD ** (-0.5)
    spans = order_ref.shape[1]
    docs = lens_ref.shape[1]
    place = where_ref[2]
    lane = lax.broadcasted_iota(jnp.int32, (1, 2 * SPAN), 1)
    pos_q = jnp.where(
        lane < SPAN,
        order_ref[0, 2 * place] * SPAN + lane,
        order_ref[0, 2 * place + 1] * SPAN + lane - SPAN,
    )
    start = jnp.zeros_like(pos_q)
    end = jnp.int32(0)
    for i in range(docs):
        end = end + lens_ref[0, i]
        start = jnp.where(pos_q >= end, end, start)
    row = lax.broadcasted_iota(jnp.int32, (SPAN, 2 * SPAN), 0)
    for s in range(spans):
        pos_k = order_ref[0, s] * SPAN + row
        allowed = (pos_k <= pos_q) & (pos_k >= start)
        bias_ref[s * SPAN : (s + 1) * SPAN, :] = jnp.where(allowed, 0.0, -jnp.inf)
    k = kv_ref[:, :HD]
    v = kv_ref[:, HD:]
    for h in range(0, HQ, 2):
        a, b, c = h * HD, (h + 1) * HD, (h + 2) * HD
        q2 = jnp.concatenate([q_ref[:, a:b], q_ref[:, b:c]], axis=0)
        d2 = jnp.concatenate([do_ref[:, a:b], do_ref[:, b:c]], axis=0)
        bias = bias_ref[...]
        s2 = nt(k, q2) + jnp.concatenate([bias, bias], axis=1)
        peak = jnp.max(s2, axis=0, keepdims=True)
        expo = jnp.exp2((s2 - peak) * (scale * LOG2E))
        inverse = 1.0 / jnp.sum(expo, axis=0, keepdims=True)
        probs = expo * inverse
        low = probs.astype(jnp.bfloat16)
        dp = nt(v, d2)
        delta = jnp.sum(low.astype(jnp.float32) * dp, axis=0, keepdims=True)
        ds = (probs * ((dp - delta) * scale)).astype(jnp.bfloat16)
        dq = tn(ds, k).astype(jnp.bfloat16)
        dq_ref[:, a:b] = dq[:HD]
        dq_ref[:, b:c] = dq[HD:]
        dv = nn(low, d2)
        dk = nn(ds, q2)
        if h > 0:
            dv += dv_ref[...]
            dk += dk_ref[...]
        if h < HQ - 2:
            dv_ref[...] = dv
            dk_ref[...] = dk
        else:
            dkv_ref[:, :HD] = dk.astype(jnp.bfloat16)
            dkv_ref[:, HD:] = dv.astype(jnp.bfloat16)


def attention(where, order, lens, query, grad, key_value):
    tokens = query.shape[0]
    total = key_value.shape[0]
    return pl.pallas_call(
        attention_kernel,
        out_shape=(
            pltpu.HBM((tokens, HQ * HD), jnp.bfloat16),
            pltpu.HBM((total, 2 * HD), jnp.bfloat16),
        ),
        grid=(1,),
        in_specs=[SMEM] * 3 + [VMEM] * 3,
        out_specs=(whole(query), whole(key_value)),
        scratch_shapes=[
            pltpu.VMEM((total, tokens), jnp.float32),
            pltpu.VMEM((total, HD), jnp.float32),
            pltpu.VMEM((total, HD), jnp.float32),
        ],
        compiler_params=pltpu.CompilerParams(vmem_limit_bytes=30 * MIB),
        cost_estimate=SMALL,
        name="attention",
    )(where, order, lens, query, grad, key_value)


def term_kernel(count, other_ref, *refs):
    parts, pieces, out_ref = refs[:count], refs[count:-1], refs[-1]
    width = out_ref.shape[1]
    at = pl.multiple_of(pl.program_id(0) * width, width)
    left = jnp.concatenate([part[...] for part in parts] + [other_ref[...]], axis=1)
    right = jnp.concatenate([g[:, pl.ds(at, width)] for g in pieces], axis=0)
    out_ref[...] = nn(left, right).astype(out_ref.dtype)


def term(parts, other, pieces, limit, name):
    half = other.shape[0]
    width = pieces[0].shape[1]
    step = 2 * HD
    return pl.pallas_call(
        lambda *refs: term_kernel(len(parts), *refs),
        grid=(width // step,),
        out_shape=pltpu.HBM((half, width), jnp.bfloat16),
        in_specs=[whole(other)] + [half_of(part, 0) for part in parts] + [VMEM] * len(pieces),
        out_specs=pl.BlockSpec((half, step), lambda j: (0, j)),
        compiler_params=pltpu.CompilerParams(vmem_limit_bytes=limit * MIB),
        cost_estimate=SMALL,
        name=name,
    )(other, *parts, *pieces)


def sum_kernel(stack_ref, out_ref):
    out_ref[...] = sum(stack_ref[i].astype(jnp.float32) for i in range(stack_ref.shape[0]))


def sum_query(stack):
    return pl.pallas_call(
        sum_kernel,
        out_shape=jax.ShapeDtypeStruct(stack.shape[1:], jnp.float32),
        in_specs=[VMEM],
        out_specs=VMEM,
        compiler_params=pltpu.CompilerParams(vmem_limit_bytes=12 * MIB),
        cost_estimate=SMALL,
        name="sum_query",
    )(stack)


def final_kernel(query_ref, stack_ref, out_ref):
    first = query_ref.shape[1]
    out_ref[:, :first] = query_ref[...]
    out_ref[:, first:] = sum(stack_ref[i].astype(jnp.float32) for i in range(stack_ref.shape[0]))


def final(query, stack):
    return pl.pallas_call(
        final_kernel,
        out_shape=jax.ShapeDtypeStruct((query.shape[0], query.shape[1] + stack.shape[2]), jnp.float32),
        in_specs=[VMEM, VMEM],
        out_specs=VMEM,
        compiler_params=pltpu.CompilerParams(vmem_limit_bytes=8 * MIB),
        cost_estimate=SMALL,
        name="final",
    )(query, stack)


def shifted(value, s):
    n = lax.axis_size("x")
    return lax.ppermute(value, "x", [(i, (i + s) % n) for i in range(n)])


def swapped(value):
    return lax.ppermute(value, "core", [(0, 1), (1, 0)])


def gather_chips(value, *others):
    own = [value] + [shifted(value, s) for s in range(1, lax.axis_size("x"))]
    return own, [swapped(after(piece, *others)) for piece in own]


def after(value, *others):
    if not others:
        return value
    return lax.optimization_barrier((value,) + others)[0]


def to_owners(value):
    owners = lax.axis_size("zlo") * lax.axis_size("zhi") * lax.axis_size("y")
    return lax.all_to_all(value.reshape(owners, value.shape[0] // owners, value.shape[1]), OWN, 0, 0, tiled=True)


def local(layer_input, w_qkv, d_out, span_order, doc_lengths):
    rows = layer_input[0]
    tokens = rows.shape[0]
    chips = lax.axis_size("x")
    seq = lax.axis_size("zhi") * lax.axis_size("y")
    place = lax.axis_index("zhi") * lax.axis_size("y") + lax.axis_index("y")
    where = jnp.stack([lax.axis_index("x"), lax.axis_index("core"), place]).astype(jnp.int32)

    copies, *packed = first(where, rows, w_qkv, seq, chips)
    gathered = lax.all_to_all(copies, SEQ, 0, 0, tiled=True).reshape(seq * tokens, 2 * HD)
    pieces = [packed[0]] + [shifted(packed[s], s) for s in range(1, chips)]
    query = project_query(after(rows, copies), w_qkv)
    d_query, terms = attention(where, span_order, doc_lengths, query, d_out[0], gathered)
    own_q, other_q = gather_chips(d_query)
    arrived = lax.all_to_all(after(terms, other_q[0]).reshape(seq, tokens, 2 * HD), SEQ, 0, 0, tiled=True)
    x_other = swapped(forward([after(piece, terms) for piece in pieces]))

    term_query = term(pieces, x_other, own_q + other_q, 60, "term_query")
    received_query = to_owners(term_query)
    owned = jnp.sum(arrived.astype(jnp.float32), axis=0).astype(jnp.bfloat16)
    own_kv, other_kv = gather_chips(after(owned, term_query))
    term_kv = term(pieces, x_other, own_kv + other_kv, 60, "term_kv")
    d_qkv = after(jnp.concatenate([d_query, owned], axis=1), term_kv)
    d_rows = nt(d_qkv, w_qkv).astype(jnp.bfloat16)
    received_kv = to_owners(after(term_kv, received_query, d_rows))
    d_w = final(sum_query(received_query), received_kv)
    return (d_rows[None], d_w)


def solution(mesh):
    fine = Mesh(mesh.devices.reshape(2, 4, 2, 2, 4), ("zlo", "x", "core", "zhi", "y"))
    dp, ctx = ("zlo", "x", "core"), ("zhi", "y")
    placed = (P(dp, ctx, None), P(), P(dp, ctx, None), P(dp, None), P(dp, None))
    return jax.shard_map(
        local,
        mesh=fine,
        in_specs=placed,
        out_specs=(P(dp, ctx, None), P(dp + ctx, None)),
        check_vma=False,
    )
```

```python
import jax
import jax.numpy as jnp
from jax import lax
from jax.experimental import pallas as pl
from jax.experimental.pallas import tpu as pltpu
from jax.sharding import Mesh, PartitionSpec as P

HD = 128
HQ = 8
SPAN = 64
LOG2E = 1.4426950408889634
SEQ = ("zhi", "y")
DEPTH = ("zlo", "zhi")


def nt(a, b):
    return lax.dot_general(a, b, (((1,), (1,)), ((), ())), preferred_element_type=jnp.float32)


def tn(a, b):
    return lax.dot_general(a, b, (((0,), (0,)), ((), ())), preferred_element_type=jnp.float32)


def nn(a, b):
    return jnp.dot(a, b, preferred_element_type=jnp.float32)


SMEM = pl.BlockSpec(memory_space=pltpu.SMEM)
VMEM = pl.BlockSpec(memory_space=pltpu.VMEM)
MIB = 1024 * 1024
SMALL = pl.CostEstimate(flops=1, bytes_accessed=1, transcendentals=0)


def whole(value):
    return pl.BlockSpec(value.shape, lambda i: (0,) * value.ndim)


def first_kernel(where_ref, x_hbm, w_hbm, kv_hbm, *refs):
    chips = len(refs) - 7
    out_hbm = refs[:chips]
    x_ref, w_ref, piece_ref, kv_ref, in_sem, piece_sem, kv_sem = refs[chips:]
    features = x_ref.shape[1]
    width = features // (4 * chips)
    chunks = in_sem.shape[0] - 1
    depth = features // chunks
    load_x = pltpu.make_async_copy(x_hbm, x_ref, in_sem.at[chunks])
    load_x.start()
    loads = []
    for i in range(chunks):
        rows = pl.ds(i * depth, depth)
        loads.append(pltpu.make_async_copy(w_hbm.at[rows, pl.ds(HQ * HD, 2 * HD)], w_ref.at[rows, :], in_sem.at[i]))
        loads[i].start()
    load_x.wait()
    stores = []
    for s in range(chips):
        chip = lax.rem(where_ref[0] + s, chips)
        for c in range(2):
            core = where_ref[1] if c == 0 else 1 - where_ref[1]
            for z in range(2):
                at = pl.multiple_of(z * (features // 2) + chip * 2 * width + core * width, width)
                piece_ref[s, (2 * c + z) * width : (2 * c + z + 1) * width, :] = x_ref[:, pl.ds(at, width)].T
        stores.append(pltpu.make_async_copy(piece_ref.at[s], out_hbm[s], piece_sem.at[s]))
        stores[s].start()
    total = None
    for i in range(chunks):
        loads[i].wait()
        part = nn(x_ref[:, i * depth : (i + 1) * depth], w_ref[i * depth : (i + 1) * depth, :])
        total = part if total is None else total + part
    kv_ref[...] = total.astype(jnp.bfloat16)
    copies = kv_hbm.shape[0]
    for i in range(copies):
        stores.append(pltpu.make_async_copy(kv_ref, kv_hbm.at[i], kv_sem.at[i]))
        stores[-1].start()
    for store in stores:
        store.wait()


def first(where, x, w, copies, chips):
    tokens, features = x.shape
    width = 2 * HD
    anywhere = pl.BlockSpec(memory_space=pltpu.HBM)
    return pl.pallas_call(
        first_kernel,
        out_shape=(pltpu.HBM((copies, tokens, width), jnp.bfloat16),)
        + (pltpu.HBM((features // chips, tokens), x.dtype),) * chips,
        in_specs=[SMEM, anywhere, anywhere],
        out_specs=(anywhere,) * (chips + 1),
        scratch_shapes=[
            pltpu.VMEM((tokens, features), x.dtype),
            pltpu.VMEM((features, width), x.dtype),
            pltpu.VMEM((chips, features // chips, tokens), x.dtype),
            pltpu.VMEM((tokens, width), jnp.bfloat16),
            pltpu.SemaphoreType.DMA((5,)),
            pltpu.SemaphoreType.DMA((chips,)),
            pltpu.SemaphoreType.DMA((copies,)),
        ],
        compiler_params=pltpu.CompilerParams(vmem_limit_bytes=60 * MIB),
        cost_estimate=SMALL,
        name="first",
    )(where, x, w)


def query_kernel(x_ref, w_ref, out_ref):
    out_ref[...] = nn(x_ref[...], w_ref[...]).astype(jnp.bfloat16)


def project_query(x, w):
    tokens, features = x.shape
    width = 2 * HD
    return pl.pallas_call(
        query_kernel,
        grid=(HQ // 2,),
        out_shape=jax.ShapeDtypeStruct((tokens, HQ * HD), jnp.bfloat16),
        in_specs=[pl.BlockSpec((tokens, features), lambda i: (0, 0)), pl.BlockSpec((features, width), lambda i: (0, i))],
        out_specs=pl.BlockSpec((tokens, width), lambda i: (0, i)),
        compiler_params=pltpu.CompilerParams(vmem_limit_bytes=44 * MIB),
        cost_estimate=SMALL,
        name="project_query",
    )(x, w)


def half_of(piece, at):
    return pl.BlockSpec((piece.shape[0] // 2, piece.shape[1]), lambda i: (at, 0))


def forward_kernel(*refs):
    pieces, out_ref = refs[:-1], refs[-1]
    tokens = pieces[0].shape[1]
    for i, piece in enumerate(pieces):
        out_ref[:, i * tokens : (i + 1) * tokens] = piece[...]


def forward(pieces):
    rows, tokens = pieces[0].shape
    out = pltpu.HBM((rows // 2, len(pieces) * tokens), jnp.bfloat16)
    return pl.pallas_call(
        forward_kernel,
        grid=(1,),
        out_shape=out,
        in_specs=[half_of(piece, 1) for piece in pieces],
        out_specs=pl.BlockSpec(out.shape, lambda i: (0, 0)),
        compiler_params=pltpu.CompilerParams(vmem_limit_bytes=60 * MIB),
        cost_estimate=SMALL,
        name="forward",
    )(*pieces)


def attention_kernel(where_ref, order_ref, lens_ref, q_ref, do_ref, kv_ref, *refs):
    dq_ref, dkv_ref, bias_ref, dk_ref, dv_ref = refs
    scale = HD ** (-0.5)
    spans = order_ref.shape[1]
    docs = lens_ref.shape[1]
    place = where_ref[2]
    lane = lax.broadcasted_iota(jnp.int32, (1, 2 * SPAN), 1)
    pos_q = jnp.where(
        lane < SPAN,
        order_ref[0, 2 * place] * SPAN + lane,
        order_ref[0, 2 * place + 1] * SPAN + lane - SPAN,
    )
    start = jnp.zeros_like(pos_q)
    end = jnp.int32(0)
    for i in range(docs):
        end = end + lens_ref[0, i]
        start = jnp.where(pos_q >= end, end, start)
    row = lax.broadcasted_iota(jnp.int32, (SPAN, 2 * SPAN), 0)
    for s in range(spans):
        pos_k = order_ref[0, s] * SPAN + row
        allowed = (pos_k <= pos_q) & (pos_k >= start)
        bias_ref[s * SPAN : (s + 1) * SPAN, :] = jnp.where(allowed, 0.0, -jnp.inf)
    k = kv_ref[:, :HD]
    v = kv_ref[:, HD:]
    for h in range(0, HQ, 2):
        a, b, c = h * HD, (h + 1) * HD, (h + 2) * HD
        q2 = jnp.concatenate([q_ref[:, a:b], q_ref[:, b:c]], axis=0)
        d2 = jnp.concatenate([do_ref[:, a:b], do_ref[:, b:c]], axis=0)
        bias = bias_ref[...]
        s2 = nt(k, q2) + jnp.concatenate([bias, bias], axis=1)
        peak = jnp.max(s2, axis=0, keepdims=True)
        expo = jnp.exp2((s2 - peak) * (scale * LOG2E))
        inverse = 1.0 / jnp.sum(expo, axis=0, keepdims=True)
        probs = expo * inverse
        low = probs.astype(jnp.bfloat16)
        dp = nt(v, d2)
        delta = jnp.sum(low.astype(jnp.float32) * dp, axis=0, keepdims=True)
        ds = (probs * ((dp - delta) * scale)).astype(jnp.bfloat16)
        dq = tn(ds, k).astype(jnp.bfloat16)
        dq_ref[:, a:b] = dq[:HD]
        dq_ref[:, b:c] = dq[HD:]
        dv = nn(low, d2)
        dk = nn(ds, q2)
        if h > 0:
            dv += dv_ref[...]
            dk += dk_ref[...]
        if h < HQ - 2:
            dv_ref[...] = dv
            dk_ref[...] = dk
        else:
            dkv_ref[:, :HD] = dk.astype(jnp.bfloat16)
            dkv_ref[:, HD:] = dv.astype(jnp.bfloat16)


def attention(where, order, lens, query, grad, key_value):
    tokens = query.shape[0]
    total = key_value.shape[0]
    return pl.pallas_call(
        attention_kernel,
        out_shape=(
            pltpu.HBM((tokens, HQ * HD), jnp.bfloat16),
            pltpu.HBM((total, 2 * HD), jnp.bfloat16),
        ),
        grid=(1,),
        in_specs=[SMEM] * 3 + [VMEM] * 3,
        out_specs=(whole(query), whole(key_value)),
        scratch_shapes=[
            pltpu.VMEM((total, tokens), jnp.float32),
            pltpu.VMEM((total, HD), jnp.float32),
            pltpu.VMEM((total, HD), jnp.float32),
        ],
        compiler_params=pltpu.CompilerParams(vmem_limit_bytes=30 * MIB),
        cost_estimate=SMALL,
        name="attention",
    )(where, order, lens, query, grad, key_value)


def product(parts, other_ref, pieces, at, width):
    left = jnp.concatenate([part[...] for part in parts] + [other_ref[...]], axis=1)
    right = jnp.concatenate([g[:, pl.ds(at, width)] for g in pieces], axis=0)
    return nn(left, right).astype(jnp.bfloat16)


def term_query_kernel(count, other_ref, *refs):
    parts, pieces, out_ref = refs[:count], refs[count:-1], refs[-1]
    blocks, _, width = out_ref.shape
    at = pl.multiple_of(pl.program_id(0) * width, width)
    part = product(parts, other_ref, pieces, at, width)
    rows = part.shape[0] // (blocks * blocks)
    for i in range(blocks):
        for y in range(blocks):
            here = (i * blocks + y) * rows
            out_ref[y, i * rows : (i + 1) * rows, :] = part[here : here + rows]


def term_query(parts, other, pieces, blocks):
    half = other.shape[0]
    width = pieces[0].shape[1]
    step = 2 * HD
    return pl.pallas_call(
        lambda *refs: term_query_kernel(len(parts), *refs),
        grid=(width // step,),
        out_shape=pltpu.HBM((blocks, half // blocks, width), jnp.bfloat16),
        in_specs=[whole(other)] + [half_of(part, 0) for part in parts] + [VMEM] * len(pieces),
        out_specs=pl.BlockSpec((blocks, half // blocks, step), lambda j: (0, 0, j)),
        compiler_params=pltpu.CompilerParams(vmem_limit_bytes=60 * MIB),
        cost_estimate=SMALL,
        name="term_query",
    )(other, *parts, *pieces)


def term_kv_kernel(count, where_ref, other_ref, *refs):
    parts, pieces, outs, full_ref = refs[:count], refs[count:-5], refs[-5:-1], refs[-1]
    full_ref[...] = product(parts, other_ref, pieces, 0, full_ref.shape[1])
    blocks = len(outs)
    rows = full_ref.shape[0] // (blocks * blocks)
    for s in range(blocks):
        y = lax.rem(where_ref[3] + s, blocks)
        for i in range(blocks):
            at = pl.multiple_of((i * blocks + y) * rows, rows)
            outs[s][i * rows : (i + 1) * rows, :] = full_ref[pl.ds(at, rows), :]


def term_kv(where, parts, other, pieces, blocks):
    half = other.shape[0]
    width = pieces[0].shape[1]
    out = pltpu.HBM((half // blocks, width), jnp.bfloat16)
    return pl.pallas_call(
        lambda *refs: term_kv_kernel(len(parts), *refs),
        grid=(1,),
        out_shape=(out,) * blocks,
        in_specs=[SMEM, whole(other)] + [half_of(part, 0) for part in parts] + [VMEM] * len(pieces),
        out_specs=(pl.BlockSpec(out.shape, lambda j: (0, 0)),) * blocks,
        scratch_shapes=[pltpu.VMEM((half, width), jnp.bfloat16)],
        compiler_params=pltpu.CompilerParams(vmem_limit_bytes=60 * MIB),
        cost_estimate=SMALL,
        name="term_kv",
    )(where, other, *parts, *pieces)


def middle_kernel(stack_ref, *refs):
    parts, out_ref = refs[:-1], refs[-1]
    first = stack_ref.shape[2]
    blocks, rows, _ = out_ref.shape
    for i in range(blocks):
        here = slice(i * rows, (i + 1) * rows)
        query = sum(stack_ref[j, here, :].astype(jnp.float32) for j in range(stack_ref.shape[0]))
        out_ref[i, :, :first] = query.astype(out_ref.dtype)
        out_ref[i, :, first:] = sum(part[here, :].astype(jnp.float32) for part in parts).astype(out_ref.dtype)


def middle(stack, parts):
    blocks, rows, width = stack.shape
    out = pltpu.HBM((blocks, rows // blocks, width + parts[0].shape[1]), jnp.bfloat16)
    return pl.pallas_call(
        middle_kernel,
        grid=(1,),
        out_shape=out,
        in_specs=[VMEM] * (1 + len(parts)),
        out_specs=pl.BlockSpec(out.shape, lambda i: (0, 0, 0)),
        compiler_params=pltpu.CompilerParams(vmem_limit_bytes=14 * MIB),
        cost_estimate=SMALL,
        name="middle",
    )(stack, *parts)


def final_kernel(stack_ref, out_ref):
    out_ref[...] = sum(stack_ref[i].astype(jnp.float32) for i in range(stack_ref.shape[0]))


def final(stack):
    return pl.pallas_call(
        final_kernel,
        out_shape=jax.ShapeDtypeStruct(stack.shape[1:], jnp.float32),
        in_specs=[VMEM],
        out_specs=VMEM,
        compiler_params=pltpu.CompilerParams(vmem_limit_bytes=8 * MIB),
        cost_estimate=SMALL,
        name="final",
    )(stack)


def input_query_kernel(g_ref, w_ref, out_ref):
    out_ref[...] = nt(g_ref[...], w_ref[...]).astype(out_ref.dtype)


def input_last_kernel(g_ref, w_ref, part_ref, out_ref):
    out_ref[...] = (part_ref[...].astype(jnp.float32) + nt(g_ref[...], w_ref[...])).astype(out_ref.dtype)


def input_grad(grad, w, at, partial=()):
    tokens, width = grad.shape
    features = w.shape[0]
    step = 2048
    out = pltpu.HBM((tokens, features), jnp.bfloat16)
    block = pl.BlockSpec((tokens, step), lambda i: (0, i))
    return pl.pallas_call(
        input_last_kernel if partial else input_query_kernel,
        grid=(features // step,),
        out_shape=out,
        in_specs=[pl.BlockSpec((tokens, width), lambda i: (0, 0)), pl.BlockSpec((step, width), lambda i: (i, at))] + [block] * len(partial),
        out_specs=block,
        compiler_params=pltpu.CompilerParams(vmem_limit_bytes=60 * MIB),
        cost_estimate=SMALL,
        name="d_x_last" if partial else "d_x_query",
    )(grad, w, *partial)


def shifted(value, s):
    n = lax.axis_size("x")
    return lax.ppermute(value, "x", [(i, (i + s) % n) for i in range(n)])


def swapped(value):
    return lax.ppermute(value, "core", [(0, 1), (1, 0)])


def gather_chips(value, *others):
    own = [value] + [shifted(value, s) for s in range(1, lax.axis_size("x"))]
    return own, [swapped(after(piece, *others)) for piece in own]


def after(value, *others):
    if not others:
        return value
    return lax.optimization_barrier((value,) + others)[0]


def shifted_y(value, s):
    return lax.ppermute(value, "y", [(i, (i + s) % 4) for i in range(4)])


def local(layer_input, w_qkv, d_out, span_order, doc_lengths):
    rows = layer_input[0]
    tokens = rows.shape[0]
    chips = lax.axis_size("x")
    seq = lax.axis_size("zhi") * lax.axis_size("y")
    place = lax.axis_index("zhi") * lax.axis_size("y") + lax.axis_index("y")
    where = jnp.stack([lax.axis_index("x"), lax.axis_index("core"), place, lax.axis_index("y")]).astype(jnp.int32)

    copies, *packed = first(where, rows, w_qkv, seq, chips)
    gathered = lax.all_to_all(copies, SEQ, 0, 0, tiled=True).reshape(seq * tokens, 2 * HD)
    pieces = [packed[0]] + [shifted(packed[s], s) for s in range(1, chips)]
    query = project_query(after(rows, copies), w_qkv)
    d_query, terms = attention(where, span_order, doc_lengths, query, d_out[0], gathered)
    own_q = [d_query] + [shifted(d_query, s) for s in range(1, chips)]
    other_q = [swapped(d_query)]
    arrived = lax.all_to_all(after(terms, other_q[0]).reshape(seq, tokens, 2 * HD), SEQ, 0, 0, tiled=True)
    x_other = swapped(forward([after(piece, terms) for piece in pieces]))
    d_x_query = input_grad(after(d_query, terms,other_q[0]), w_qkv, 0)

    other_q += [swapped(after(piece, d_x_query)) for piece in own_q[1:]]
    places = lax.axis_size("y")
    stacked = term_query(pieces, x_other, own_q + other_q, places)
    group_query = lax.all_to_all(stacked, "y", 0, 0, tiled=True)
    owned = jnp.sum(arrived.astype(jnp.float32), axis=0).astype(jnp.bfloat16)
    own_kv, other_kv = gather_chips(after(owned, stacked))
    parts = term_kv(where, pieces, x_other, own_kv + other_kv, places)
    d_rows = input_grad(after(owned, parts[0]), w_qkv, HQ // 2, (d_x_query,))
    group_kv = [parts[0]] + [after(shifted_y(parts[s], s), d_rows) for s in range(1, places)]
    d_w = final(lax.all_to_all(middle(group_query, group_kv), DEPTH, 0, 0, tiled=True))
    return (d_rows[None], d_w)


def solution(mesh):
    fine = Mesh(mesh.devices.reshape(2, 4, 2, 2, 4), ("zlo", "x", "core", "zhi", "y"))
    dp, ctx = ("zlo", "x", "core"), ("zhi", "y")
    placed = (P(dp, ctx, None), P(), P(dp, ctx, None), P(dp, None), P(dp, None))
    return jax.shard_map(
        local,
        mesh=fine,
        in_specs=placed,
        out_specs=(P(dp, ctx, None), P(dp + ctx, None)),
        check_vma=False,
    )
```

```python
import jax
import jax.numpy as jnp
from jax import lax
from jax.experimental import pallas as pl
from jax.experimental.pallas import tpu as pltpu
from jax.sharding import Mesh, PartitionSpec as P

HD = 128
HQ = 8
SPAN = 64
LOG2E = 1.4426950408889634
FIRST = 768
SEQ = ("zhi", "y")
DEPTH = ("zlo", "zhi")


def nt(a, b):
    return lax.dot_general(a, b, (((1,), (1,)), ((), ())), preferred_element_type=jnp.float32)


def tn(a, b):
    return lax.dot_general(a, b, (((0,), (0,)), ((), ())), preferred_element_type=jnp.float32)


def nn(a, b):
    return jnp.dot(a, b, preferred_element_type=jnp.float32)


SMEM = pl.BlockSpec(memory_space=pltpu.SMEM)
VMEM = pl.BlockSpec(memory_space=pltpu.VMEM)
MIB = 1024 * 1024
SMALL = pl.CostEstimate(flops=1, bytes_accessed=1, transcendentals=0)


def whole(value):
    return pl.BlockSpec(value.shape, lambda i: (0,) * value.ndim)


def first_kernel(where_ref, x_hbm, w_hbm, kv_hbm, *refs):
    chips = len(refs) - 7
    out_hbm = refs[:chips]
    x_ref, w_ref, piece_ref, kv_ref, in_sem, piece_sem, kv_sem = refs[chips:]
    features = x_ref.shape[1]
    width = features // (4 * chips)
    chunks = in_sem.shape[0] - 1
    depth = features // chunks
    load_x = pltpu.make_async_copy(x_hbm, x_ref, in_sem.at[chunks])
    load_x.start()
    loads = []
    for i in range(chunks):
        rows = pl.ds(i * depth, depth)
        loads.append(pltpu.make_async_copy(w_hbm.at[rows, pl.ds(HQ * HD, 2 * HD)], w_ref.at[rows, :], in_sem.at[i]))
        loads[i].start()
    load_x.wait()
    stores = []
    for s in range(chips):
        chip = lax.rem(where_ref[0] + s, chips)
        for c in range(2):
            for z in range(2):
                at = pl.multiple_of(z * (features // 2) + chip * 2 * width + c * width, width)
                piece_ref[s, (2 * c + z) * width : (2 * c + z + 1) * width, :] = x_ref[:, pl.ds(at, width)].T
        stores.append(pltpu.make_async_copy(piece_ref.at[s], out_hbm[s], piece_sem.at[s]))
        stores[s].start()
    total = None
    for i in range(chunks):
        loads[i].wait()
        part = nn(x_ref[:, i * depth : (i + 1) * depth], w_ref[i * depth : (i + 1) * depth, :])
        total = part if total is None else total + part
    kv_ref[...] = total.astype(jnp.bfloat16)
    copies = kv_hbm.shape[0]
    for i in range(copies):
        stores.append(pltpu.make_async_copy(kv_ref, kv_hbm.at[i], kv_sem.at[i]))
        stores[-1].start()
    for store in stores:
        store.wait()


def first(where, x, w, copies, chips):
    tokens, features = x.shape
    width = 2 * HD
    anywhere = pl.BlockSpec(memory_space=pltpu.HBM)
    return pl.pallas_call(
        first_kernel,
        out_shape=(pltpu.HBM((copies, tokens, width), jnp.bfloat16),)
        + (pltpu.HBM((features // chips, tokens), x.dtype),) * chips,
        in_specs=[SMEM, anywhere, anywhere],
        out_specs=(anywhere,) * (chips + 1),
        scratch_shapes=[
            pltpu.VMEM((tokens, features), x.dtype),
            pltpu.VMEM((features, width), x.dtype),
            pltpu.VMEM((chips, features // chips, tokens), x.dtype),
            pltpu.VMEM((tokens, width), jnp.bfloat16),
            pltpu.SemaphoreType.DMA((5,)),
            pltpu.SemaphoreType.DMA((chips,)),
            pltpu.SemaphoreType.DMA((copies,)),
        ],
        compiler_params=pltpu.CompilerParams(vmem_limit_bytes=60 * MIB),
        cost_estimate=SMALL,
        name="first",
    )(where, x, w)


def query_kernel(x_ref, w_ref, out_ref):
    out_ref[...] = nn(x_ref[...], w_ref[...]).astype(jnp.bfloat16)


def project_query(x, w):
    tokens, features = x.shape
    width = 2 * HD
    return pl.pallas_call(
        query_kernel,
        grid=(HQ // 2,),
        out_shape=jax.ShapeDtypeStruct((tokens, HQ * HD), jnp.bfloat16),
        in_specs=[pl.BlockSpec((tokens, features), lambda i: (0, 0)), pl.BlockSpec((features, width), lambda i: (0, i))],
        out_specs=pl.BlockSpec((tokens, width), lambda i: (0, i)),
        compiler_params=pltpu.CompilerParams(vmem_limit_bytes=44 * MIB),
        cost_estimate=SMALL,
        name="project_query",
    )(x, w)


def halves_kernel(where_ref, *refs):
    pieces, own_ref, send_ref = refs[:-2], refs[-2], refs[-1]
    half, tokens = own_ref.shape[0], pieces[0].shape[1]
    own = pl.multiple_of(where_ref[1] * half, half)
    send = pl.multiple_of((1 - where_ref[1]) * half, half)
    for i, piece in enumerate(pieces):
        own_ref[:, i * tokens : (i + 1) * tokens] = piece[pl.ds(own, half), :]
        send_ref[:, i * tokens : (i + 1) * tokens] = piece[pl.ds(send, half), :]


def halves(where, pieces):
    rows, tokens = pieces[0].shape
    n = len(pieces)
    shape = (rows // 2, n * tokens)
    return pl.pallas_call(
        halves_kernel,
        grid=(1,),
        out_shape=(pltpu.HBM(shape, jnp.bfloat16),) * 2,
        in_specs=[SMEM] + [VMEM] * n,
        out_specs=(pl.BlockSpec(shape, lambda i: (0, 0)),) * 2,
        compiler_params=pltpu.CompilerParams(vmem_limit_bytes=60 * MIB),
        cost_estimate=SMALL,
        name="halves",
    )(where, *pieces)


def attention_kernel(where_ref, order_ref, lens_ref, q_ref, do_ref, kv_ref, *refs):
    dq_ref, dkv_ref, bias_ref, dk_ref, dv_ref = refs
    scale = HD ** (-0.5)
    spans = order_ref.shape[1]
    docs = lens_ref.shape[1]
    place = where_ref[2]
    lane = lax.broadcasted_iota(jnp.int32, (1, 2 * SPAN), 1)
    pos_q = jnp.where(
        lane < SPAN,
        order_ref[0, 2 * place] * SPAN + lane,
        order_ref[0, 2 * place + 1] * SPAN + lane - SPAN,
    )
    start = jnp.zeros_like(pos_q)
    end = jnp.int32(0)
    for i in range(docs):
        end = end + lens_ref[0, i]
        start = jnp.where(pos_q >= end, end, start)
    row = lax.broadcasted_iota(jnp.int32, (SPAN, 2 * SPAN), 0)
    for s in range(spans):
        pos_k = order_ref[0, s] * SPAN + row
        allowed = (pos_k <= pos_q) & (pos_k >= start)
        bias_ref[s * SPAN : (s + 1) * SPAN, :] = jnp.where(allowed, 0.0, -jnp.inf)
    k = kv_ref[:, :HD]
    v = kv_ref[:, HD:]
    for h in range(0, HQ, 2):
        a, b, c = h * HD, (h + 1) * HD, (h + 2) * HD
        q2 = jnp.concatenate([q_ref[:, a:b], q_ref[:, b:c]], axis=0)
        d2 = jnp.concatenate([do_ref[:, a:b], do_ref[:, b:c]], axis=0)
        bias = bias_ref[...]
        s2 = nt(k, q2) + jnp.concatenate([bias, bias], axis=1)
        peak = jnp.max(s2, axis=0, keepdims=True)
        expo = jnp.exp2((s2 - peak) * (scale * LOG2E))
        inverse = 1.0 / jnp.sum(expo, axis=0, keepdims=True)
        probs = expo * inverse
        low = probs.astype(jnp.bfloat16)
        dp = nt(v, d2)
        delta = jnp.sum(low.astype(jnp.float32) * dp, axis=0, keepdims=True)
        ds = (probs * ((dp - delta) * scale)).astype(jnp.bfloat16)
        dq = tn(ds, k).astype(jnp.bfloat16)
        dq_ref[:, a:b] = dq[:HD]
        dq_ref[:, b:c] = dq[HD:]
        dv = nn(low, d2)
        dk = nn(ds, q2)
        if h > 0:
            dv += dv_ref[...]
            dk += dk_ref[...]
        if h < HQ - 2:
            dv_ref[...] = dv
            dk_ref[...] = dk
        else:
            dkv_ref[:, :HD] = dk.astype(jnp.bfloat16)
            dkv_ref[:, HD:] = dv.astype(jnp.bfloat16)


def attention(where, order, lens, query, grad, key_value):
    tokens = query.shape[0]
    total = key_value.shape[0]
    return pl.pallas_call(
        attention_kernel,
        out_shape=(
            pltpu.HBM((tokens, HQ * HD), jnp.bfloat16),
            pltpu.HBM((total, 2 * HD), jnp.bfloat16),
        ),
        grid=(1,),
        in_specs=[SMEM] * 3 + [VMEM] * 3,
        out_specs=(whole(query), whole(key_value)),
        scratch_shapes=[
            pltpu.VMEM((total, tokens), jnp.float32),
            pltpu.VMEM((total, HD), jnp.float32),
            pltpu.VMEM((total, HD), jnp.float32),
        ],
        compiler_params=pltpu.CompilerParams(vmem_limit_bytes=30 * MIB),
        cost_estimate=SMALL,
        name="attention",
    )(where, order, lens, query, grad, key_value)


def term_query_kernel(*refs):
    parts, pieces, out_ref, done_ref = refs[:2], refs[2:-2], refs[-2], refs[-1]
    step = pl.program_id(0)
    width = out_ref.shape[2]
    at = pl.multiple_of(step * width, width)
    left = jnp.concatenate([part[...] for part in parts], axis=1)
    right = jnp.concatenate([g[:, pl.ds(at, width)] for g in pieces], axis=0)
    part = nn(left, right).astype(out_ref.dtype)
    blocks = out_ref.shape[0]
    rows = left.shape[0] // (blocks * blocks)

    @pl.when(step < FIRST // (2 * HD))
    def _():
        for i in range(blocks):
            for y in range(blocks):
                here = (i * blocks + y) * rows
                out_ref[y, i * rows : (i + 1) * rows, :] = part[here : here + rows]

    @pl.when(step >= FIRST // (2 * HD))
    def _():
        done_ref[...] = part


def term_query(parts, pieces, blocks):
    half = parts[0].shape[0]
    width = pieces[0].shape[1]
    step = 2 * HD
    first = FIRST // step
    return pl.pallas_call(
        term_query_kernel,
        grid=(width // step,),
        out_shape=(
            pltpu.HBM((blocks, half // blocks, FIRST), jnp.bfloat16),
            pltpu.HBM((half, width - FIRST), jnp.bfloat16),
        ),
        in_specs=[VMEM] * (len(parts) + len(pieces)),
        out_specs=(
            pl.BlockSpec((blocks, half // blocks, step), lambda j: (0, 0, jnp.minimum(j, first - 1))),
            pl.BlockSpec((half, step), lambda j: (0, jnp.maximum(j - first, 0))),
        ),
        compiler_params=pltpu.CompilerParams(vmem_limit_bytes=20 * MIB),
        cost_estimate=SMALL,
        name="term_query",
    )(*parts, *pieces)


def ring_block(where_ref, s):
    place = lax.rem(where_ref[3] + s, 4)
    return 2 * lax.rem(place, 2) + place // 2


def term_second_kernel(where_ref, *refs):
    parts, done_ref, pieces, outs = refs[:2], refs[2], refs[3:-4], refs[-4:]
    rows = outs[0].shape[0]
    done = done_ref.shape[1]
    right = jnp.concatenate([g[...] for g in pieces], axis=0)
    for s in range(4):
        at = pl.multiple_of(ring_block(where_ref, s) * rows, rows)
        left = jnp.concatenate([part[pl.ds(at, rows), :] for part in parts], axis=1)
        outs[s][:, :done] = done_ref[pl.ds(at, rows), :]
        outs[s][:, done:] = nn(left, right).astype(outs[s].dtype)


def term_second(where, parts, done, pieces):
    half = parts[0].shape[0]
    width = pieces[0].shape[1]
    out = pltpu.HBM((half // 4, done.shape[1] + width), jnp.bfloat16)
    return pl.pallas_call(
        term_second_kernel,
        grid=(1,),
        out_shape=(out,) * 4,
        in_specs=[SMEM] + [VMEM] * (1 + len(parts) + len(pieces)),
        out_specs=(pl.BlockSpec(out.shape, lambda i: (0, 0)),) * 4,
        compiler_params=pltpu.CompilerParams(vmem_limit_bytes=60 * MIB),
        cost_estimate=SMALL,
        name="term_second",
    )(where, *parts, done, *pieces)


def middle_z_kernel(stack_ref, out_ref):
    rows = out_ref.shape[1]
    for i in range(out_ref.shape[0]):
        parts = [stack_ref[j, i * rows : (i + 1) * rows, :].astype(jnp.float32) for j in range(stack_ref.shape[0])]
        out_ref[i] = sum(parts).astype(out_ref.dtype)


def middle_z(stack):
    blocks, rows, width = stack.shape
    out = pltpu.HBM((blocks, rows // blocks, width), jnp.bfloat16)
    return pl.pallas_call(
        middle_z_kernel,
        grid=(1,),
        out_shape=out,
        in_specs=[VMEM],
        out_specs=pl.BlockSpec(out.shape, lambda i: (0, 0, 0)),
        compiler_params=pltpu.CompilerParams(vmem_limit_bytes=14 * MIB),
        cost_estimate=SMALL,
        name="middle_z",
    )(stack)


def middle_y_kernel(where_ref, *refs):
    parts, outs = refs[:-4], refs[-4:]
    rows = outs[0].shape[0]
    for s in range(4):
        at = pl.multiple_of(lax.rem(where_ref[4] + s, 4) * rows, rows)
        total = sum(part[pl.ds(at, rows), :].astype(jnp.float32) for part in parts)
        outs[s][...] = total.astype(outs[s].dtype)


def middle_y(where, parts):
    rows, width = parts[0].shape
    return pl.pallas_call(
        middle_y_kernel,
        grid=(1,),
        out_shape=(jax.ShapeDtypeStruct((rows // 4, width), jnp.float32),) + (pltpu.HBM((rows // 4, width), jnp.bfloat16),) * 3,
        in_specs=[SMEM] + [VMEM] * len(parts),
        out_specs=(VMEM,) + (pl.BlockSpec((rows // 4, width), lambda i: (0, 0)),) * 3,
        compiler_params=pltpu.CompilerParams(vmem_limit_bytes=14 * MIB),
        cost_estimate=SMALL,
        name="middle_y",
    )(where, *parts)


def final_kernel(stack_ref, *refs):
    parts, out_ref = refs[:-1], refs[-1]
    out_ref[:, :FIRST] = sum(stack_ref[i].astype(jnp.float32) for i in range(stack_ref.shape[0]))
    out_ref[:, FIRST:] = sum(part[...].astype(jnp.float32) for part in parts)


def final(stack, parts):
    rows = stack.shape[1]
    width = FIRST + parts[0].shape[1]
    return pl.pallas_call(
        final_kernel,
        out_shape=jax.ShapeDtypeStruct((rows, width), jnp.float32),
        in_specs=[VMEM] * 5,
        out_specs=VMEM,
        compiler_params=pltpu.CompilerParams(vmem_limit_bytes=8 * MIB),
        cost_estimate=SMALL,
        name="final",
    )(stack, *parts)


def input_first_kernel(g_ref, w_ref, out_ref):
    out_ref[...] = nt(g_ref[...], w_ref[...]).astype(out_ref.dtype)


def input_last_kernel(g_ref, kv_ref, w_ref, w_kv_ref, part_ref, out_ref):
    total = nt(g_ref[...], w_ref[...]) + nt(kv_ref[...], w_kv_ref[...])
    out_ref[...] = (total + part_ref[...].astype(jnp.float32)).astype(out_ref.dtype)


def input_grad(query, w, key_value=None, partial=None):
    tokens, width = query.shape
    features = w.shape[0]
    half = width // 2
    step = 2048
    out = pl.BlockSpec((tokens, step), lambda i: (0, i))
    if partial is None:
        kernel, values = input_first_kernel, (query, w)
        specs = [pl.BlockSpec((tokens, half), lambda i: (0, 0)), pl.BlockSpec((step, half), lambda i: (i, 0))]
    else:
        kernel, values = input_last_kernel, (query, key_value, w, w, partial)
        specs = [
            pl.BlockSpec((tokens, half), lambda i: (0, 1)),
            pl.BlockSpec(key_value.shape, lambda i: (0, 0)),
            pl.BlockSpec((step, half), lambda i: (i, 1)),
            pl.BlockSpec((step, 2 * HD), lambda i: (i, HQ // 2)),
            out,
        ]
    return pl.pallas_call(
        kernel,
        grid=(features // step,),
        out_shape=pltpu.HBM((tokens, features), jnp.bfloat16),
        in_specs=specs,
        out_specs=out,
        compiler_params=pltpu.CompilerParams(vmem_limit_bytes=60 * MIB),
        cost_estimate=SMALL,
        name="d_x_first" if partial is None else "d_x_last",
    )(*values)


def shifted(value, s):
    n = lax.axis_size("x")
    return lax.ppermute(value, "x", [(i, (i + s) % n) for i in range(n)])


def swapped(value):
    return lax.ppermute(value, "core", [(0, 1), (1, 0)])


def gather_chips(value, *others):
    own = [value] + [shifted(value, s) for s in range(1, lax.axis_size("x"))]
    return own, [swapped(after(piece, *others)) for piece in own]


def after(value, *others):
    if not others:
        return value
    return lax.optimization_barrier((value,) + others)[0]


def ring_index(place):
    return 2 * (place % 2) + place // 2


def shifted_z(value, s):
    return lax.ppermute(value, DEPTH, [(ring_index(i), ring_index((i + s) % 4)) for i in range(4)])


def shifted_y(value, s):
    return lax.ppermute(value, "y", [(i, (i + s) % 4) for i in range(4)])


def local(layer_input, w_qkv, d_out, span_order, doc_lengths):
    rows = layer_input[0]
    tokens = rows.shape[0]
    chips = lax.axis_size("x")
    seq = lax.axis_size("zhi") * lax.axis_size("y")
    at_zlo, at_zhi, at_y = lax.axis_index("zlo"), lax.axis_index("zhi"), lax.axis_index("y")
    where = jnp.stack(
        [lax.axis_index("x"), lax.axis_index("core"), at_zhi * lax.axis_size("y") + at_y, at_zhi * 2 + at_zlo, at_y]
    ).astype(jnp.int32)

    copies, *packed = first(where, rows, w_qkv, seq, chips)
    gathered = lax.all_to_all(copies, SEQ, 0, 0, tiled=True).reshape(seq * tokens, 2 * HD)
    pieces = [packed[0]] + [shifted(packed[s], s) for s in range(1, chips)]
    query = project_query(after(rows, copies), w_qkv)
    d_query, terms = attention(where, span_order, doc_lengths, query, d_out[0], gathered)
    own_q = [d_query] + [shifted(d_query, s) for s in range(1, chips)]
    other_q = [swapped(d_query)]
    d_x_first = input_grad(after(d_query, terms, other_q[0]), w_qkv)
    other_q += [swapped(after(piece, d_x_first)) for piece in own_q[1:]]
    arrived = lax.all_to_all(after(terms, other_q[0]).reshape(seq, tokens, 2 * HD), SEQ, 0, 0, tiled=True)
    x_own, x_send = halves(where, [after(piece, terms) for piece in pieces])
    columns = [x_own, swapped(x_send)]

    stacked, done = term_query(columns, own_q + other_q, lax.axis_size("y"))
    group_y = lax.all_to_all(stacked, "y", 0, 0, tiled=True)
    owned = jnp.sum(arrived.astype(jnp.float32), axis=0).astype(jnp.bfloat16)
    own_kv, other_kv = gather_chips(after(owned, done))
    parts = term_second(where, columns, done, own_kv + other_kv)
    second_z = lax.all_to_all(middle_z(group_y), DEPTH, 0, 0, tiled=True)
    d_rows = input_grad(d_query, w_qkv, after(owned, group_y), d_x_first)
    group_z = [parts[0]] + [after(shifted_z(parts[s], s), d_rows) for s in range(1, 4)]
    sums = middle_y(where, group_z)
    d_w = final(second_z, [sums[0]] + [shifted_y(sums[s], s) for s in range(1, 4)])
    return (d_rows[None], d_w)


def solution(mesh):
    fine = Mesh(mesh.devices.reshape(2, 4, 2, 2, 4), ("zlo", "x", "core", "zhi", "y"))
    dp, ctx = ("zlo", "x", "core"), ("zhi", "y")
    placed = (P(dp, ctx, None), P(), P(dp, ctx, None), P(dp, None), P(dp, None))
    return jax.shard_map(
        local,
        mesh=fine,
        in_specs=placed,
        out_specs=(P(dp, ctx, None), P(dp + ctx, None)),
        check_vma=False,
    )
```

```python
import jax
import jax.numpy as jnp
from jax import lax
from jax.experimental import pallas as pl
from jax.experimental.pallas import tpu as pltpu
from jax.sharding import Mesh, PartitionSpec as P

HD = 128
HQ = 8
SPAN = 64
LOG2E = 1.4426950408889634
SEQ = ("zhi", "y")
DEPTH = ("zlo", "zhi")


def nt(a, b):
    return lax.dot_general(a, b, (((1,), (1,)), ((), ())), preferred_element_type=jnp.float32)


def tn(a, b):
    return lax.dot_general(a, b, (((0,), (0,)), ((), ())), preferred_element_type=jnp.float32)


def nn(a, b):
    return jnp.dot(a, b, preferred_element_type=jnp.float32)


SMEM = pl.BlockSpec(memory_space=pltpu.SMEM)
VMEM = pl.BlockSpec(memory_space=pltpu.VMEM)
MIB = 1024 * 1024
SMALL = pl.CostEstimate(flops=1, bytes_accessed=1, transcendentals=0)


def whole(value):
    return pl.BlockSpec(value.shape, lambda i: (0,) * value.ndim)


def first_kernel(where_ref, x_hbm, w_hbm, kv_hbm, *refs):
    chips = len(refs) - 7
    out_hbm = refs[:chips]
    x_ref, w_ref, piece_ref, kv_ref, in_sem, piece_sem, kv_sem = refs[chips:]
    features = x_ref.shape[1]
    width = features // (4 * chips)
    chunks = in_sem.shape[0] - 1
    depth = features // chunks
    load_x = pltpu.make_async_copy(x_hbm, x_ref, in_sem.at[chunks])
    load_x.start()
    loads = []
    for i in range(chunks):
        rows = pl.ds(i * depth, depth)
        loads.append(pltpu.make_async_copy(w_hbm.at[rows, pl.ds(HQ * HD, 2 * HD)], w_ref.at[rows, :], in_sem.at[i]))
        loads[i].start()
    load_x.wait()
    stores = []
    for s in range(chips):
        chip = lax.rem(where_ref[0] + s, chips)
        for c in range(2):
            core = where_ref[1] if c == 0 else 1 - where_ref[1]
            for z in range(2):
                at = pl.multiple_of(z * (features // 2) + chip * 2 * width + core * width, width)
                piece_ref[s, (2 * c + z) * width : (2 * c + z + 1) * width, :] = x_ref[:, pl.ds(at, width)].T
        stores.append(pltpu.make_async_copy(piece_ref.at[s], out_hbm[s], piece_sem.at[s]))
        stores[s].start()
    total = None
    for i in range(chunks):
        loads[i].wait()
        part = nn(x_ref[:, i * depth : (i + 1) * depth], w_ref[i * depth : (i + 1) * depth, :])
        total = part if total is None else total + part
    kv_ref[...] = total.astype(jnp.bfloat16)
    copies = kv_hbm.shape[0]
    for i in range(copies):
        stores.append(pltpu.make_async_copy(kv_ref, kv_hbm.at[i], kv_sem.at[i]))
        stores[-1].start()
    for store in stores:
        store.wait()


def first(where, x, w, copies, chips):
    tokens, features = x.shape
    width = 2 * HD
    anywhere = pl.BlockSpec(memory_space=pltpu.HBM)
    return pl.pallas_call(
        first_kernel,
        out_shape=(pltpu.HBM((copies, tokens, width), jnp.bfloat16),)
        + (pltpu.HBM((features // chips, tokens), x.dtype),) * chips,
        in_specs=[SMEM, anywhere, anywhere],
        out_specs=(anywhere,) * (chips + 1),
        scratch_shapes=[
            pltpu.VMEM((tokens, features), x.dtype),
            pltpu.VMEM((features, width), x.dtype),
            pltpu.VMEM((chips, features // chips, tokens), x.dtype),
            pltpu.VMEM((tokens, width), jnp.bfloat16),
            pltpu.SemaphoreType.DMA((5,)),
            pltpu.SemaphoreType.DMA((chips,)),
            pltpu.SemaphoreType.DMA((copies,)),
        ],
        compiler_params=pltpu.CompilerParams(vmem_limit_bytes=60 * MIB),
        cost_estimate=SMALL,
        name="first",
    )(where, x, w)


def query_kernel(x_ref, w_ref, out_ref):
    out_ref[...] = nn(x_ref[...], w_ref[...]).astype(jnp.bfloat16)


def project_query(x, w):
    tokens, features = x.shape
    width = 2 * HD
    return pl.pallas_call(
        query_kernel,
        grid=(HQ // 2,),
        out_shape=jax.ShapeDtypeStruct((tokens, HQ * HD), jnp.bfloat16),
        in_specs=[pl.BlockSpec((tokens, features), lambda i: (0, 0)), pl.BlockSpec((features, width), lambda i: (0, i))],
        out_specs=pl.BlockSpec((tokens, width), lambda i: (0, i)),
        compiler_params=pltpu.CompilerParams(vmem_limit_bytes=44 * MIB),
        cost_estimate=SMALL,
        name="project_query",
    )(x, w)


def half_of(piece, at):
    return pl.BlockSpec((piece.shape[0] // 2, piece.shape[1]), lambda i: (at, 0))


def forward_kernel(*refs):
    pieces, out_ref = refs[:-1], refs[-1]
    tokens = pieces[0].shape[1]
    for i, piece in enumerate(pieces):
        out_ref[:, i * tokens : (i + 1) * tokens] = piece[...]


def forward(pieces):
    rows, tokens = pieces[0].shape
    out = pltpu.HBM((rows // 2, len(pieces) * tokens), jnp.bfloat16)
    return pl.pallas_call(
        forward_kernel,
        grid=(1,),
        out_shape=out,
        in_specs=[half_of(piece, 1) for piece in pieces],
        out_specs=pl.BlockSpec(out.shape, lambda i: (0, 0)),
        compiler_params=pltpu.CompilerParams(vmem_limit_bytes=60 * MIB),
        cost_estimate=SMALL,
        name="forward",
    )(*pieces)


def attention_kernel(where_ref, order_ref, lens_ref, q_ref, do_ref, kv_ref, *refs):
    dq_ref, dkv_ref, bias_ref, dk_ref, dv_ref = refs
    scale = HD ** (-0.5)
    spans = order_ref.shape[1]
    docs = lens_ref.shape[1]
    place = where_ref[2]
    lane = lax.broadcasted_iota(jnp.int32, (1, 2 * SPAN), 1)
    pos_q = jnp.where(
        lane < SPAN,
        order_ref[0, 2 * place] * SPAN + lane,
        order_ref[0, 2 * place + 1] * SPAN + lane - SPAN,
    )
    start = jnp.zeros_like(pos_q)
    end = jnp.int32(0)
    for i in range(docs):
        end = end + lens_ref[0, i]
        start = jnp.where(pos_q >= end, end, start)
    row = lax.broadcasted_iota(jnp.int32, (SPAN, 2 * SPAN), 0)
    for s in range(spans):
        pos_k = order_ref[0, s] * SPAN + row
        allowed = (pos_k <= pos_q) & (pos_k >= start)
        bias_ref[s * SPAN : (s + 1) * SPAN, :] = jnp.where(allowed, 0.0, -jnp.inf)
    k = kv_ref[:, :HD]
    v = kv_ref[:, HD:]
    for h in range(0, HQ, 2):
        a, b, c = h * HD, (h + 1) * HD, (h + 2) * HD
        q2 = jnp.concatenate([q_ref[:, a:b], q_ref[:, b:c]], axis=0)
        d2 = jnp.concatenate([do_ref[:, a:b], do_ref[:, b:c]], axis=0)
        bias = bias_ref[...]
        s2 = nt(k, q2) + jnp.concatenate([bias, bias], axis=1)
        peak = jnp.max(s2, axis=0, keepdims=True)
        expo = jnp.exp2((s2 - peak) * (scale * LOG2E))
        inverse = 1.0 / jnp.sum(expo, axis=0, keepdims=True)
        probs = expo * inverse
        low = probs.astype(jnp.bfloat16)
        dp = nt(v, d2)
        delta = jnp.sum(low.astype(jnp.float32) * dp, axis=0, keepdims=True)
        ds = (probs * ((dp - delta) * scale)).astype(jnp.bfloat16)
        dq = tn(ds, k).astype(jnp.bfloat16)
        dq_ref[:, a:b] = dq[:HD]
        dq_ref[:, b:c] = dq[HD:]
        dv = nn(low, d2)
        dk = nn(ds, q2)
        if h > 0:
            dv += dv_ref[...]
            dk += dk_ref[...]
        if h < HQ - 2:
            dv_ref[...] = dv
            dk_ref[...] = dk
        else:
            dkv_ref[:, :HD] = dk.astype(jnp.bfloat16)
            dkv_ref[:, HD:] = dv.astype(jnp.bfloat16)


def attention(where, order, lens, query, grad, key_value):
    tokens = query.shape[0]
    total = key_value.shape[0]
    return pl.pallas_call(
        attention_kernel,
        out_shape=(
            pltpu.HBM((tokens, HQ * HD), jnp.bfloat16),
            pltpu.HBM((total, 2 * HD), jnp.bfloat16),
        ),
        grid=(1,),
        in_specs=[SMEM] * 3 + [VMEM] * 3,
        out_specs=(whole(query), whole(key_value)),
        scratch_shapes=[
            pltpu.VMEM((total, tokens), jnp.float32),
            pltpu.VMEM((total, HD), jnp.float32),
            pltpu.VMEM((total, HD), jnp.float32),
        ],
        compiler_params=pltpu.CompilerParams(vmem_limit_bytes=30 * MIB),
        cost_estimate=SMALL,
        name="attention",
    )(where, order, lens, query, grad, key_value)


def product(parts, other_ref, pieces, at, width):
    left = jnp.concatenate([part[...] for part in parts] + [other_ref[...]], axis=1)
    right = jnp.concatenate([g[:, pl.ds(at, width)] for g in pieces], axis=0)
    return nn(left, right).astype(jnp.bfloat16)


def term_query_kernel(count, other_ref, *refs):
    parts, pieces, out_ref = refs[:count], refs[count:-1], refs[-1]
    blocks, _, width = out_ref.shape
    at = pl.multiple_of(pl.program_id(0) * width, width)
    part = product(parts, other_ref, pieces, at, width)
    rows = part.shape[0] // (blocks * blocks)
    for i in range(blocks):
        for y in range(blocks):
            here = (i * blocks + y) * rows
            out_ref[y, i * rows : (i + 1) * rows, :] = part[here : here + rows]


def term_query(parts, other, pieces, blocks):
    half = other.shape[0]
    width = pieces[0].shape[1]
    step = 2 * HD
    return pl.pallas_call(
        lambda *refs: term_query_kernel(len(parts), *refs),
        grid=(width // step,),
        out_shape=pltpu.HBM((blocks, half // blocks, width), jnp.bfloat16),
        in_specs=[whole(other)] + [half_of(part, 0) for part in parts] + [VMEM] * len(pieces),
        out_specs=pl.BlockSpec((blocks, half // blocks, step), lambda j: (0, 0, j)),
        compiler_params=pltpu.CompilerParams(vmem_limit_bytes=60 * MIB),
        cost_estimate=SMALL,
        name="term_query",
    )(other, *parts, *pieces)


def ring_block(where_ref, s):
    place = lax.rem(where_ref[3] + s, 4)
    return 2 * lax.rem(place, 2) + place // 2


def term_kv_kernel(count, where_ref, other_ref, *refs):
    parts, pieces, outs, full_ref = refs[:count], refs[count:-5], refs[-5:-1], refs[-1]
    full_ref[...] = product(parts, other_ref, pieces, 0, full_ref.shape[1])
    rows = outs[0].shape[0]
    for s in range(len(outs)):
        at = pl.multiple_of(ring_block(where_ref, s) * rows, rows)
        outs[s][...] = full_ref[pl.ds(at, rows), :]


def term_kv(where, parts, other, pieces, blocks):
    half = other.shape[0]
    width = pieces[0].shape[1]
    out = pltpu.HBM((half // blocks, width), jnp.bfloat16)
    return pl.pallas_call(
        lambda *refs: term_kv_kernel(len(parts), *refs),
        grid=(1,),
        out_shape=(out,) * blocks,
        in_specs=[SMEM, whole(other)] + [half_of(part, 0) for part in parts] + [VMEM] * len(pieces),
        out_specs=(pl.BlockSpec(out.shape, lambda j: (0, 0)),) * blocks,
        scratch_shapes=[pltpu.VMEM((half, width), jnp.bfloat16)],
        compiler_params=pltpu.CompilerParams(vmem_limit_bytes=60 * MIB),
        cost_estimate=SMALL,
        name="term_kv",
    )(where, other, *parts, *pieces)


def middle_z_kernel(stack_ref, out_ref):
    rows = out_ref.shape[1]
    for i in range(out_ref.shape[0]):
        parts = [stack_ref[j, i * rows : (i + 1) * rows, :].astype(jnp.float32) for j in range(stack_ref.shape[0])]
        out_ref[i] = sum(parts).astype(out_ref.dtype)


def middle_z(stack):
    blocks, rows, width = stack.shape
    out = pltpu.HBM((blocks, rows // blocks, width), jnp.bfloat16)
    return pl.pallas_call(
        middle_z_kernel,
        grid=(1,),
        out_shape=out,
        in_specs=[VMEM],
        out_specs=pl.BlockSpec(out.shape, lambda i: (0, 0, 0)),
        compiler_params=pltpu.CompilerParams(vmem_limit_bytes=14 * MIB),
        cost_estimate=SMALL,
        name="middle_z",
    )(stack)


def middle_y_kernel(where_ref, *refs):
    parts, outs = refs[:-4], refs[-4:]
    rows = outs[0].shape[0]
    for s in range(4):
        at = pl.multiple_of(lax.rem(where_ref[4] + s, 4) * rows, rows)
        total = sum(part[pl.ds(at, rows), :].astype(jnp.float32) for part in parts)
        outs[s][...] = total.astype(outs[s].dtype)


def middle_y(where, parts):
    rows, width = parts[0].shape
    return pl.pallas_call(
        middle_y_kernel,
        grid=(1,),
        out_shape=(jax.ShapeDtypeStruct((rows // 4, width), jnp.float32),) + (pltpu.HBM((rows // 4, width), jnp.bfloat16),) * 3,
        in_specs=[SMEM] + [VMEM] * len(parts),
        out_specs=(VMEM,) + (pl.BlockSpec((rows // 4, width), lambda i: (0, 0)),) * 3,
        compiler_params=pltpu.CompilerParams(vmem_limit_bytes=14 * MIB),
        cost_estimate=SMALL,
        name="middle_y",
    )(where, *parts)


def final_kernel(stack_ref, *refs):
    parts, out_ref = refs[:-1], refs[-1]
    first = stack_ref.shape[2]
    out_ref[:, :first] = sum(stack_ref[i].astype(jnp.float32) for i in range(stack_ref.shape[0]))
    out_ref[:, first:] = sum(part[...].astype(jnp.float32) for part in parts)


def final(stack, parts):
    rows = stack.shape[1]
    width = stack.shape[2] + parts[0].shape[1]
    return pl.pallas_call(
        final_kernel,
        out_shape=jax.ShapeDtypeStruct((rows, width), jnp.float32),
        in_specs=[VMEM] * 5,
        out_specs=VMEM,
        compiler_params=pltpu.CompilerParams(vmem_limit_bytes=8 * MIB),
        cost_estimate=SMALL,
        name="final",
    )(stack, *parts)


def input_first_kernel(g_ref, w_ref, out_ref):
    out_ref[...] = nt(g_ref[...], w_ref[...]).astype(out_ref.dtype)


def input_last_kernel(g_ref, kv_ref, w_ref, w_kv_ref, part_ref, out_ref):
    total = nt(g_ref[...], w_ref[...]) + nt(kv_ref[...], w_kv_ref[...])
    out_ref[...] = (total + part_ref[...].astype(jnp.float32)).astype(out_ref.dtype)


def input_grad(query, w, key_value=None, partial=None):
    tokens, width = query.shape
    features = w.shape[0]
    half = width // 2
    step = 2048
    out = pl.BlockSpec((tokens, step), lambda i: (0, i))
    if partial is None:
        kernel, values = input_first_kernel, (query, w)
        specs = [pl.BlockSpec((tokens, half), lambda i: (0, 0)), pl.BlockSpec((step, half), lambda i: (i, 0))]
    else:
        kernel, values = input_last_kernel, (query, key_value, w, w, partial)
        specs = [
            pl.BlockSpec((tokens, half), lambda i: (0, 1)),
            pl.BlockSpec(key_value.shape, lambda i: (0, 0)),
            pl.BlockSpec((step, half), lambda i: (i, 1)),
            pl.BlockSpec((step, 2 * HD), lambda i: (i, HQ // 2)),
            out,
        ]
    return pl.pallas_call(
        kernel,
        grid=(features // step,),
        out_shape=pltpu.HBM((tokens, features), jnp.bfloat16),
        in_specs=specs,
        out_specs=out,
        compiler_params=pltpu.CompilerParams(vmem_limit_bytes=60 * MIB),
        cost_estimate=SMALL,
        name="d_x_first" if partial is None else "d_x_last",
    )(*values)


def shifted(value, s):
    n = lax.axis_size("x")
    return lax.ppermute(value, "x", [(i, (i + s) % n) for i in range(n)])


def swapped(value):
    return lax.ppermute(value, "core", [(0, 1), (1, 0)])


def gather_chips(value, *others):
    own = [value] + [shifted(value, s) for s in range(1, lax.axis_size("x"))]
    return own, [swapped(after(piece, *others)) for piece in own]


def after(value, *others):
    if not others:
        return value
    return lax.optimization_barrier((value,) + others)[0]


def ring_index(place):
    return 2 * (place % 2) + place // 2


def shifted_z(value, s):
    return lax.ppermute(value, DEPTH, [(ring_index(i), ring_index((i + s) % 4)) for i in range(4)])


def shifted_y(value, s):
    return lax.ppermute(value, "y", [(i, (i + s) % 4) for i in range(4)])


def local(layer_input, w_qkv, d_out, span_order, doc_lengths):
    rows = layer_input[0]
    tokens = rows.shape[0]
    chips = lax.axis_size("x")
    seq = lax.axis_size("zhi") * lax.axis_size("y")
    place = lax.axis_index("zhi") * lax.axis_size("y") + lax.axis_index("y")
    ring = lax.axis_index("zhi") * 2 + lax.axis_index("zlo")
    where = jnp.stack([lax.axis_index("x"), lax.axis_index("core"), place, ring, lax.axis_index("y")]).astype(jnp.int32)

    copies, *packed = first(where, rows, w_qkv, seq, chips)
    gathered = lax.all_to_all(copies, SEQ, 0, 0, tiled=True).reshape(seq * tokens, 2 * HD)
    pieces = [packed[0]] + [shifted(packed[s], s) for s in range(1, chips)]
    query = project_query(after(rows, copies), w_qkv)
    d_query, terms = attention(where, span_order, doc_lengths, query, d_out[0], gathered)
    own_q = [d_query] + [shifted(d_query, s) for s in range(1, chips)]
    other_q = [swapped(d_query)]
    d_x_first = input_grad(after(d_query, terms, other_q[0]), w_qkv)
    other_q += [swapped(after(piece, d_x_first)) for piece in own_q[1:]]
    arrived = lax.all_to_all(after(terms, other_q[0]).reshape(seq, tokens, 2 * HD), SEQ, 0, 0, tiled=True)
    x_other = swapped(forward([after(piece, terms) for piece in pieces]))

    places = lax.axis_size("y")
    stacked = term_query(pieces, x_other, own_q + other_q, places)
    group_y = lax.all_to_all(stacked, "y", 0, 0, tiled=True)
    owned = jnp.sum(arrived.astype(jnp.float32), axis=0).astype(jnp.bfloat16)
    own_kv, other_kv = gather_chips(after(owned, stacked))
    parts = term_kv(where, pieces, x_other, own_kv + other_kv, places)
    d_rows = input_grad(d_query, w_qkv, after(owned, parts[0]), d_x_first)
    group_z = [parts[0]] + [after(shifted_z(parts[s], s), d_rows) for s in range(1, places)]
    sums = middle_y(where, group_z)
    second_z = lax.all_to_all(middle_z(after(group_y, sums[1])), DEPTH, 0, 0, tiled=True)
    d_w = final(second_z, [sums[0]] + [shifted_y(sums[s], s) for s in range(1, places)])
    return (d_rows[None], d_w)


def solution(mesh):
    fine = Mesh(mesh.devices.reshape(2, 4, 2, 2, 4), ("zlo", "x", "core", "zhi", "y"))
    dp, ctx = ("zlo", "x", "core"), ("zhi", "y")
    placed = (P(dp, ctx, None), P(), P(dp, ctx, None), P(dp, None), P(dp, None))
    return jax.shard_map(
        local,
        mesh=fine,
        in_specs=placed,
        out_specs=(P(dp, ctx, None), P(dp + ctx, None)),
        check_vma=False,
    )
```

```python
import jax
import jax.numpy as jnp
from jax import lax
from jax.experimental import pallas as pl
from jax.experimental.pallas import tpu as pltpu
from jax.sharding import Mesh, PartitionSpec as P

HD = 128
HQ = 8
SPAN = 64
LOG2E = 1.4426950408889634
SEQ = ("zhi", "y")
DEPTH = ("zlo", "zhi")


def nt(a, b):
    return lax.dot_general(a, b, (((1,), (1,)), ((), ())), preferred_element_type=jnp.float32)


def tn(a, b):
    return lax.dot_general(a, b, (((0,), (0,)), ((), ())), preferred_element_type=jnp.float32)


def nn(a, b):
    return jnp.dot(a, b, preferred_element_type=jnp.float32)


SMEM = pl.BlockSpec(memory_space=pltpu.SMEM)
VMEM = pl.BlockSpec(memory_space=pltpu.VMEM)
MIB = 1024 * 1024
SMALL = pl.CostEstimate(flops=1, bytes_accessed=1, transcendentals=0)


def whole(value):
    return pl.BlockSpec(value.shape, lambda i: (0,) * value.ndim)


def first_kernel(where_ref, x_hbm, w_hbm, kv_hbm, *refs):
    chips = len(refs) - 7
    out_hbm = refs[:chips]
    x_ref, w_ref, piece_ref, kv_ref, in_sem, piece_sem, kv_sem = refs[chips:]
    features = x_ref.shape[1]
    width = features // (4 * chips)
    chunks = in_sem.shape[0] - 1
    depth = features // chunks
    load_x = pltpu.make_async_copy(x_hbm, x_ref, in_sem.at[chunks])
    load_x.start()
    loads = []
    for i in range(chunks):
        rows = pl.ds(i * depth, depth)
        loads.append(pltpu.make_async_copy(w_hbm.at[rows, pl.ds(HQ * HD, 2 * HD)], w_ref.at[rows, :], in_sem.at[i]))
        loads[i].start()
    load_x.wait()
    stores = []
    for s in range(chips):
        chip = lax.rem(where_ref[0] + s, chips)
        for c in range(2):
            core = where_ref[1] if c == 0 else 1 - where_ref[1]
            for z in range(2):
                at = pl.multiple_of(z * (features // 2) + chip * 2 * width + core * width, width)
                piece_ref[s, (2 * c + z) * width : (2 * c + z + 1) * width, :] = x_ref[:, pl.ds(at, width)].T
        stores.append(pltpu.make_async_copy(piece_ref.at[s], out_hbm[s], piece_sem.at[s]))
        stores[s].start()
    total = None
    for i in range(chunks):
        loads[i].wait()
        part = nn(x_ref[:, i * depth : (i + 1) * depth], w_ref[i * depth : (i + 1) * depth, :])
        total = part if total is None else total + part
    kv_ref[...] = total.astype(jnp.bfloat16)
    copies = kv_hbm.shape[0]
    for i in range(copies):
        stores.append(pltpu.make_async_copy(kv_ref, kv_hbm.at[i], kv_sem.at[i]))
        stores[-1].start()
    for store in stores:
        store.wait()


def first(where, x, w, copies, chips):
    tokens, features = x.shape
    width = 2 * HD
    anywhere = pl.BlockSpec(memory_space=pltpu.HBM)
    return pl.pallas_call(
        first_kernel,
        out_shape=(pltpu.HBM((copies, tokens, width), jnp.bfloat16),)
        + (pltpu.HBM((features // chips, tokens), x.dtype),) * chips,
        in_specs=[SMEM, anywhere, anywhere],
        out_specs=(anywhere,) * (chips + 1),
        scratch_shapes=[
            pltpu.VMEM((tokens, features), x.dtype),
            pltpu.VMEM((features, width), x.dtype),
            pltpu.VMEM((chips, features // chips, tokens), x.dtype),
            pltpu.VMEM((tokens, width), jnp.bfloat16),
            pltpu.SemaphoreType.DMA((5,)),
            pltpu.SemaphoreType.DMA((chips,)),
            pltpu.SemaphoreType.DMA((copies,)),
        ],
        compiler_params=pltpu.CompilerParams(vmem_limit_bytes=60 * MIB),
        cost_estimate=SMALL,
        name="first",
    )(where, x, w)


def query_kernel(x_ref, w_ref, out_ref):
    out_ref[...] = nn(x_ref[...], w_ref[...]).astype(jnp.bfloat16)


def project_query(x, w):
    tokens, features = x.shape
    width = 2 * HD
    return pl.pallas_call(
        query_kernel,
        grid=(HQ // 2,),
        out_shape=jax.ShapeDtypeStruct((tokens, HQ * HD), jnp.bfloat16),
        in_specs=[pl.BlockSpec((tokens, features), lambda i: (0, 0)), pl.BlockSpec((features, width), lambda i: (0, i))],
        out_specs=pl.BlockSpec((tokens, width), lambda i: (0, i)),
        compiler_params=pltpu.CompilerParams(vmem_limit_bytes=44 * MIB),
        cost_estimate=SMALL,
        name="project_query",
    )(x, w)


def half_of(piece, at):
    return pl.BlockSpec((piece.shape[0] // 2, piece.shape[1]), lambda i: (at, 0))


def forward_kernel(*refs):
    pieces, out_ref = refs[:-1], refs[-1]
    tokens = pieces[0].shape[1]
    for i, piece in enumerate(pieces):
        out_ref[:, i * tokens : (i + 1) * tokens] = piece[...]


def forward(pieces):
    rows, tokens = pieces[0].shape
    out = pltpu.HBM((rows // 2, len(pieces) * tokens), jnp.bfloat16)
    return pl.pallas_call(
        forward_kernel,
        grid=(1,),
        out_shape=out,
        in_specs=[half_of(piece, 1) for piece in pieces],
        out_specs=pl.BlockSpec(out.shape, lambda i: (0, 0)),
        compiler_params=pltpu.CompilerParams(vmem_limit_bytes=60 * MIB),
        cost_estimate=SMALL,
        name="forward",
    )(*pieces)


def attention_kernel(where_ref, order_ref, lens_ref, q_ref, do_ref, kv_ref, *refs):
    dq_ref, dkv_ref, bias_ref, dk_ref, dv_ref = refs
    scale = HD ** (-0.5)
    spans = order_ref.shape[1]
    docs = lens_ref.shape[1]
    place = where_ref[2]
    lane = lax.broadcasted_iota(jnp.int32, (1, 2 * SPAN), 1)
    pos_q = jnp.where(
        lane < SPAN,
        order_ref[0, 2 * place] * SPAN + lane,
        order_ref[0, 2 * place + 1] * SPAN + lane - SPAN,
    )
    start = jnp.zeros_like(pos_q)
    end = jnp.int32(0)
    for i in range(docs):
        end = end + lens_ref[0, i]
        start = jnp.where(pos_q >= end, end, start)
    row = lax.broadcasted_iota(jnp.int32, (SPAN, 2 * SPAN), 0)
    for s in range(spans):
        pos_k = order_ref[0, s] * SPAN + row
        allowed = (pos_k <= pos_q) & (pos_k >= start)
        bias_ref[s * SPAN : (s + 1) * SPAN, :] = jnp.where(allowed, 0.0, -jnp.inf)
    k = kv_ref[:, :HD]
    v = kv_ref[:, HD:]
    for h in range(0, HQ, 2):
        a, b, c = h * HD, (h + 1) * HD, (h + 2) * HD
        q2 = jnp.concatenate([q_ref[:, a:b], q_ref[:, b:c]], axis=0)
        d2 = jnp.concatenate([do_ref[:, a:b], do_ref[:, b:c]], axis=0)
        bias = bias_ref[...]
        s2 = nt(k, q2) + jnp.concatenate([bias, bias], axis=1)
        peak = jnp.max(s2, axis=0, keepdims=True)
        expo = jnp.exp2((s2 - peak) * (scale * LOG2E))
        inverse = 1.0 / jnp.sum(expo, axis=0, keepdims=True)
        probs = expo * inverse
        low = probs.astype(jnp.bfloat16)
        dp = nt(v, d2)
        delta = jnp.sum(low.astype(jnp.float32) * dp, axis=0, keepdims=True)
        ds = (probs * ((dp - delta) * scale)).astype(jnp.bfloat16)
        dq = tn(ds, k).astype(jnp.bfloat16)
        dq_ref[:, a:b] = dq[:HD]
        dq_ref[:, b:c] = dq[HD:]
        dv = nn(low, d2)
        dk = nn(ds, q2)
        if h > 0:
            dv += dv_ref[...]
            dk += dk_ref[...]
        if h < HQ - 2:
            dv_ref[...] = dv
            dk_ref[...] = dk
        else:
            dkv_ref[:, :HD] = dk.astype(jnp.bfloat16)
            dkv_ref[:, HD:] = dv.astype(jnp.bfloat16)


def attention(where, order, lens, query, grad, key_value):
    tokens = query.shape[0]
    total = key_value.shape[0]
    return pl.pallas_call(
        attention_kernel,
        out_shape=(
            pltpu.HBM((tokens, HQ * HD), jnp.bfloat16),
            pltpu.HBM((total, 2 * HD), jnp.bfloat16),
        ),
        grid=(1,),
        in_specs=[SMEM] * 3 + [VMEM] * 3,
        out_specs=(whole(query), whole(key_value)),
        scratch_shapes=[
            pltpu.VMEM((total, tokens), jnp.float32),
            pltpu.VMEM((total, HD), jnp.float32),
            pltpu.VMEM((total, HD), jnp.float32),
        ],
        compiler_params=pltpu.CompilerParams(vmem_limit_bytes=30 * MIB),
        cost_estimate=SMALL,
        name="attention",
    )(where, order, lens, query, grad, key_value)


def product(parts, other_ref, pieces, at, width):
    left = jnp.concatenate([part[...] for part in parts] + [other_ref[...]], axis=1)
    right = jnp.concatenate([g[:, pl.ds(at, width)] for g in pieces], axis=0)
    return nn(left, right).astype(jnp.bfloat16)


def term_query_kernel(count, other_ref, *refs):
    parts, pieces, out_ref = refs[:count], refs[count:-1], refs[-1]
    blocks, _, width = out_ref.shape
    at = pl.multiple_of(pl.program_id(0) * width, width)
    part = product(parts, other_ref, pieces, at, width)
    rows = part.shape[0] // (blocks * blocks)
    for i in range(blocks):
        for y in range(blocks):
            here = (i * blocks + y) * rows
            out_ref[y, i * rows : (i + 1) * rows, :] = part[here : here + rows]


def term_query(parts, other, pieces, blocks):
    half = other.shape[0]
    width = pieces[0].shape[1]
    step = 2 * HD
    return pl.pallas_call(
        lambda *refs: term_query_kernel(len(parts), *refs),
        grid=(width // step,),
        out_shape=pltpu.HBM((blocks, half // blocks, width), jnp.bfloat16),
        in_specs=[whole(other)] + [half_of(part, 0) for part in parts] + [VMEM] * len(pieces),
        out_specs=pl.BlockSpec((blocks, half // blocks, step), lambda j: (0, 0, j)),
        compiler_params=pltpu.CompilerParams(vmem_limit_bytes=20 * MIB),
        cost_estimate=SMALL,
        name="term_query",
    )(other, *parts, *pieces)


def ring_block(where_ref, s):
    place = lax.rem(where_ref[3] + s, 4)
    return 2 * lax.rem(place, 2) + place // 2


def term_kv_kernel(count, where_ref, other_ref, *refs):
    parts, pieces, outs, full_ref = refs[:count], refs[count:-5], refs[-5:-1], refs[-1]
    full_ref[...] = product(parts, other_ref, pieces, 0, full_ref.shape[1])
    rows = outs[0].shape[0]
    for s in range(len(outs)):
        at = pl.multiple_of(ring_block(where_ref, s) * rows, rows)
        outs[s][...] = full_ref[pl.ds(at, rows), :]


def term_kv(where, parts, other, pieces, blocks):
    half = other.shape[0]
    width = pieces[0].shape[1]
    out = pltpu.HBM((half // blocks, width), jnp.bfloat16)
    return pl.pallas_call(
        lambda *refs: term_kv_kernel(len(parts), *refs),
        grid=(1,),
        out_shape=(out,) * blocks,
        in_specs=[SMEM, whole(other)] + [half_of(part, 0) for part in parts] + [VMEM] * len(pieces),
        out_specs=(pl.BlockSpec(out.shape, lambda j: (0, 0)),) * blocks,
        scratch_shapes=[pltpu.VMEM((half, width), jnp.bfloat16)],
        compiler_params=pltpu.CompilerParams(vmem_limit_bytes=60 * MIB),
        cost_estimate=SMALL,
        name="term_kv",
    )(where, other, *parts, *pieces)


def middle_z_kernel(stack_ref, out_ref):
    rows = out_ref.shape[1]
    for i in range(out_ref.shape[0]):
        parts = [stack_ref[j, i * rows : (i + 1) * rows, :].astype(jnp.float32) for j in range(stack_ref.shape[0])]
        out_ref[i] = sum(parts).astype(out_ref.dtype)


def middle_z(stack):
    blocks, rows, width = stack.shape
    out = pltpu.HBM((blocks, rows // blocks, width), jnp.bfloat16)
    return pl.pallas_call(
        middle_z_kernel,
        grid=(1,),
        out_shape=out,
        in_specs=[VMEM],
        out_specs=pl.BlockSpec(out.shape, lambda i: (0, 0, 0)),
        compiler_params=pltpu.CompilerParams(vmem_limit_bytes=14 * MIB),
        cost_estimate=SMALL,
        name="middle_z",
    )(stack)


def middle_y_kernel(where_ref, *refs):
    parts, outs = refs[:-4], refs[-4:]
    rows = outs[0].shape[0]
    for s in range(4):
        at = pl.multiple_of(lax.rem(where_ref[4] + s, 4) * rows, rows)
        total = sum(part[pl.ds(at, rows), :].astype(jnp.float32) for part in parts)
        outs[s][...] = total.astype(outs[s].dtype)


def middle_y(where, parts):
    rows, width = parts[0].shape
    return pl.pallas_call(
        middle_y_kernel,
        grid=(1,),
        out_shape=(jax.ShapeDtypeStruct((rows // 4, width), jnp.float32),) + (pltpu.HBM((rows // 4, width), jnp.bfloat16),) * 3,
        in_specs=[SMEM] + [VMEM] * len(parts),
        out_specs=(VMEM,) + (pl.BlockSpec((rows // 4, width), lambda i: (0, 0)),) * 3,
        compiler_params=pltpu.CompilerParams(vmem_limit_bytes=14 * MIB),
        cost_estimate=SMALL,
        name="middle_y",
    )(where, *parts)


def final_kernel(stack_ref, *refs):
    parts, out_ref = refs[:-1], refs[-1]
    first = stack_ref.shape[2]
    out_ref[:, :first] = sum(stack_ref[i].astype(jnp.float32) for i in range(stack_ref.shape[0]))
    out_ref[:, first:] = sum(part[...].astype(jnp.float32) for part in parts)


def final(stack, parts):
    rows = stack.shape[1]
    width = stack.shape[2] + parts[0].shape[1]
    return pl.pallas_call(
        final_kernel,
        out_shape=jax.ShapeDtypeStruct((rows, width), jnp.float32),
        in_specs=[VMEM] * 5,
        out_specs=VMEM,
        compiler_params=pltpu.CompilerParams(vmem_limit_bytes=8 * MIB),
        cost_estimate=SMALL,
        name="final",
    )(stack, *parts)


def input_first_kernel(g_ref, w_ref, out_ref):
    out_ref[...] = nt(g_ref[...], w_ref[...]).astype(out_ref.dtype)


def input_last_kernel(g_ref, kv_ref, w_ref, w_kv_ref, part_ref, out_ref):
    total = nt(g_ref[...], w_ref[...]) + nt(kv_ref[...], w_kv_ref[...])
    out_ref[...] = (total + part_ref[...].astype(jnp.float32)).astype(out_ref.dtype)


def input_grad(query, w, key_value=None, partial=None):
    tokens, width = query.shape
    features = w.shape[0]
    half = width // 2
    step = 2048
    out = pl.BlockSpec((tokens, step), lambda i: (0, i))
    if partial is None:
        kernel, values = input_first_kernel, (query, w)
        specs = [pl.BlockSpec((tokens, half), lambda i: (0, 0)), pl.BlockSpec((step, half), lambda i: (i, 0))]
    else:
        kernel, values = input_last_kernel, (query, key_value, w, w, partial)
        specs = [
            pl.BlockSpec((tokens, half), lambda i: (0, 1)),
            pl.BlockSpec(key_value.shape, lambda i: (0, 0)),
            pl.BlockSpec((step, half), lambda i: (i, 1)),
            pl.BlockSpec((step, 2 * HD), lambda i: (i, HQ // 2)),
            out,
        ]
    return pl.pallas_call(
        kernel,
        grid=(features // step,),
        out_shape=pltpu.HBM((tokens, features), jnp.bfloat16),
        in_specs=specs,
        out_specs=out,
        compiler_params=pltpu.CompilerParams(vmem_limit_bytes=60 * MIB),
        cost_estimate=SMALL,
        name="d_x_first" if partial is None else "d_x_last",
    )(*values)


def shifted(value, s):
    n = lax.axis_size("x")
    return lax.ppermute(value, "x", [(i, (i + s) % n) for i in range(n)])


def swapped(value):
    return lax.ppermute(value, "core", [(0, 1), (1, 0)])


def gather_chips(value, *others):
    own = [value] + [shifted(value, s) for s in range(1, lax.axis_size("x"))]
    return own, [swapped(after(piece, *others)) for piece in own]


def after(value, *others):
    if not others:
        return value
    return lax.optimization_barrier((value,) + others)[0]


def ring_index(place):
    return 2 * (place % 2) + place // 2


def shifted_z(value, s):
    return lax.ppermute(value, DEPTH, [(ring_index(i), ring_index((i + s) % 4)) for i in range(4)])


def shifted_y(value, s):
    return lax.ppermute(value, "y", [(i, (i + s) % 4) for i in range(4)])


def local(layer_input, w_qkv, d_out, span_order, doc_lengths):
    rows = layer_input[0]
    tokens = rows.shape[0]
    chips = lax.axis_size("x")
    seq = lax.axis_size("zhi") * lax.axis_size("y")
    place = lax.axis_index("zhi") * lax.axis_size("y") + lax.axis_index("y")
    ring = lax.axis_index("zhi") * 2 + lax.axis_index("zlo")
    where = jnp.stack([lax.axis_index("x"), lax.axis_index("core"), place, ring, lax.axis_index("y")]).astype(jnp.int32)

    copies, *packed = first(where, rows, w_qkv, seq, chips)
    gathered = lax.all_to_all(copies, SEQ, 0, 0, tiled=True).reshape(seq * tokens, 2 * HD)
    pieces = [packed[0]] + [shifted(packed[s], s) for s in range(1, chips)]
    query = project_query(after(rows, copies), w_qkv)
    d_query, terms = attention(where, span_order, doc_lengths, query, d_out[0], gathered)
    own_q = [d_query] + [shifted(d_query, s) for s in range(1, chips)]
    other_q = [swapped(d_query)]
    d_x_first = input_grad(after(d_query, terms, other_q[0]), w_qkv)
    other_q += [swapped(after(piece, d_x_first)) for piece in own_q[1:]]
    arrived = lax.all_to_all(after(terms, other_q[0]).reshape(seq, tokens, 2 * HD), SEQ, 0, 0, tiled=True)
    x_other = swapped(forward([after(piece, terms) for piece in pieces]))

    places = lax.axis_size("y")
    stacked = term_query(pieces, x_other, own_q + other_q, places)
    group_y = lax.all_to_all(stacked, "y", 0, 0, tiled=True)
    owned = jnp.sum(arrived.astype(jnp.float32), axis=0).astype(jnp.bfloat16)
    own_kv, other_kv = gather_chips(after(owned, stacked))
    parts = term_kv(where, pieces, x_other, own_kv + other_kv, places)
    d_rows = input_grad(d_query, w_qkv, after(owned, parts[0]), d_x_first)
    group_z = [parts[0]] + [after(shifted_z(parts[s], s), d_rows) for s in range(1, places)]
    sums = middle_y(where, group_z)
    second_z = lax.all_to_all(middle_z(after(group_y, sums[1])), DEPTH, 0, 0, tiled=True)
    d_w = final(second_z, [sums[0]] + [shifted_y(sums[s], s) for s in range(1, places)])
    return (d_rows[None], d_w)


def solution(mesh):
    fine = Mesh(mesh.devices.reshape(2, 4, 2, 2, 4), ("zlo", "x", "core", "zhi", "y"))
    dp, ctx = ("zlo", "x", "core"), ("zhi", "y")
    placed = (P(dp, ctx, None), P(), P(dp, ctx, None), P(dp, None), P(dp, None))
    return jax.shard_map(
        local,
        mesh=fine,
        in_specs=placed,
        out_specs=(P(dp, ctx, None), P(dp + ctx, None)),
        check_vma=False,
    )
```
